128 devices in a mesh: tile: 32 (over z, x, core), row: 4 (over y).
Axes of the slice: x: 4, y: 4, z: 4, core: 2. Of those that a mesh axis runs over, the one named last changes fastest.
Arguments:
- object_field: float32 [2, 2048, 16384], P(None, 'row', 'tile'), may hold values from -5 to 5
- probe: float32 [2, 256, 256], replicated, may hold values from -5 to 5
- intensity: bfloat16 [4096, 256, 256], P(('tile', 'row')), may hold values from 0 to 4
- pool_rows: int32 [4096], P(('tile', 'row')), may hold values from 0 to 511
- pool_cols: int32 [4096], P(('tile', 'row')), may hold values from 0 to 511
- batch: int32 [2, 1536], P(None, ('tile', 'row')), may hold values from 0 to 31
- live: int32 [2, 128], P(None, ('tile', 'row')), may hold values from 1 to 12, 768 in all within a row
Outputs:
- object_out: float32 [2, 2048, 16384], P(None, 'row', 'tile')
- probe_out: float32 [2, 256, 256], replicated
The draws below stay inside these ranges and needn't reach their ends.
Inputs may be any that keep to these rules, and one draw needn't show every extreme that they name: `pool_rows`: row offset inside the owning device's block. `pool_cols`: column offset inside the owning device's block. `batch`: index into the device's own 32 stored positions. For each iteration k, the counts live[k, 0] .. live[k, 127] of all 128 devices of the mesh together sum to 768; one device of each iteration has exactly 12.
All inputs are finite; a program needn't handle non-finite values.
Results may differ from the reference program's by a relative error of at most 0.015.
The reference program's roundings to bfloat16 on the way count: a program that leaves them out, or rounds other values in their place, can miss the bound.
Values sent between devices are 32-bit elements; how exact they have to be, the bound alone decides.
No kernel may reach another device: no remote copies, remote signals or barrier semaphores. Data moves between devices by JAX's collectives and lax.ppermute only.
A program may use at most 64 MiB of HBM per device.

```python
import math
import jax
import jax.numpy as jnp
import numpy as np
from jax import lax

PROBE = 256
BR = 512
BC = 512
POOL = 32
CAP = 12
LIVE = 6
ITERS = 2
NR = 2048
NC = 16384
POOLS = 4096
SLOTS = 1536
TOTAL = 768
N_TILE = 32
N_ROW = 4
DEVICES = 128


def place_ends(result, key, least, largest):
    shape = result.shape
    place = [jax.random.randint(jax.random.fold_in(key, axis), (), 0, shape[axis]) for axis in range(len(shape))]
    result = result.at[tuple(place)].set(least)
    longest = shape.index(max(shape))
    place[longest] = (place[longest] + 1) % shape[longest]
    return result.at[tuple(place)].set(largest)


def block_scale(rng, dims, pieces, smallest, largest):
    factor_of, own = 1.0, jax.random.fold_in(rng, 6)
    for dim, blocks in pieces:
        heights = jnp.exp(jax.random.uniform(jax.random.fold_in(own, dim), (blocks,), jnp.float32, smallest / len(pieces), largest / len(pieces)))
        factor_of = factor_of * jnp.repeat(heights, dims[dim] // blocks).reshape([-1 if axis == dim else 1 for axis in range(len(dims))])
    return factor_of


def profile(count, total, bound, slope):
    loads = [(1 << 20) // math.isqrt(standing ** slope) + 1 for standing in range(2, count + 1)]
    rest, given = total - bound - (count - 1), [1] * (count - 1)
    while rest > 0:
        free = [i for i in range(count - 1) if given[i] < bound]
        mass, remaining = sum([loads[i] for i in free]), rest
        for i in free:
            extra = min(bound - given[i], max(1, remaining * loads[i] // mass), rest)
            given[i] = given[i] + extra
            rest = rest - extra
    return np.array([bound] + given)


def uneven_parts(rng, number_of, total, reach, slope):
    if number_of == 2:
        one = jax.random.randint(rng, (), max(1, total - reach), min(reach, total - 1) + 1)
        return jnp.stack([one, total - one])
    lengths = jnp.asarray(profile(number_of, total, reach, slope), jnp.int32)
    couples = (number_of - 1) // 2
    source_of, taker = lengths[1:1 + 2 * couples:2], lengths[2:2 + 2 * couples:2]
    slack = jnp.minimum(source_of - 1, reach - taker)
    passed = jax.random.randint(jax.random.fold_in(rng, 1), (couples,), 0, 1 << 20) % (slack + 1)
    lengths = lengths.at[1:1 + 2 * couples:2].set(source_of - passed).at[2:2 + 2 * couples:2].set(taker + passed)
    return lengths[jax.random.permutation(jax.random.fold_in(rng, 2), number_of)]


def centred(stream_key, shape, deviation, bound, shards=(), kind=jnp.bfloat16):
    level = block_scale(stream_key, shape, shards, -0.22, 0.18) if shards else 1.0
    array = jax.random.normal(stream_key, shape, jnp.float32) * deviation * level
    return jnp.minimum(jnp.maximum(array, -bound), bound).astype(kind)


def setup_inputs(seed: int = 0) -> dict:
    arg_keys = jax.random.split(jax.random.key(seed), 8)
    object_field = centred(arg_keys[0], (2, NR, NC), 0.7, 5.0, ((1, 4), (2, 32)), jnp.float32)
    probe = centred(arg_keys[1], (2, PROBE, PROBE), 0.7, 5.0, (), jnp.float32)
    intensity = jnp.clip(4.0 * jax.random.uniform(arg_keys[2], (POOLS, PROBE, PROBE), jnp.float32) ** block_scale(arg_keys[2], (POOLS, PROBE, PROBE), ((0, 128),), -0.2, 0.2), 0.0, 4.0).astype(jnp.bfloat16)
    pool_rows = place_ends(jax.random.randint(arg_keys[3], (POOLS,), 0, BR), jax.random.fold_in(arg_keys[3], 1), 0, BR - 1).astype(jnp.int32)
    pool_cols = place_ends(jax.random.randint(arg_keys[4], (POOLS,), 0, BC), jax.random.fold_in(arg_keys[4], 1), 0, BC - 1).astype(jnp.int32)
    batch = place_ends(jax.random.randint(arg_keys[5], (ITERS, SLOTS), 0, POOL), jax.random.fold_in(arg_keys[5], 1), 0, POOL - 1).astype(jnp.int32)
    live = jax.vmap(lambda own: uneven_parts(own, DEVICES, TOTAL, CAP, 2))(jax.random.split(arg_keys[6], ITERS)).reshape((ITERS, DEVICES)).astype(jnp.int32)
    return {"object_field": object_field, "probe": probe, "intensity": intensity, "pool_rows": pool_rows, "pool_cols": pool_cols, "batch": batch, "live": live}


def tables(length):
    counter = lax.iota(jnp.int32, length)
    product = counter[:, None] * counter[None, :] % length
    angle = product.astype(jnp.float32) * (2.0 * math.pi / length)
    factor = 1.0 / math.sqrt(length)
    return ((jnp.cos(angle) * factor).astype(jnp.bfloat16), (jnp.sin(angle) * factor).astype(jnp.bfloat16))

def mul(left, right):
    return jnp.dot(left.astype(jnp.float32), right.astype(jnp.float32), precision=lax.Precision.HIGHEST)

def transform(real_part, imag_part, cosine, sine_table, sign):
    half_real = (mul(cosine, real_part) + sign * mul(sine_table, imag_part)).astype(jnp.bfloat16)
    half_imag = (mul(cosine, imag_part) - sign * mul(sine_table, real_part)).astype(jnp.bfloat16)
    out_real = mul(half_real, cosine) + sign * mul(half_imag, sine_table)
    out_imag = mul(half_imag, cosine) - sign * mul(half_real, sine_table)
    return (out_real, out_imag)

def reference(object_field, probe, intensity, pool_rows, pool_cols, batch, live):
    field = object_field
    current = probe
    devices = N_TILE * N_ROW
    probe_rate = 0.125 / math.sqrt(LIVE * devices)
    zero_index = jnp.zeros((), jnp.int32)
    cosine, sine_table = tables(PROBE)
    for step_index in range(ITERS):
        padded = jnp.pad(field, ((0, 0), (0, PROBE), (0, PROBE)))

        def one_slot(carry, slot_index):
            grad_field, grad_probe = carry
            device = slot_index // CAP
            within = slot_index % CAP
            tile_pos = device // N_ROW
            row_pos = device % N_ROW
            stored = device * POOL + batch[step_index, slot_index]
            row_start = (row_pos * BR + pool_rows[stored]).astype(jnp.int32)
            col_start = (tile_pos * BC + pool_cols[stored]).astype(jnp.int32)
            patch = lax.dynamic_slice(padded, (zero_index, row_start, col_start), (2, PROBE, PROBE))
            alive = (within < live[step_index, device]).astype(field.dtype)
            exit_real = (current[0] * patch[0] - current[1] * patch[1]).astype(jnp.bfloat16)
            exit_imag = (current[0] * patch[1] + current[1] * patch[0]).astype(jnp.bfloat16)
            far_real, far_imag = transform(exit_real, exit_imag, cosine, sine_table, 1.0)
            excess = (far_real * far_real + far_imag * far_imag - intensity[stored].astype(field.dtype)) * alive
            wave_real = (excess * far_real).astype(jnp.bfloat16)
            wave_imag = (excess * far_imag).astype(jnp.bfloat16)
            back_real, back_imag = transform(wave_real, wave_imag, cosine, sine_table, -1.0)
            obj_real = current[0] * back_real + current[1] * back_imag
            obj_imag = current[0] * back_imag - current[1] * back_real
            prb_real = patch[0] * back_real + patch[1] * back_imag
            prb_imag = patch[0] * back_imag - patch[1] * back_real
            old = lax.dynamic_slice(grad_field, (zero_index, row_start, col_start), (2, PROBE, PROBE))
            grad_field = lax.dynamic_update_slice(grad_field, old + jnp.stack([obj_real, obj_imag]), (zero_index, row_start, col_start))
            grad_probe = grad_probe + jnp.stack([prb_real, prb_imag])
            return ((grad_field, grad_probe), None)
        start = (jnp.zeros_like(padded), jnp.zeros_like(current))
        (grad_field, grad_probe), _ = lax.scan(one_slot, start, jnp.arange(devices * CAP, dtype=jnp.int32))
        field = field - 0.25 * grad_field[:, :BR * N_ROW, :BC * N_TILE]
        current = current - probe_rate * grad_probe
    return (field, current)
```

```python
import functools
import math

import jax
import jax.numpy as jnp
import numpy as np
from jax import lax
from jax.experimental import pallas as pl
from jax.experimental.pallas import tpu as pltpu
from jax.sharding import PartitionSpec as P

LIVE = 6
LANES = 128
F32 = jnp.float32
BF16 = jnp.bfloat16


def passed_along(value, axis, steps):
    count = lax.axis_size(axis)
    first, last = (max(0, -steps), min(count, count - steps))
    return lax.ppermute(value, axis, [(source, source + steps) for source in range(first, last)])


def tables(length):
    counter = np.arange(length, dtype=np.int32)
    product = counter[:, None] * counter[None, :] % length
    angle = product.astype(np.float32) * np.float32(2.0 * math.pi / length)
    factor = np.float32(1.0 / math.sqrt(length))
    cosine = (np.cos(angle) * factor).astype(BF16)
    sine = (np.sin(angle) * factor).astype(BF16)
    forward = np.block([[cosine, sine], [-sine, cosine]])
    backward = np.block([[cosine, -sine], [sine, cosine]])
    return forward, backward


def mul(left, right):
    return jnp.dot(left, right, preferred_element_type=F32)


def start_slots(step, batch, intensity, measured, sems):
    copies = []
    for s in range(batch.shape[1]):
        copies.append(
            pltpu.make_async_copy(intensity.at[batch[step, s]], measured.at[s], sems.at[s]))
    for copy in copies:
        copy.start()
    return copies


def clear(grad, gprobe, waves, patches):
    grad[...] = jnp.zeros_like(grad)
    gprobe[...] = jnp.zeros_like(gprobe)
    waves[1][...] = jnp.zeros_like(waves[1])
    patches[1][...] = jnp.zeros_like(patches[1])


def slot_loop(step, side, batch, live, rows, cols, mats, probe, ext, grad, gprobe,
              measured, exits, waves, patches, back):
    forward, backward = mats
    lane = lax.broadcasted_iota(jnp.int32, (side, LANES), 1)
    halves = side // LANES
    count = live[step, 0]

    def corner_of(s):
        stored = batch[step, s]
        col = cols[stored]
        return rows[stored], col // LANES, col % LANES

    def window(part, tile, row, shift):
        turn = (LANES - shift) & (LANES - 1)
        turned = [
            pltpu.roll(ext[part, tile + j, pl.ds(row, side), :], turn, 1) for j in range(halves + 1)
        ]
        keep = lane < LANES - shift
        return [jnp.where(keep, turned[j], turned[j + 1]) for j in range(halves)]

    def place(part, tile, row, shift, values):
        turned = [pltpu.roll(v, shift, 1) for v in values]
        keep = lane >= shift
        zero = jnp.zeros((side, LANES), F32)
        for j in range(halves + 1):
            here = turned[j] if j < halves else zero
            prior = turned[j - 1] if j else zero
            at = (part, tile + j, pl.ds(row, side), slice(None))
            grad[at] = grad[at] + jnp.where(keep, here, prior)

    def first_half(s, buffer, alive):
        row, tile, shift = corner_of(s)
        exit_in, wave, patch = exits[buffer], waves[buffer], patches[buffer]
        patch_r = window(0, tile, row, shift)
        patch_i = window(1, tile, row, shift)
        for j in range(halves):
            p_r, p_i = probe[0, j], probe[1, j]
            at = slice(j * LANES, (j + 1) * LANES)
            patch[0, j] = patch_r[j]
            patch[1, j] = patch_i[j]
            exit_in[0:side, at] = (p_r * patch_r[j] - p_i * patch_i[j]).astype(BF16)
            exit_in[side:, at] = (p_r * patch_i[j] + p_i * patch_r[j]).astype(BF16)
        half = mul(forward[...], exit_in[...]).astype(BF16)
        far = mul(jnp.concatenate([half[:side], half[side:]], axis=1), backward[...])
        far_r, far_i = far[:, :side], far[:, side:]
        excess = far_r * far_r + far_i * far_i - measured[s].astype(F32)
        if alive is not None:
            excess = excess * alive
        wave[0:side, :] = (excess * far_r).astype(BF16)
        wave[side:, :] = (excess * far_i).astype(BF16)

    def second_half(s, buffer):
        row, tile, shift = corner_of(s)
        wave, patch = waves[buffer], patches[buffer]
        mid = mul(backward[...], wave[...]).astype(BF16)
        back[buffer][...] = mul(jnp.concatenate([mid[:side], mid[side:]], axis=1), forward[...])
        object_r, object_i = [], []
        for j in range(halves):
            p_r, p_i = probe[0, j], probe[1, j]
            o_r, o_i = patch[0, j], patch[1, j]
            b_r = back[buffer][:, j * LANES:(j + 1) * LANES]
            b_i = back[buffer][:, side + j * LANES:side + (j + 1) * LANES]
            object_r.append(p_r * b_r + p_i * b_i)
            object_i.append(p_r * b_i - p_i * b_r)
            gprobe[0, j] += o_r * b_r + o_i * b_i
            gprobe[1, j] += o_r * b_i - o_i * b_r
        place(0, tile, row, shift, object_r)
        place(1, tile, row, shift, object_i)

    def two_slots(k, carry):
        even = 2 * k
        odd = jnp.minimum(even + 1, batch.shape[1] - 1)
        alive = jnp.where(even + 1 < count, 1.0, 0.0).astype(F32)
        second_half(jnp.maximum(even - 1, 0), 1)
        first_half(even, 0, None)
        second_half(even, 0)
        first_half(odd, 1, alive)
        return carry

    pairs = (count + 1) // 2
    lax.fori_loop(0, pairs, two_slots, 0)
    second_half(jnp.minimum(2 * pairs - 1, batch.shape[1] - 1), 1)


def tiled_copies(field, part_rows, part_cols, ext, row0, col0):
    pairs = []
    for part in range(2):
        for j in range(part_cols // LANES):
            pairs.append((
                field.at[part, :, pl.ds(j * LANES, LANES)],
                ext.at[part, col0 // LANES + j, pl.ds(row0, part_rows), :],
            ))
    return pairs


def run_copies(pairs, sems, base=0):
    copies = [pltpu.make_async_copy(src, dst, sems.at[base + i]) for i, (src, dst) in enumerate(pairs)]
    for copy in copies:
        copy.start()
    return copies


def first_kernel(dims, batch, live, rows, cols, forward, backward, probe, intensity,
                 field, below_a, below_b, beside, corner,
                 part_out, gprobe, right_c, left_c, down_b, up_b, right_b, left_b,
                 ext, grad, measured, exit_0, exit_1, wave_0, wave_1, patch_0, patch_1,
                 back_0, back_1, sems, moves):
    side, nrows, ncols = dims
    pairs = tiled_copies(field, nrows, ncols, ext, 0, 0)
    pairs += tiled_copies(below_a, side, side, ext, nrows, 0)
    pairs += tiled_copies(below_b, side, ncols - side, ext, nrows, side)
    pairs += tiled_copies(beside, nrows, side, ext, 0, ncols)
    pairs += tiled_copies(corner, side, side, ext, nrows, ncols)
    copies = run_copies(pairs, moves)
    copies += start_slots(0, batch, intensity, measured, sems)
    waves, patches = (wave_0, wave_1), (patch_0, patch_1)
    clear(grad, gprobe, waves, patches)
    for copy in copies:
        copy.wait()
    slot_loop(0, side, batch, live, rows, cols, (forward, backward), probe, ext, grad, gprobe,
              measured, (exit_0, exit_1), waves, patches, (back_0, back_1))
    t = side // LANES
    last = ncols // LANES
    a_rows, c_rows = pl.ds(0, side), pl.ds(nrows, side)
    b_rows = pl.ds(side, nrows - side)
    left, mid, right = pl.ds(0, t), pl.ds(t, last - t), pl.ds(last, t)
    pairs = [
        (grad.at[:, right, a_rows, :], right_c.at[0]),
        (grad.at[:, right, c_rows, :], right_c.at[1]),
        (grad.at[:, left, a_rows, :], left_c.at[0]),
        (grad.at[:, left, c_rows, :], left_c.at[1]),
        (grad.at[:, mid, c_rows, :], down_b),
        (grad.at[:, mid, a_rows, :], up_b),
        (grad.at[:, right, b_rows, :], right_b),
        (grad.at[:, left, b_rows, :], left_b),
    ]
    copies = run_copies(pairs, moves)
    ext[...] = ext[...] - 0.25 * grad[...]
    copies += run_copies([(ext, part_out)], moves, len(pairs))
    for copy in copies:
        copy.wait()


def join_kernel(left_c, right_c, from_left, from_right, down, up, own, other, moves, stores):
    places = []
    for band, target in ((1, down), (0, up)):
        for side, (mine, received) in enumerate(((left_c, from_left), (right_c, from_right))):
            places.append((mine.at[band], received.at[band], target.at[side]))
    loads = []
    for i, (mine, received, target) in enumerate(places):
        loads.append((pltpu.make_async_copy(mine, own.at[i], moves.at[2 * i]),
                      pltpu.make_async_copy(received, other.at[i], moves.at[2 * i + 1])))
    for pair in loads:
        for copy in pair:
            copy.start()
    copies = []
    for i, (mine, received, target) in enumerate(places):
        for copy in loads[i]:
            copy.wait()
        own[i] = own[i] + other[i]
        copies.append(pltpu.make_async_copy(own.at[i], target, stores.at[i]))
        copies[-1].start()
    for copy in copies:
        copy.wait()


def share_kernel(received, given):
    summed = received[0]
    for i in range(1, received.shape[0]):
        summed = summed + received[i]
    for i in range(received.shape[0]):
        given[i] = summed


def second_kernel(dims, rate, batch, live, rows, cols, edge, forward, backward, probe, summed,
                  intensity, part_in, from_left_c, from_right_c, from_up_c, from_down_c,
                  from_up, from_down, from_left, from_right,
                  own_out, gprobe, right_c, right_ab, down_a, down_b,
                  ext, grad, measured, exit_0, exit_1, wave_0, wave_1, patch_0, patch_1,
                  back_0, back_1, now, lc_in, rc_in, uc_in, dc_in, u_in, d_in, l_in, r_in, sems, moves):
    side, nrows, ncols = dims
    t = side // LANES
    last = ncols // LANES
    pairs = [(part_in, ext), (from_left_c, lc_in), (from_right_c, rc_in), (from_up_c, uc_in),
             (from_down_c, dc_in), (from_up, u_in), (from_down, d_in),
             (from_left, l_in), (from_right, r_in)]
    copies = run_copies(pairs, moves)
    copies += start_slots(1, batch, intensity, measured, sems)
    waves, patches = (wave_0, wave_1), (patch_0, patch_1)
    clear(grad, gprobe, waves, patches)
    now[...] = probe[...] - rate * summed[...]
    for copy in copies:
        copy.wait()
    a_rows, c_rows = slice(0, side), slice(nrows, nrows + side)
    b_rows = slice(side, nrows)
    left, mid, right = slice(0, t), slice(t, last), slice(last, last + t)
    for rows_of, corner, strip, k in ((a_rows, uc_in, u_in, 0), (c_rows, dc_in, d_in, 1)):
        ext[:, left, rows_of, :] -= 0.25 * (corner[0] + lc_in[k])
        ext[:, mid, rows_of, :] -= 0.25 * strip[...]
        ext[:, right, rows_of, :] -= 0.25 * (corner[1] + rc_in[k])
    ext[:, left, b_rows, :] -= 0.25 * l_in[...]
    ext[:, right, b_rows, :] -= 0.25 * r_in[...]

    @pl.when(edge[0] == 1)
    def _():
        ext[:, :, c_rows, :] = jnp.zeros((2, last + t, side, LANES), F32)

    @pl.when(edge[1] == 1)
    def _():
        ext[:, right, :, :] = jnp.zeros((2, t, nrows + side, LANES), F32)

    slot_loop(1, side, batch, live, rows, cols, (forward, backward), now, ext, grad, gprobe,
              measured, (exit_0, exit_1), waves, patches, (back_0, back_1))
    c_rows, own_rows = pl.ds(nrows, side), pl.ds(0, nrows)
    own_cols, right = pl.ds(0, last), pl.ds(last, t)
    pairs = [
        (grad.at[:, right, c_rows, :], right_c),
        (grad.at[:, pl.ds(t, last - t), c_rows, :], down_b),
        (grad.at[:, pl.ds(0, t), c_rows, :], down_a),
        (grad.at[:, right, own_rows, :], right_ab),
    ]
    copies = run_copies(pairs, moves)
    ext[:, 0:last, 0:nrows, :] = ext[:, 0:last, 0:nrows, :] - 0.25 * grad[:, 0:last, 0:nrows, :]
    copies += run_copies([(ext.at[:, own_cols, own_rows, :], own_out)], moves, len(pairs))
    for copy in copies:
        copy.wait()


def last_kernel(dims, rate, own, left_ab, above_a, above_b, probe, sum_one, sum_two,
                object_out, probe_out):
    side, nrows, ncols = dims
    t = side // LANES
    for part in range(2):
        for j in range(ncols // LANES):
            lanes = slice(j * LANES, (j + 1) * LANES)
            if j < t:
                top = own[part, j, 0:side, :] - 0.25 * (
                    left_ab[part, j, 0:side, :] + above_a[part, j])
                low = own[part, j, side:, :] - 0.25 * left_ab[part, j, side:, :]
            else:
                top = own[part, j, 0:side, :] - 0.25 * above_b[part, j - t]
                low = own[part, j, side:, :]
            object_out[part, 0:side, lanes] = top
            object_out[part, side:, lanes] = low
        for j in range(t):
            probe_out[part, :, j * LANES:(j + 1) * LANES] = (
                probe[part, j] - rate * (sum_one[part, j] + sum_two[part, j]))


def call(kernel, dims, slots, scalars, vectors, plain, outs, extra, name):
    side, nrows, ncols = dims
    big = (2, (ncols + side) // LANES, nrows + side, LANES)
    smem = pl.BlockSpec(memory_space=pltpu.SMEM)
    vmem = pl.BlockSpec(memory_space=pltpu.VMEM)
    anywhere = pl.BlockSpec(memory_space=pl.ANY)
    return pl.pallas_call(
        kernel,
        out_shape=[jax.ShapeDtypeStruct(shape, F32) for shape in outs],
        in_specs=[smem] * len(scalars) + [vmem] * len(vectors) + [anywhere] * len(plain),
        out_specs=[vmem if i == 1 else anywhere for i in range(len(outs))],
        scratch_shapes=[
            pltpu.VMEM(big, F32),
            pltpu.VMEM(big, F32),
            pltpu.VMEM((slots, side, side), BF16),
        ] + [pltpu.VMEM((2 * side, side), BF16)] * 4
        + [pltpu.VMEM((2, side // LANES, side, LANES), F32)] * 2
        + [pltpu.VMEM((side, 2 * side), F32)] * 2
        + [pltpu.VMEM(shape, F32) for shape in extra] + [
            pltpu.SemaphoreType.DMA((slots,)),
            pltpu.SemaphoreType.DMA((48,)),
        ],
        compiler_params=pltpu.CompilerParams(vmem_limit_bytes=48 * 1024 * 1024),
        name=name,
    )(*scalars, *vectors, *plain)


def swap(shares):
    return lax.all_to_all(shares, ("tile", "row"), 0, 0, tiled=True)


def hand_out(mine, shape):
    given = pl.pallas_call(
        share_kernel, out_shape=jax.ShapeDtypeStruct(mine.shape, F32), name="sum_shares",
    )(mine)
    return swap(given).reshape(shape)


def join(left_c, right_c, from_left, from_right):
    anywhere = pl.BlockSpec(memory_space=pl.ANY)
    block = (4,) + left_c.shape[1:]
    return pl.pallas_call(
        join_kernel,
        out_shape=[jax.ShapeDtypeStruct(left_c.shape, F32)] * 2,
        in_specs=[anywhere] * 4,
        out_specs=[anywhere] * 2,
        scratch_shapes=[pltpu.VMEM(block, F32), pltpu.VMEM(block, F32),
                        pltpu.SemaphoreType.DMA((8,)), pltpu.SemaphoreType.DMA((4,))],
        compiler_params=pltpu.CompilerParams(vmem_limit_bytes=16 * 1024 * 1024),
        name="join_corners",
    )(left_c, right_c, from_left, from_right)


def local(object_field, probe, intensity, pool_rows, pool_cols, batch, live):
    side = probe.shape[1]
    nrows, ncols = object_field.shape[1:]
    dims = (side, nrows, ncols)
    slots = batch.shape[1]
    t = side // LANES
    total = (ncols + side) // LANES
    devices = lax.axis_size("tile") * lax.axis_size("row")
    probe_rate = 0.125 / math.sqrt(LIVE * devices)
    forward, backward = tables(side)
    forward, backward = jnp.asarray(forward), jnp.asarray(backward)
    current = probe.reshape(2, side, t, LANES).transpose(0, 2, 1, 3)

    below_a = passed_along(object_field[:, :side, :side], "row", -1)
    beside = passed_along(object_field[:, :, :side], "tile", -1)
    below_b = passed_along(object_field[:, :side, side:], "row", -1)
    corner = passed_along(below_a, "tile", -1)

    scalars = (batch, live, pool_rows, pool_cols)
    corners = (2, 2, t, side, LANES)
    edge_b = (2, ncols // LANES - t, side, LANES)
    edge_r = (2, t, nrows - side, LANES)
    part, gprobe, right_c, left_c, down_b, up_b, right_b, left_b = call(
        functools.partial(first_kernel, dims), dims, slots, scalars, (forward, backward, current),
        (intensity, object_field, below_a, below_b, beside, corner),
        [(2, total, nrows + side, LANES), current.shape, corners, corners,
         edge_b, edge_b, edge_r, edge_r], [], "first_iteration")

    from_left_c = passed_along(right_c, "tile", 1)
    from_right_c = passed_along(left_c, "tile", -1)
    from_up_b = passed_along(down_b, "row", 1)
    from_down_b = passed_along(up_b, "row", -1)
    mine = swap(gprobe.reshape(devices, -1, LANES))
    mine, from_left_c, from_right_c = lax.optimization_barrier((mine, from_left_c, from_right_c))
    down_c, up_c = join(left_c, right_c, from_left_c, from_right_c)
    from_up_c = passed_along(down_c, "row", 1)
    from_down_c = passed_along(up_c, "row", -1)
    mine, right_b, left_b, from_up_b, from_down_b, _ = lax.optimization_barrier(
        (mine, right_b, left_b, from_up_b, from_down_b, down_c))
    from_left_b = passed_along(right_b, "tile", 1)
    from_right_b = passed_along(left_b, "tile", -1)
    sum_one = hand_out(mine, current.shape)

    edge = jnp.stack([
        (lax.axis_index("row") == lax.axis_size("row") - 1).astype(jnp.int32),
        (lax.axis_index("tile") == lax.axis_size("tile") - 1).astype(jnp.int32)])
    own, gprobe, right_c, right_ab, down_a, down_b = call(
        functools.partial(second_kernel, dims, probe_rate), dims, slots, scalars + (edge,),
        (forward, backward, current, sum_one),
        (intensity, part, from_left_c, from_right_c, from_up_c, from_down_c,
         from_up_b, from_down_b, from_left_b, from_right_b),
        [(2, ncols // LANES, nrows, LANES), current.shape, (2, t, side, LANES),
         (2, t, nrows, LANES), (2, t, side, LANES), edge_b],
        [current.shape, corners, corners, corners, corners, edge_b, edge_b, edge_r, edge_r],
        "second_iteration")

    from_left_c = passed_along(right_c, "tile", 1)
    above_b = passed_along(down_b, "row", 1)
    mine = swap(gprobe.reshape(devices, -1, LANES))
    down_a = down_a + from_left_c
    above_a = passed_along(down_a, "row", 1)
    mine, right_ab, above_b, _ = lax.optimization_barrier((mine, right_ab, above_b, down_a))
    left_ab = passed_along(right_ab, "tile", 1)
    sum_two = hand_out(mine, current.shape)
    return pl.pallas_call(
        functools.partial(last_kernel, dims, probe_rate),
        out_shape=[jax.ShapeDtypeStruct(object_field.shape, F32),
                   jax.ShapeDtypeStruct(probe.shape, F32)],
        compiler_params=pltpu.CompilerParams(vmem_limit_bytes=48 * 1024 * 1024),
        name="last_update",
    )(own, left_ab, above_a, above_b, current, sum_one, sum_two)


def solution(mesh):
    placed = (
        P(None, "row", "tile"),
        P(),
        P(("tile", "row"), None, None),
        P(("tile", "row")),
        P(("tile", "row")),
        P(None, ("tile", "row")),
        P(None, ("tile", "row")),
    )
    return jax.shard_map(
        local, mesh=mesh, in_specs=placed, out_specs=(P(None, "row", "tile"), P()), check_vma=False
    )
```

```python
import functools
import math

import jax
import jax.numpy as jnp
import numpy as np
from jax import lax
from jax.experimental import pallas as pl
from jax.experimental.pallas import tpu as pltpu
from jax.sharding import PartitionSpec as P

LIVE = 6
LANES = 128
F32 = jnp.float32
BF16 = jnp.bfloat16


def passed_along(value, axis, steps):
    count = lax.axis_size(axis)
    first, last = (max(0, -steps), min(count, count - steps))
    return lax.ppermute(value, axis, [(source, source + steps) for source in range(first, last)])


def tables(length):
    counter = np.arange(length, dtype=np.int32)
    product = counter[:, None] * counter[None, :] % length
    angle = product.astype(np.float32) * np.float32(2.0 * math.pi / length)
    factor = np.float32(1.0 / math.sqrt(length))
    cosine = (np.cos(angle) * factor).astype(BF16)
    sine = (np.sin(angle) * factor).astype(BF16)
    forward = np.block([[cosine, sine], [-sine, cosine]])
    backward = np.block([[cosine, -sine], [sine, cosine]])
    return forward, backward


def mul(left, right):
    return jnp.dot(left, right, preferred_element_type=F32)


def start_slots(step, batch, intensity, measured, sems):
    copies = []
    for s in range(batch.shape[1]):
        copies.append(
            pltpu.make_async_copy(intensity.at[batch[step, s]], measured.at[s], sems.at[s]))
    for copy in copies:
        copy.start()
    return copies


def clear(grad, gprobe, waves, patches):
    grad[...] = jnp.zeros_like(grad)
    gprobe[...] = jnp.zeros_like(gprobe)
    waves[1][...] = jnp.zeros_like(waves[1])
    patches[1][...] = jnp.zeros_like(patches[1])


def slot_loop(step, side, batch, live, rows, cols, mats, probe, ext, grad, gprobe,
              measured, exits, waves, patches, back):
    forward, backward = mats
    lane = lax.broadcasted_iota(jnp.int32, (side, LANES), 1)
    halves = side // LANES
    count = live[step, 0]

    def corner_of(s):
        stored = batch[step, s]
        col = cols[stored]
        return rows[stored], col // LANES, col % LANES

    def window(part, tile, row, shift):
        turn = (LANES - shift) & (LANES - 1)
        turned = [
            pltpu.roll(ext[part, tile + j, pl.ds(row, side), :], turn, 1) for j in range(halves + 1)
        ]
        keep = lane < LANES - shift
        return [jnp.where(keep, turned[j], turned[j + 1]) for j in range(halves)]

    def place(part, tile, row, shift, values):
        turned = [pltpu.roll(v, shift, 1) for v in values]
        keep = lane >= shift
        zero = jnp.zeros((side, LANES), F32)
        for j in range(halves + 1):
            here = turned[j] if j < halves else zero
            prior = turned[j - 1] if j else zero
            at = (part, tile + j, pl.ds(row, side), slice(None))
            grad[at] = grad[at] + jnp.where(keep, here, prior)

    def first_half(s, buffer, alive):
        row, tile, shift = corner_of(s)
        exit_in, wave, patch = exits[buffer], waves[buffer], patches[buffer]
        patch_r = window(0, tile, row, shift)
        patch_i = window(1, tile, row, shift)
        for j in range(halves):
            p_r, p_i = probe[0, j], probe[1, j]
            at = slice(j * LANES, (j + 1) * LANES)
            patch[0, j] = patch_r[j]
            patch[1, j] = patch_i[j]
            exit_in[0:side, at] = (p_r * patch_r[j] - p_i * patch_i[j]).astype(BF16)
            exit_in[side:, at] = (p_r * patch_i[j] + p_i * patch_r[j]).astype(BF16)
        half = mul(forward[...], exit_in[...]).astype(BF16)
        far = mul(jnp.concatenate([half[:side], half[side:]], axis=1), backward[...])
        far_r, far_i = far[:, :side], far[:, side:]
        excess = far_r * far_r + far_i * far_i - measured[s].astype(F32)
        if alive is not None:
            excess = excess * alive
        wave[0:side, :] = (excess * far_r).astype(BF16)
        wave[side:, :] = (excess * far_i).astype(BF16)

    def second_half(s, buffer):
        row, tile, shift = corner_of(s)
        wave, patch = waves[buffer], patches[buffer]
        mid = mul(backward[...], wave[...]).astype(BF16)
        back[buffer][...] = mul(jnp.concatenate([mid[:side], mid[side:]], axis=1), forward[...])
        object_r, object_i = [], []
        for j in range(halves):
            p_r, p_i = probe[0, j], probe[1, j]
            o_r, o_i = patch[0, j], patch[1, j]
            b_r = back[buffer][:, j * LANES:(j + 1) * LANES]
            b_i = back[buffer][:, side + j * LANES:side + (j + 1) * LANES]
            object_r.append(p_r * b_r + p_i * b_i)
            object_i.append(p_r * b_i - p_i * b_r)
            gprobe[0, j] += o_r * b_r + o_i * b_i
            gprobe[1, j] += o_r * b_i - o_i * b_r
        place(0, tile, row, shift, object_r)
        place(1, tile, row, shift, object_i)

    def two_slots(k, carry):
        even = 2 * k
        odd = jnp.minimum(even + 1, batch.shape[1] - 1)
        alive = jnp.where(even + 1 < count, 1.0, 0.0).astype(F32)
        second_half(jnp.maximum(even - 1, 0), 1)
        first_half(even, 0, None)
        second_half(even, 0)
        first_half(odd, 1, alive)
        return carry

    pairs = (count + 1) // 2
    lax.fori_loop(0, pairs, two_slots, 0)
    second_half(jnp.minimum(2 * pairs - 1, batch.shape[1] - 1), 1)


def tiled_copies(field, part_rows, part_cols, ext, row0, col0):
    pairs = []
    for part in range(2):
        for j in range(part_cols // LANES):
            pairs.append((
                field.at[part, :, pl.ds(j * LANES, LANES)],
                ext.at[part, col0 // LANES + j, pl.ds(row0, part_rows), :],
            ))
    return pairs


def run_copies(pairs, sems, base=0):
    copies = [pltpu.make_async_copy(src, dst, sems.at[base + i]) for i, (src, dst) in enumerate(pairs)]
    for copy in copies:
        copy.start()
    return copies


def first_kernel(dims, batch, live, rows, cols, forward, backward, probe, intensity,
                 field, below_a, below_b, beside, corner,
                 middle, gprobe, right_col, left_col, down_b, up_b,
                 ext, grad, measured, exit_0, exit_1, wave_0, wave_1, patch_0, patch_1,
                 back_0, back_1, sems, moves):
    side, nrows, ncols = dims
    pairs = tiled_copies(field, nrows, ncols, ext, 0, 0)
    pairs += tiled_copies(below_a, side, side, ext, nrows, 0)
    pairs += tiled_copies(below_b, side, ncols - side, ext, nrows, side)
    pairs += tiled_copies(beside, nrows, side, ext, 0, ncols)
    pairs += tiled_copies(corner, side, side, ext, nrows, ncols)
    copies = run_copies(pairs, moves)
    copies += start_slots(0, batch, intensity, measured, sems)
    waves, patches = (wave_0, wave_1), (patch_0, patch_1)
    clear(grad, gprobe, waves, patches)
    for copy in copies:
        copy.wait()
    slot_loop(0, side, batch, live, rows, cols, (forward, backward), probe, ext, grad, gprobe,
              measured, (exit_0, exit_1), waves, patches, (back_0, back_1))
    t = side // LANES
    last = ncols // LANES
    a_rows, c_rows = pl.ds(0, side), pl.ds(nrows, side)
    b_rows = pl.ds(side, nrows - side)
    left, mid, right = pl.ds(0, t), pl.ds(t, last - t), pl.ds(last, t)
    copies = run_copies([
        (grad.at[:, right], right_col),
        (grad.at[:, left], left_col),
        (grad.at[:, mid, c_rows, :], down_b),
        (grad.at[:, mid, a_rows, :], up_b),
        (grad.at[:, mid, b_rows, :], middle),
    ], moves)
    for copy in copies:
        copy.wait()


def join_kernel(left_col, right_col, from_left, from_right, down, up, own, other, moves, stores):
    side = down.shape[3]
    nrows = left_col.shape[2] - side
    places = []
    for row, target in ((nrows, down), (0, up)):
        band = pl.ds(row, side)
        for which, (mine, received) in enumerate(((left_col, from_left), (right_col, from_right))):
            places.append((mine.at[:, :, band, :], received.at[:, :, band, :], target.at[which]))
    loads = []
    for i, (mine, received, target) in enumerate(places):
        loads.append((pltpu.make_async_copy(mine, own.at[i], moves.at[2 * i]),
                      pltpu.make_async_copy(received, other.at[i], moves.at[2 * i + 1])))
    for pair in loads:
        for copy in pair:
            copy.start()
    copies = []
    for i, (mine, received, target) in enumerate(places):
        for copy in loads[i]:
            copy.wait()
        own[i] = own[i] + other[i]
        copies.append(pltpu.make_async_copy(own.at[i], target, stores.at[i]))
        copies[-1].start()
    for copy in copies:
        copy.wait()


def update_kernel(dims, edge, field, below_a, below_b, beside, corner,
                  middle, left_col, right_col, down_b, up_b,
                  from_left, from_right, from_up, from_down, part):
    side, nrows, ncols = dims
    t = side // LANES
    last = ncols // LANES
    for p in range(2):
        for j in range(last + t):
            lanes = slice(j * LANES % side, j * LANES % side + LANES)
            at = slice(j * LANES, (j + 1) * LANES)
            if j < last:
                old = field[p, :, at]
                low = below_a[p, :, lanes] if j < t else below_b[p, :, j * LANES - side:at.stop - side]
            else:
                old = beside[p, :, lanes]
                low = corner[p, :, lanes]
            if j < t:
                step = left_col[p, j] + from_left[p, j]
                part[p, j, 0:nrows, :] = old - 0.25 * step[:nrows]
                part[p, j, nrows:, :] = low - 0.25 * step[nrows:]
            elif j < last:
                part[p, j, 0:side, :] = old[:side] - 0.25 * (up_b[p, j - t] + from_up[p, j - t])
                part[p, j, side:nrows, :] = old[side:] - 0.25 * middle[p, j - t]
                part[p, j, nrows:, :] = low - 0.25 * (down_b[p, j - t] + from_down[p, j - t])
            else:
                step = right_col[p, j - last] + from_right[p, j - last]
                part[p, j, 0:nrows, :] = old - 0.25 * step[:nrows]
                part[p, j, nrows:, :] = low - 0.25 * step[nrows:]

    @pl.when(edge[0] == 1)
    def _():
        part[:, :, nrows:, :] = jnp.zeros((2, last + t, side, LANES), F32)

    @pl.when(edge[1] == 1)
    def _():
        part[:, last:, :, :] = jnp.zeros((2, t, nrows + side, LANES), F32)


def share_kernel(received, given):
    summed = received[0]
    for i in range(1, received.shape[0]):
        summed = summed + received[i]
    for i in range(received.shape[0]):
        given[i] = summed


def second_kernel(dims, rate, batch, live, rows, cols, edge, forward, backward, probe, summed,
                  intensity, part_in, from_up, from_down,
                  own_out, gprobe, right_col, down_a, down_b,
                  ext, grad, measured, exit_0, exit_1, wave_0, wave_1, patch_0, patch_1,
                  back_0, back_1, now, u_in, d_in, sems, moves):
    side, nrows, ncols = dims
    t = side // LANES
    last = ncols // LANES
    copies = run_copies([(part_in, ext), (from_up, u_in), (from_down, d_in)], moves)
    copies += start_slots(1, batch, intensity, measured, sems)
    waves, patches = (wave_0, wave_1), (patch_0, patch_1)
    clear(grad, gprobe, waves, patches)
    now[...] = probe[...] - rate * summed[...]
    for copy in copies:
        copy.wait()
    a_rows, c_rows = slice(0, side), slice(nrows, nrows + side)
    left, right = slice(0, t), slice(last, last + t)
    ext[:, left, a_rows, :] -= 0.25 * u_in[0]
    ext[:, left, c_rows, :] -= 0.25 * d_in[0]

    @pl.when(edge[1] == 0)
    def _():
        ext[:, right, a_rows, :] -= 0.25 * u_in[1]
        ext[:, right, c_rows, :] -= 0.25 * d_in[1]

    slot_loop(1, side, batch, live, rows, cols, (forward, backward), now, ext, grad, gprobe,
              measured, (exit_0, exit_1), waves, patches, (back_0, back_1))
    c_rows, own_rows = pl.ds(nrows, side), pl.ds(0, nrows)
    own_cols, right = pl.ds(0, last), pl.ds(last, t)
    pairs = [
        (grad.at[:, right], right_col),
        (grad.at[:, pl.ds(t, last - t), c_rows, :], down_b),
        (grad.at[:, pl.ds(0, t), c_rows, :], down_a),
    ]
    copies = run_copies(pairs, moves)
    ext[:, 0:last, 0:nrows, :] = ext[:, 0:last, 0:nrows, :] - 0.25 * grad[:, 0:last, 0:nrows, :]
    copies += run_copies([(ext.at[:, own_cols, own_rows, :], own_out)], moves, len(pairs))
    for copy in copies:
        copy.wait()


def object_kernel(dims, own, left_col, above_a, above_b, object_out):
    side, nrows, ncols = dims
    t = side // LANES
    for part in range(2):
        for j in range(ncols // LANES):
            lanes = slice(j * LANES, (j + 1) * LANES)
            if j < t:
                top = own[part, j, 0:side, :] - 0.25 * (
                    left_col[part, j, 0:side, :] + above_a[part, j])
                low = own[part, j, side:, :] - 0.25 * left_col[part, j, side:nrows, :]
            else:
                top = own[part, j, 0:side, :] - 0.25 * above_b[part, j - t]
                low = own[part, j, side:, :]
            object_out[part, 0:side, lanes] = top
            object_out[part, side:, lanes] = low


def probe_kernel(rate, probe, sum_one, sum_two, probe_out):
    for part in range(2):
        for j in range(probe.shape[1]):
            probe_out[part, :, j * LANES:(j + 1) * LANES] = (
                probe[part, j] - rate * (sum_one[part, j] + sum_two[part, j]))


def call(kernel, dims, slots, scalars, vectors, plain, outs, extra, name):
    side, nrows, ncols = dims
    big = (2, (ncols + side) // LANES, nrows + side, LANES)
    smem = pl.BlockSpec(memory_space=pltpu.SMEM)
    vmem = pl.BlockSpec(memory_space=pltpu.VMEM)
    anywhere = pl.BlockSpec(memory_space=pltpu.HBM)
    return pl.pallas_call(
        kernel,
        out_shape=[jax.ShapeDtypeStruct(shape, F32) for shape in outs],
        in_specs=[smem] * len(scalars) + [vmem] * len(vectors) + [anywhere] * len(plain),
        out_specs=[vmem if i == 1 else anywhere for i in range(len(outs))],
        scratch_shapes=[
            pltpu.VMEM(big, F32),
            pltpu.VMEM(big, F32),
            pltpu.VMEM((slots, side, side), BF16),
        ] + [pltpu.VMEM((2 * side, side), BF16)] * 4
        + [pltpu.VMEM((2, side // LANES, side, LANES), F32)] * 2
        + [pltpu.VMEM((side, 2 * side), F32)] * 2
        + [pltpu.VMEM(shape, F32) for shape in extra] + [
            pltpu.SemaphoreType.DMA((slots,)),
            pltpu.SemaphoreType.DMA((48,)),
        ],
        compiler_params=pltpu.CompilerParams(vmem_limit_bytes=48 * 1024 * 1024),
        name=name,
    )(*scalars, *vectors, *plain)


def swap(shares):
    return lax.all_to_all(shares, ("tile", "row"), 0, 0, tiled=True)


def hand_out(mine, shape):
    given = pl.pallas_call(
        share_kernel, out_shape=jax.ShapeDtypeStruct(mine.shape, F32), name="sum_shares",
    )(mine)
    return swap(given).reshape(shape)


def join(left_col, right_col, from_left, from_right, side):
    anywhere = pl.BlockSpec(memory_space=pltpu.HBM)
    corners = (2,) + left_col.shape[:2] + (side, LANES)
    block = (4,) + corners[1:]
    return pl.pallas_call(
        join_kernel,
        out_shape=[jax.ShapeDtypeStruct(corners, F32)] * 2,
        in_specs=[anywhere] * 4,
        out_specs=[anywhere] * 2,
        scratch_shapes=[pltpu.VMEM(block, F32), pltpu.VMEM(block, F32),
                        pltpu.SemaphoreType.DMA((8,)), pltpu.SemaphoreType.DMA((4,))],
        compiler_params=pltpu.CompilerParams(vmem_limit_bytes=16 * 1024 * 1024),
        name="join_corners",
    )(left_col, right_col, from_left, from_right)


def simple(kernel, shape, name, scalars, vectors):
    smem = pl.BlockSpec(memory_space=pltpu.SMEM)
    vmem = pl.BlockSpec(memory_space=pltpu.VMEM)
    return pl.pallas_call(
        kernel,
        out_shape=jax.ShapeDtypeStruct(shape, F32),
        in_specs=[smem] * len(scalars) + [vmem] * len(vectors),
        out_specs=vmem,
        compiler_params=pltpu.CompilerParams(vmem_limit_bytes=48 * 1024 * 1024),
        name=name,
    )(*scalars, *vectors)


def local(object_field, probe, intensity, pool_rows, pool_cols, batch, live):
    side = probe.shape[1]
    nrows, ncols = object_field.shape[1:]
    dims = (side, nrows, ncols)
    slots = batch.shape[1]
    t = side // LANES
    total = (ncols + side) // LANES
    devices = lax.axis_size("tile") * lax.axis_size("row")
    probe_rate = 0.125 / math.sqrt(LIVE * devices)
    forward, backward = tables(side)
    forward, backward = jnp.asarray(forward), jnp.asarray(backward)
    current = probe.reshape(2, side, t, LANES).transpose(0, 2, 1, 3)

    first, rest = lax.optimization_barrier((object_field[:, :side, :side], object_field))
    below_a = passed_along(first, "row", -1)
    beside = passed_along(rest[:, :, :side], "tile", -1)
    below_b = passed_along(rest[:, :side, side:], "row", -1)
    corner = passed_along(below_a, "tile", -1)

    scalars = (batch, live, pool_rows, pool_cols)
    halo = (object_field, below_a, below_b, beside, corner)
    column = (2, t, nrows + side, LANES)
    strip = (2, ncols // LANES - t, side, LANES)
    middle = (2, ncols // LANES - t, nrows - side, LANES)
    middle, gprobe, right_col, left_col, down_b, up_b = call(
        functools.partial(first_kernel, dims), dims, slots, scalars, (forward, backward, current),
        (intensity,) + halo,
        [middle, current.shape, column, column, strip, strip], [], "first_iteration")

    from_left = passed_along(right_col, "tile", 1)
    from_right = passed_along(left_col, "tile", -1)
    from_up_b = passed_along(down_b, "row", 1)
    from_down_b = passed_along(up_b, "row", -1)
    mine = swap(gprobe.reshape(devices, -1, LANES))
    mine, from_left, from_right = lax.optimization_barrier((mine, from_left, from_right))
    down_c, up_c = join(left_col, right_col, from_left, from_right, side)
    from_up_c = passed_along(down_c, "row", 1)
    from_down_c = passed_along(up_c, "row", -1)
    mine, from_up_b, from_down_b, _ = lax.optimization_barrier(
        (mine, from_up_b, from_down_b, down_c))
    sum_one = hand_out(mine, current.shape)
    edge = jnp.stack([
        (lax.axis_index("row") == lax.axis_size("row") - 1).astype(jnp.int32),
        (lax.axis_index("tile") == lax.axis_size("tile") - 1).astype(jnp.int32)])
    part = simple(
        functools.partial(update_kernel, dims), (2, total, nrows + side, LANES), "update_object",
        (edge,), halo + (middle, left_col, right_col, down_b, up_b,
                         from_left, from_right, from_up_b, from_down_b))

    corners = (2, 2, t, side, LANES)
    own, gprobe, right_col, down_a, down_b = call(
        functools.partial(second_kernel, dims, probe_rate), dims, slots, scalars + (edge,),
        (forward, backward, current, sum_one), (intensity, part, from_up_c, from_down_c),
        [(2, ncols // LANES, nrows, LANES), current.shape, column, (2, t, side, LANES), strip],
        [current.shape, corners, corners], "second_iteration")

    from_left = passed_along(right_col, "tile", 1)
    above_b = passed_along(down_b, "row", 1)
    mine = swap(gprobe.reshape(devices, -1, LANES))
    down_a = down_a + from_left[:, :, nrows:, :]
    above_a = passed_along(down_a, "row", 1)
    mine, above_b, _ = lax.optimization_barrier((mine, above_b, down_a))
    sum_two = hand_out(mine, current.shape)
    object_out = simple(functools.partial(object_kernel, dims), object_field.shape, "last_object",
                        (), (own, from_left, above_a, above_b))
    probe_out = simple(functools.partial(probe_kernel, probe_rate), probe.shape, "last_probe",
                       (), (current, sum_one, sum_two))
    return (object_out, probe_out)


def solution(mesh):
    placed = (
        P(None, "row", "tile"),
        P(),
        P(("tile", "row"), None, None),
        P(("tile", "row")),
        P(("tile", "row")),
        P(None, ("tile", "row")),
        P(None, ("tile", "row")),
    )
    return jax.shard_map(
        local, mesh=mesh, in_specs=placed, out_specs=(P(None, "row", "tile"), P()), check_vma=False
    )
```

```python
import functools
import math

import jax
import jax.numpy as jnp
import numpy as np
from jax import lax
from jax.experimental import pallas as pl
from jax.experimental.pallas import tpu as pltpu
from jax.sharding import PartitionSpec as P

LIVE = 6
LANES = 128
MIB = 1024 * 1024
F32 = jnp.float32
BF16 = jnp.bfloat16


def passed_along(value, axis, steps):
    count = lax.axis_size(axis)
    first, last = (max(0, -steps), min(count, count - steps))
    return lax.ppermute(value, axis, [(source, source + steps) for source in range(first, last)])


def tables(length):
    counter = np.arange(length, dtype=np.int32)
    product = counter[:, None] * counter[None, :] % length
    angle = product.astype(np.float32) * np.float32(2.0 * math.pi / length)
    factor = np.float32(1.0 / math.sqrt(length))
    cosine = (np.cos(angle) * factor).astype(BF16)
    sine = (np.sin(angle) * factor).astype(BF16)
    forward = np.block([[cosine, sine], [-sine, cosine]])
    backward = np.block([[cosine, -sine], [sine, cosine]])
    return forward, backward


def mul(left, right):
    return jnp.dot(left, right, preferred_element_type=F32)


def start_slots(step, batch, intensity, measured, sems):
    copies = []
    for s in range(batch.shape[1]):
        copies.append(
            pltpu.make_async_copy(intensity.at[batch[step, s]], measured.at[s], sems.at[s]))
    for copy in copies:
        copy.start()
    return copies


def clear(grad, gprobe, waves, patches):
    grad[...] = jnp.zeros_like(grad)
    gprobe[...] = jnp.zeros_like(gprobe)
    waves[1][...] = jnp.zeros_like(waves[1])
    patches[1][...] = jnp.zeros_like(patches[1])


def slot_loop(step, side, batch, live, rows, cols, mats, probe, ext, grad, gprobe,
              measured, exits, waves, patches):
    forward, backward = mats
    lane = lax.broadcasted_iota(jnp.int32, (side, LANES), 1)
    halves = side // LANES
    count = live[step, 0]

    def corner_of(s):
        stored = batch[step, s]
        col = cols[stored]
        return rows[stored], col // LANES, col % LANES

    def window(part, tile, row, shift):
        turn = (LANES - shift) & (LANES - 1)
        turned = [
            pltpu.roll(ext[part, tile + j, pl.ds(row, side), :], turn, 1) for j in range(halves + 1)
        ]
        keep = lane < LANES - shift
        return [jnp.where(keep, turned[j], turned[j + 1]) for j in range(halves)]

    def place(part, tile, row, shift, values):
        turned = [pltpu.roll(v, shift, 1) for v in values]
        keep = lane >= shift
        zero = jnp.zeros((side, LANES), F32)
        for j in range(halves + 1):
            here = turned[j] if j < halves else zero
            prior = turned[j - 1] if j else zero
            at = (part, tile + j, pl.ds(row, side), slice(None))
            grad[at] = grad[at] + jnp.where(keep, here, prior)

    def first_half(s, buffer, alive):
        row, tile, shift = corner_of(s)
        exit_in, wave, patch = exits[buffer], waves[buffer], patches[buffer]
        patch_r = window(0, tile, row, shift)
        patch_i = window(1, tile, row, shift)
        for j in range(halves):
            p_r, p_i = probe[0, j], probe[1, j]
            at = slice(j * LANES, (j + 1) * LANES)
            patch[0, j] = patch_r[j]
            patch[1, j] = patch_i[j]
            exit_in[0:side, at] = (p_r * patch_r[j] - p_i * patch_i[j]).astype(BF16)
            exit_in[side:, at] = (p_r * patch_i[j] + p_i * patch_r[j]).astype(BF16)
        half = mul(forward[...], exit_in[...]).astype(BF16)
        far = mul(jnp.concatenate([half[:side], half[side:]], axis=1), backward[...])
        far_r, far_i = far[:, :side], far[:, side:]
        excess = far_r * far_r + far_i * far_i - measured[s].astype(F32)
        if alive is not None:
            excess = excess * alive
        wave[0:side, :] = (excess * far_r).astype(BF16)
        wave[side:, :] = (excess * far_i).astype(BF16)

    def second_half(s, buffer):
        row, tile, shift = corner_of(s)
        wave, patch = waves[buffer], patches[buffer]
        mid = mul(backward[...], wave[...]).astype(BF16)
        back = mul(jnp.concatenate([mid[:side], mid[side:]], axis=1), forward[...])
        object_r, object_i = [], []
        for j in range(halves):
            p_r, p_i = probe[0, j], probe[1, j]
            o_r, o_i = patch[0, j], patch[1, j]
            b_r = back[:, j * LANES:(j + 1) * LANES]
            b_i = back[:, side + j * LANES:side + (j + 1) * LANES]
            object_r.append(p_r * b_r + p_i * b_i)
            object_i.append(p_r * b_i - p_i * b_r)
            gprobe[0, j] += o_r * b_r + o_i * b_i
            gprobe[1, j] += o_r * b_i - o_i * b_r
        place(0, tile, row, shift, object_r)
        place(1, tile, row, shift, object_i)

    def two_slots(k, carry):
        even = 2 * k
        odd = jnp.minimum(even + 1, batch.shape[1] - 1)
        alive = jnp.where(even + 1 < count, 1.0, 0.0).astype(F32)
        second_half(jnp.maximum(even - 1, 0), 1)
        first_half(even, 0, None)
        second_half(even, 0)
        first_half(odd, 1, alive)
        return carry

    pairs = (count + 1) // 2
    lax.fori_loop(0, pairs, two_slots, 0)
    second_half(jnp.minimum(2 * pairs - 1, batch.shape[1] - 1), 1)


def tiled_copies(field, part_rows, part_cols, ext, row0, col0):
    pairs = []
    for part in range(2):
        for j in range(part_cols // LANES):
            pairs.append((
                field.at[part, :, pl.ds(j * LANES, LANES)],
                ext.at[part, col0 // LANES + j, pl.ds(row0, part_rows), :],
            ))
    return pairs


def run_copies(pairs, sems, base=0):
    copies = [pltpu.make_async_copy(src, dst, sems.at[base + i]) for i, (src, dst) in enumerate(pairs)]
    for copy in copies:
        copy.start()
    return copies


def first_kernel(dims, batch, live, rows, cols, forward, backward, probe, intensity,
                 field, below_a, below_b, beside, corner,
                 part_out, gprobe_out, right_c, left_c, right_b, left_b, down_b, up_b,
                 ext, grad, measured, exit_0, exit_1, wave_0, wave_1, patch_0, patch_1,
                 gprobe, sems, moves):
    side, nrows, ncols = dims
    pairs = tiled_copies(field, nrows, ncols, ext, 0, 0)
    pairs += tiled_copies(below_a, side, side, ext, nrows, 0)
    pairs += tiled_copies(below_b, side, ncols - side, ext, nrows, side)
    pairs += tiled_copies(beside, nrows, side, ext, 0, ncols)
    pairs += tiled_copies(corner, side, side, ext, nrows, ncols)
    copies = run_copies(pairs, moves)
    copies += start_slots(0, batch, intensity, measured, sems)
    waves, patches = (wave_0, wave_1), (patch_0, patch_1)
    clear(grad, gprobe, waves, patches)
    for copy in copies:
        copy.wait()
    slot_loop(0, side, batch, live, rows, cols, (forward, backward), probe, ext, grad, gprobe,
              measured, (exit_0, exit_1), waves, patches)
    t = side // LANES
    last = ncols // LANES
    a_rows, c_rows = pl.ds(0, side), pl.ds(nrows, side)
    b_rows = pl.ds(side, nrows - side)
    left, mid, right = pl.ds(0, t), pl.ds(t, last - t), pl.ds(last, t)
    pairs = [
        (gprobe, gprobe_out),
        (grad.at[:, right, a_rows, :], right_c.at[0]),
        (grad.at[:, right, c_rows, :], right_c.at[1]),
        (grad.at[:, left, a_rows, :], left_c.at[0]),
        (grad.at[:, left, c_rows, :], left_c.at[1]),
        (grad.at[:, right, b_rows, :], right_b),
        (grad.at[:, left, b_rows, :], left_b),
        (grad.at[:, mid, c_rows, :], down_b),
        (grad.at[:, mid, a_rows, :], up_b),
    ]
    copies = run_copies(pairs, moves)
    ext[...] = ext[...] - 0.25 * grad[...]
    copies += run_copies([(ext, part_out)], moves, len(pairs))
    for copy in copies:
        copy.wait()


def join_kernel(left_c, right_c, from_left, from_right, down, up, own, moves, stores):
    places = []
    for band, target in ((1, down), (0, up)):
        for which, (mine, received) in enumerate(((left_c, from_left), (right_c, from_right))):
            places.append((mine.at[band], received, band, target.at[which]))
    loads = [pltpu.make_async_copy(place[0], own.at[i], moves.at[i])
             for i, place in enumerate(places)]
    for copy in loads:
        copy.start()
    copies = []
    for i, (mine, received, band, target) in enumerate(places):
        loads[i].wait()
        own[i] = own[i] + received[band]
        copies.append(pltpu.make_async_copy(own.at[i], target, stores.at[i]))
        copies[-1].start()
    for copy in copies:
        copy.wait()


def share_kernel(received, given):
    summed = received[0]
    for i in range(1, received.shape[0]):
        summed = summed + received[i]
    for i in range(received.shape[0]):
        given[i] = summed


def second_kernel(dims, rate, batch, live, rows, cols, edge, forward, backward, probe,
                  summed, intensity, part_in, from_left_c, from_right_c, from_up_c, from_down_c,
                  from_left, from_right, from_up, from_down,
                  own_out, gprobe_out, right_c, right_ab, down_a, down_b,
                  ext, grad, measured, exit_0, exit_1, wave_0, wave_1, patch_0, patch_1,
                  gprobe, now, sems, moves):
    side, nrows, ncols = dims
    t = side // LANES
    last = ncols // LANES
    copies = run_copies([(part_in, ext)], moves)
    copies += start_slots(1, batch, intensity, measured, sems)
    waves, patches = (wave_0, wave_1), (patch_0, patch_1)
    clear(grad, gprobe, waves, patches)
    now[...] = probe[...] - rate * summed[...]
    for copy in copies:
        copy.wait()
    a_rows, c_rows = slice(0, side), slice(nrows, nrows + side)
    b_rows = slice(side, nrows)
    left, mid, right = slice(0, t), slice(t, last), slice(last, last + t)
    for rows_of, corner, strip, k in ((a_rows, from_up_c, from_up, 0),
                                      (c_rows, from_down_c, from_down, 1)):
        ext[:, left, rows_of, :] -= 0.25 * (corner[0] + from_left_c[k])
        ext[:, mid, rows_of, :] -= 0.25 * strip[...]
        ext[:, right, rows_of, :] -= 0.25 * (corner[1] + from_right_c[k])
    ext[:, left, b_rows, :] -= 0.25 * from_left[...]
    ext[:, right, b_rows, :] -= 0.25 * from_right[...]

    @pl.when(edge[0] == 1)
    def _():
        ext[:, :, c_rows, :] = jnp.zeros((2, last + t, side, LANES), F32)

    @pl.when(edge[1] == 1)
    def _():
        ext[:, right, :, :] = jnp.zeros((2, t, nrows + side, LANES), F32)

    slot_loop(1, side, batch, live, rows, cols, (forward, backward), now, ext, grad, gprobe,
              measured, (exit_0, exit_1), waves, patches)
    c_rows, own_rows = pl.ds(nrows, side), pl.ds(0, nrows)
    own_cols, right = pl.ds(0, last), pl.ds(last, t)
    pairs = [
        (gprobe, gprobe_out),
        (grad.at[:, right, c_rows, :], right_c),
        (grad.at[:, pl.ds(t, last - t), c_rows, :], down_b),
        (grad.at[:, pl.ds(0, t), c_rows, :], down_a),
        (grad.at[:, right, own_rows, :], right_ab),
    ]
    copies = run_copies(pairs, moves)
    ext[:, 0:last, 0:nrows, :] = ext[:, 0:last, 0:nrows, :] - 0.25 * grad[:, 0:last, 0:nrows, :]
    copies += run_copies([(ext.at[:, own_cols, own_rows, :], own_out)], moves, len(pairs))
    for copy in copies:
        copy.wait()


def object_kernel(dims, own, left_ab, above_a, above_b, object_out):
    side, nrows, ncols = dims
    t = side // LANES
    for part in range(2):
        for j in range(ncols // LANES):
            lanes = slice(j * LANES, (j + 1) * LANES)
            if j < t:
                top = own[part, j, 0:side, :] - 0.25 * (
                    left_ab[part, j, 0:side, :] + above_a[part, j])
                low = own[part, j, side:, :] - 0.25 * left_ab[part, j, side:, :]
            else:
                top = own[part, j, 0:side, :] - 0.25 * above_b[part, j - t]
                low = own[part, j, side:, :]
            object_out[part, 0:side, lanes] = top
            object_out[part, side:, lanes] = low


def probe_kernel(rate, probe, sum_one, sum_two, probe_out):
    for part in range(2):
        for j in range(probe.shape[1]):
            probe_out[part, :, j * LANES:(j + 1) * LANES] = (
                probe[part, j] - rate * (sum_one[part, j] + sum_two[part, j]))


def call(kernel, dims, slots, scalars, vectors, plain, received, outs, extra, limit,
         name):
    side, nrows, ncols = dims
    big = (2, (ncols + side) // LANES, nrows + side, LANES)
    smem = pl.BlockSpec(memory_space=pltpu.SMEM)
    vmem = pl.BlockSpec(memory_space=pltpu.VMEM)
    hbm = pl.BlockSpec(memory_space=pltpu.HBM)
    return pl.pallas_call(
        kernel,
        out_shape=[jax.ShapeDtypeStruct(shape, F32) for shape in outs],
        in_specs=([smem] * len(scalars) + [vmem] * len(vectors) + [hbm] * len(plain)
                  + [vmem] * len(received)),
        out_specs=[hbm] * len(outs),
        scratch_shapes=[
            pltpu.VMEM(big, F32),
            pltpu.VMEM(big, F32),
            pltpu.VMEM((slots, side, side), BF16),
        ] + [pltpu.VMEM((2 * side, side), BF16)] * 4
        + [pltpu.VMEM((2, side // LANES, side, LANES), F32)] * 3
        + [pltpu.VMEM(shape, F32) for shape in extra] + [
            pltpu.SemaphoreType.DMA((slots,)),
            pltpu.SemaphoreType.DMA((48,)),
        ],
        compiler_params=pltpu.CompilerParams(vmem_limit_bytes=limit * MIB),
        name=name,
    )(*scalars, *vectors, *plain, *received)


def swap(shares):
    return lax.all_to_all(shares, ("tile", "row"), 0, 0, tiled=True)


def add_up(mine):
    return pl.pallas_call(
        share_kernel, out_shape=jax.ShapeDtypeStruct(mine.shape, F32), name="sum_shares",
    )(mine)


def join(left_c, right_c, from_left, from_right):
    vmem = pl.BlockSpec(memory_space=pltpu.VMEM)
    hbm = pl.BlockSpec(memory_space=pltpu.HBM)
    return pl.pallas_call(
        join_kernel,
        out_shape=[jax.ShapeDtypeStruct(left_c.shape, F32)] * 2,
        in_specs=[hbm] * 2 + [vmem] * 2,
        out_specs=[hbm] * 2,
        scratch_shapes=[pltpu.VMEM((4,) + left_c.shape[1:], F32),
                        pltpu.SemaphoreType.DMA((4,)), pltpu.SemaphoreType.DMA((4,))],
        compiler_params=pltpu.CompilerParams(vmem_limit_bytes=8 * MIB),
        name="join_corners",
    )(left_c, right_c, from_left, from_right)


def simple(kernel, shape, name, limit, vectors):
    vmem = pl.BlockSpec(memory_space=pltpu.VMEM)
    return pl.pallas_call(
        kernel,
        out_shape=jax.ShapeDtypeStruct(shape, F32),
        in_specs=[vmem] * len(vectors),
        out_specs=vmem,
        compiler_params=pltpu.CompilerParams(vmem_limit_bytes=limit * MIB),
        name=name,
    )(*vectors)


def local(object_field, probe, intensity, pool_rows, pool_cols, batch, live):
    side = probe.shape[1]
    nrows, ncols = object_field.shape[1:]
    dims = (side, nrows, ncols)
    slots = batch.shape[1]
    t = side // LANES
    total = (ncols + side) // LANES
    probe_rate = 0.125 / math.sqrt(LIVE * lax.axis_size("tile") * lax.axis_size("row"))
    forward, backward = tables(side)
    forward, backward = jnp.asarray(forward), jnp.asarray(backward)
    current = probe.reshape(2, side, t, LANES).transpose(0, 2, 1, 3)

    first, rest = lax.optimization_barrier((object_field[:, :side, :side], object_field))
    below_a = passed_along(first, "row", -1)
    beside = passed_along(rest[:, :, :side], "tile", -1)
    below_b = passed_along(rest[:, :side, side:], "row", -1)
    corner = passed_along(below_a, "tile", -1)

    edge = jnp.stack([
        (lax.axis_index("row") == lax.axis_size("row") - 1).astype(jnp.int32),
        (lax.axis_index("tile") == lax.axis_size("tile") - 1).astype(jnp.int32)])
    scalars = (batch, live, pool_rows, pool_cols)
    devices = lax.axis_size("tile") * lax.axis_size("row")
    big = (2, total, nrows + side, LANES)
    corners = (2, 2, t, side, LANES)
    strip = (2, ncols // LANES - t, side, LANES)
    side_b = (2, t, nrows - side, LANES)
    part, gprobe, right_c, left_c, right_b, left_b, down_b, up_b = call(
        functools.partial(first_kernel, dims), dims, slots, scalars, (forward, backward, current),
        (intensity, object_field), (below_a, below_b, beside, corner),
        [big, current.shape, corners, corners, side_b, side_b, strip, strip], [],
        28, "first_iteration")

    from_left_c = passed_along(right_c, "tile", 1)
    from_right_c = passed_along(left_c, "tile", -1)
    from_up_b = passed_along(down_b, "row", 1)
    from_down_b = passed_along(up_b, "row", -1)
    mine = swap(gprobe.reshape(devices, -1, LANES))
    mine, from_left_c, from_right_c = lax.optimization_barrier((mine, from_left_c, from_right_c))
    down_c, up_c = join(left_c, right_c, from_left_c, from_right_c)
    from_up_c = passed_along(down_c, "row", 1)
    from_down_c = passed_along(up_c, "row", -1)
    mine, from_up_b, from_down_b, _ = lax.optimization_barrier(
        (mine, from_up_b, from_down_b, down_c))
    given, right_b, left_b = lax.optimization_barrier((add_up(mine), right_b, left_b))
    from_left_b = passed_along(right_b, "tile", 1)
    from_right_b = passed_along(left_b, "tile", -1)
    sum_one = swap(given).reshape(current.shape)

    own, gprobe, right_c, right_ab, down_a, down_b = call(
        functools.partial(second_kernel, dims, probe_rate), dims, slots, scalars + (edge,),
        (forward, backward, current, sum_one), (intensity, part),
        (from_left_c, from_right_c, from_up_c, from_down_c,
         from_left_b, from_right_b, from_up_b, from_down_b),
        [(2, ncols // LANES, nrows, LANES), current.shape, (2, t, side, LANES),
         (2, t, nrows, LANES), (2, t, side, LANES), strip],
        [current.shape], 28, "second_iteration")

    from_left_c = passed_along(right_c, "tile", 1)
    above_b = passed_along(down_b, "row", 1)
    mine = swap(gprobe.reshape(devices, -1, LANES))
    down_a = down_a + from_left_c
    above_a = passed_along(down_a, "row", 1)
    mine, above_b, _ = lax.optimization_barrier((mine, above_b, down_a))
    given, right_ab = lax.optimization_barrier((add_up(mine), right_ab))
    left_ab = passed_along(right_ab, "tile", 1)
    sum_two = swap(given).reshape(current.shape)
    object_out = simple(functools.partial(object_kernel, dims), object_field.shape, "last_object",
                        16, (own, left_ab, above_a, above_b))
    sum_two, _ = lax.optimization_barrier((sum_two, object_out))
    probe_out = simple(functools.partial(probe_kernel, probe_rate), probe.shape, "last_probe",
                       8, (current, sum_one, sum_two))
    return (object_out, probe_out)


def solution(mesh):
    placed = (
        P(None, "row", "tile"),
        P(),
        P(("tile", "row"), None, None),
        P(("tile", "row")),
        P(("tile", "row")),
        P(None, ("tile", "row")),
        P(None, ("tile", "row")),
    )
    return jax.shard_map(
        local, mesh=mesh, in_specs=placed, out_specs=(P(None, "row", "tile"), P()), check_vma=False
    )
```

```python
import functools
import math

import jax
import jax.numpy as jnp
import numpy as np
from jax import lax
from jax.experimental import pallas as pl
from jax.experimental.pallas import tpu as pltpu
from jax.sharding import PartitionSpec as P

LIVE = 6
LANES = 128
MIB = 1024 * 1024
F32 = jnp.float32
BF16 = jnp.bfloat16


def passed_along(value, axis, steps):
    count = lax.axis_size(axis)
    first, last = (max(0, -steps), min(count, count - steps))
    return lax.ppermute(value, axis, [(source, source + steps) for source in range(first, last)])


def tables(length):
    counter = np.arange(length, dtype=np.int32)
    product = counter[:, None] * counter[None, :] % length
    angle = product.astype(np.float32) * np.float32(2.0 * math.pi / length)
    factor = np.float32(1.0 / math.sqrt(length))
    cosine = (np.cos(angle) * factor).astype(BF16)
    sine = (np.sin(angle) * factor).astype(BF16)
    forward = np.block([[cosine, sine], [-sine, cosine]])
    backward = np.block([[cosine, -sine], [sine, cosine]])
    return forward, backward


def mul(left, right):
    return jnp.dot(left, right, preferred_element_type=F32)


def start_slots(step, batch, intensity, measured, sems):
    copies = []
    for s in range(batch.shape[1]):
        copies.append(
            pltpu.make_async_copy(intensity.at[batch[step, s]], measured.at[s], sems.at[s]))
    for copy in copies:
        copy.start()
    return copies


def clear(grad, gprobe, waves, patches):
    grad[...] = jnp.zeros_like(grad)
    gprobe[...] = jnp.zeros_like(gprobe)
    waves[1][...] = jnp.zeros_like(waves[1])
    patches[1][...] = jnp.zeros_like(patches[1])


def slot_loop(step, side, batch, live, rows, cols, mats, probe, ext, grad, gprobe,
              measured, exits, waves, patches):
    forward, backward = mats.at[0], mats.at[1]
    lane = lax.broadcasted_iota(jnp.int32, (side, LANES), 1)
    halves = side // LANES
    count = live[step, 0]

    def corner_of(s):
        stored = batch[step, s]
        col = cols[stored]
        return rows[stored], col // LANES, col % LANES

    def window(part, tile, row, shift):
        turn = (LANES - shift) & (LANES - 1)
        turned = [
            pltpu.roll(ext[part, tile + j, pl.ds(row, side), :], turn, 1) for j in range(halves + 1)
        ]
        keep = lane < LANES - shift
        return [jnp.where(keep, turned[j], turned[j + 1]) for j in range(halves)]

    def place(part, tile, row, shift, values):
        turned = [pltpu.roll(v, shift, 1) for v in values]
        keep = lane >= shift
        zero = jnp.zeros((side, LANES), F32)
        for j in range(halves + 1):
            here = turned[j] if j < halves else zero
            prior = turned[j - 1] if j else zero
            at = (part, tile + j, pl.ds(row, side), slice(None))
            grad[at] = grad[at] + jnp.where(keep, here, prior)

    def first_half(s, buffer, alive):
        row, tile, shift = corner_of(s)
        exit_in, wave, patch = exits[buffer], waves[buffer], patches[buffer]
        patch_r = window(0, tile, row, shift)
        patch_i = window(1, tile, row, shift)
        for j in range(halves):
            p_r, p_i = probe[0, j], probe[1, j]
            at = slice(j * LANES, (j + 1) * LANES)
            patch[0, j] = patch_r[j]
            patch[1, j] = patch_i[j]
            exit_in[0:side, at] = (p_r * patch_r[j] - p_i * patch_i[j]).astype(BF16)
            exit_in[side:, at] = (p_r * patch_i[j] + p_i * patch_r[j]).astype(BF16)
        half = mul(forward[...], exit_in[...]).astype(BF16)
        far = mul(jnp.concatenate([half[:side], half[side:]], axis=1), backward[...])
        far_r, far_i = far[:, :side], far[:, side:]
        excess = far_r * far_r + far_i * far_i - measured[s].astype(F32)
        if alive is not None:
            excess = excess * alive
        wave[0:side, :] = (excess * far_r).astype(BF16)
        wave[side:, :] = (excess * far_i).astype(BF16)

    def second_half(s, buffer):
        row, tile, shift = corner_of(s)
        wave, patch = waves[buffer], patches[buffer]
        mid = mul(backward[...], wave[...]).astype(BF16)
        back = mul(jnp.concatenate([mid[:side], mid[side:]], axis=1), forward[...])
        object_r, object_i = [], []
        for j in range(halves):
            p_r, p_i = probe[0, j], probe[1, j]
            o_r, o_i = patch[0, j], patch[1, j]
            b_r = back[:, j * LANES:(j + 1) * LANES]
            b_i = back[:, side + j * LANES:side + (j + 1) * LANES]
            object_r.append(p_r * b_r + p_i * b_i)
            object_i.append(p_r * b_i - p_i * b_r)
            gprobe[0, j] += o_r * b_r + o_i * b_i
            gprobe[1, j] += o_r * b_i - o_i * b_r
        place(0, tile, row, shift, object_r)
        place(1, tile, row, shift, object_i)

    def two_slots(k, carry):
        even = 2 * k
        odd = jnp.minimum(even + 1, batch.shape[1] - 1)
        alive = jnp.where(even + 1 < count, 1.0, 0.0).astype(F32)
        second_half(jnp.maximum(even - 1, 0), 1)
        first_half(even, 0, None)
        second_half(even, 0)
        first_half(odd, 1, alive)
        return carry

    pairs = (count + 1) // 2
    lax.fori_loop(0, pairs, two_slots, 0)
    second_half(jnp.minimum(2 * pairs - 1, batch.shape[1] - 1), 1)


def tiled_copies(field, part_rows, part_cols, ext, row0, col0):
    pairs = []
    for part in range(2):
        for j in range(part_cols // LANES):
            pairs.append((
                field.at[part, :, pl.ds(j * LANES, LANES)],
                ext.at[part, col0 // LANES + j, pl.ds(row0, part_rows), :],
            ))
    return pairs


def run_copies(pairs, sems, base=0):
    copies = [pltpu.make_async_copy(src, dst, sems.at[base + i]) for i, (src, dst) in enumerate(pairs)]
    for copy in copies:
        copy.start()
    return copies


def update_out(ext, grad, target, sems, base):
    parts, tiles, rows = target.shape[:3]
    copies = []
    for part in range(parts):
        for j in range(tiles):
            ext[part, j, 0:rows, :] -= 0.25 * grad[part, j, 0:rows, :]
            copies += run_copies([(ext.at[part, j, pl.ds(0, rows), :], target.at[part, j])],
                                 sems, base + len(copies))
    return copies


def first_kernel(dims, batch, live, rows, cols, probe, intensity, tables_in,
                 field, below_a, below_b, beside, corner,
                 part_out, gprobe_out, right_c, left_c, right_b, left_b, down_b, up_b,
                 ext, grad, mats, measured, exit_0, exit_1, wave_0, wave_1, patch_0, patch_1,
                 gprobe, sems, moves):
    side, nrows, ncols = dims
    pairs = tiled_copies(field, nrows, ncols, ext, 0, 0)
    pairs += tiled_copies(below_a, side, side, ext, nrows, 0)
    pairs += tiled_copies(below_b, side, ncols - side, ext, nrows, side)
    pairs += tiled_copies(beside, nrows, side, ext, 0, ncols)
    pairs += tiled_copies(corner, side, side, ext, nrows, ncols)
    copies = run_copies(pairs + [(tables_in, mats)], moves)
    copies += start_slots(0, batch, intensity, measured, sems)
    waves, patches = (wave_0, wave_1), (patch_0, patch_1)
    clear(grad, gprobe, waves, patches)
    for copy in copies:
        copy.wait()
    slot_loop(0, side, batch, live, rows, cols, mats, probe, ext, grad, gprobe,
              measured, (exit_0, exit_1), waves, patches)
    t = side // LANES
    last = ncols // LANES
    a_rows, c_rows = pl.ds(0, side), pl.ds(nrows, side)
    b_rows = pl.ds(side, nrows - side)
    left, mid, right = pl.ds(0, t), pl.ds(t, last - t), pl.ds(last, t)
    pairs = [
        (gprobe, gprobe_out),
        (grad.at[:, right, a_rows, :], right_c.at[0]),
        (grad.at[:, right, c_rows, :], right_c.at[1]),
        (grad.at[:, left, a_rows, :], left_c.at[0]),
        (grad.at[:, left, c_rows, :], left_c.at[1]),
        (grad.at[:, right, b_rows, :], right_b),
        (grad.at[:, left, b_rows, :], left_b),
        (grad.at[:, mid, c_rows, :], down_b),
        (grad.at[:, mid, a_rows, :], up_b),
    ]
    copies = run_copies(pairs, moves)
    copies += update_out(ext, grad, part_out, moves, len(pairs))
    for copy in copies:
        copy.wait()


def share_kernel(received, given):
    summed = received[0]
    for i in range(1, received.shape[0]):
        summed = summed + received[i]
    for i in range(received.shape[0]):
        given[i] = summed


def second_kernel(dims, rate, batch, live, rows, cols, edge, probe, summed,
                  intensity, tables_in, part_in, from_left_c, from_right_c, from_up_c, from_down_c,
                  from_left, from_right, from_up, from_down,
                  own_out, gprobe_out, right_c, right_ab, down_a, down_b,
                  ext, grad, mats, measured, exit_0, exit_1, wave_0, wave_1, patch_0, patch_1,
                  gprobe, now, sems, moves):
    side, nrows, ncols = dims
    t = side // LANES
    last = ncols // LANES
    copies = run_copies([(part_in, ext), (tables_in, mats)], moves)
    copies += start_slots(1, batch, intensity, measured, sems)
    waves, patches = (wave_0, wave_1), (patch_0, patch_1)
    clear(grad, gprobe, waves, patches)
    now[...] = probe[...] - rate * summed[...]
    for copy in copies:
        copy.wait()
    a_rows, c_rows = slice(0, side), slice(nrows, nrows + side)
    b_rows = slice(side, nrows)
    left, mid, right = slice(0, t), slice(t, last), slice(last, last + t)
    for rows_of, corner, strip, k in ((a_rows, from_up_c, from_up, 0),
                                      (c_rows, from_down_c, from_down, 1)):
        ext[:, left, rows_of, :] -= 0.25 * (corner[0] + from_left_c[k])
        ext[:, mid, rows_of, :] -= 0.25 * strip[...]
        ext[:, right, rows_of, :] -= 0.25 * (corner[1] + from_right_c[k])
    ext[:, left, b_rows, :] -= 0.25 * from_left[...]
    ext[:, right, b_rows, :] -= 0.25 * from_right[...]

    @pl.when(edge[0] == 1)
    def _():
        ext[:, :, c_rows, :] = jnp.zeros((2, last + t, side, LANES), F32)

    @pl.when(edge[1] == 1)
    def _():
        ext[:, right, :, :] = jnp.zeros((2, t, nrows + side, LANES), F32)

    slot_loop(1, side, batch, live, rows, cols, mats, now, ext, grad, gprobe,
              measured, (exit_0, exit_1), waves, patches)
    c_rows, own_rows = pl.ds(nrows, side), pl.ds(0, nrows)
    right = pl.ds(last, t)
    pairs = [
        (gprobe, gprobe_out),
        (grad.at[:, right, c_rows, :], right_c),
        (grad.at[:, pl.ds(t, last - t), c_rows, :], down_b),
        (grad.at[:, pl.ds(0, t), c_rows, :], down_a),
        (grad.at[:, right, own_rows, :], right_ab),
    ]
    copies = run_copies(pairs, moves)
    copies += update_out(ext, grad, own_out, moves, len(pairs))
    for copy in copies:
        copy.wait()


def object_kernel(dims, own, left_ab, above_a, above_b, object_out):
    side, nrows, ncols = dims
    t = side // LANES
    for part in range(2):
        for j in range(ncols // LANES):
            lanes = slice(j * LANES, (j + 1) * LANES)
            if j < t:
                top = own[part, j, 0:side, :] - 0.25 * (
                    left_ab[part, j, 0:side, :] + above_a[part, j])
                low = own[part, j, side:, :] - 0.25 * left_ab[part, j, side:, :]
            else:
                top = own[part, j, 0:side, :] - 0.25 * above_b[part, j - t]
                low = own[part, j, side:, :]
            object_out[part, 0:side, lanes] = top
            object_out[part, side:, lanes] = low


def probe_kernel(rate, probe, sum_one, sum_two, probe_out):
    for part in range(2):
        for j in range(probe.shape[1]):
            probe_out[part, :, j * LANES:(j + 1) * LANES] = (
                probe[part, j] - rate * (sum_one[part, j] + sum_two[part, j]))


def call(kernel, dims, slots, scalars, vectors, plain, received, outs, extra, limit,
         name):
    side, nrows, ncols = dims
    big = (2, (ncols + side) // LANES, nrows + side, LANES)
    smem = pl.BlockSpec(memory_space=pltpu.SMEM)
    vmem = pl.BlockSpec(memory_space=pltpu.VMEM)
    hbm = pl.BlockSpec(memory_space=pltpu.HBM)
    return pl.pallas_call(
        kernel,
        out_shape=[jax.ShapeDtypeStruct(shape, F32) for shape in outs],
        in_specs=([smem] * len(scalars) + [vmem] * len(vectors) + [hbm] * len(plain)
                  + [vmem] * len(received)),
        out_specs=[hbm] * len(outs),
        scratch_shapes=[
            pltpu.VMEM(big, F32),
            pltpu.VMEM(big, F32),
            pltpu.VMEM((2, 2 * side, 2 * side), BF16),
            pltpu.VMEM((slots, side, side), BF16),
        ] + [pltpu.VMEM((2 * side, side), BF16)] * 4
        + [pltpu.VMEM((2, side // LANES, side, LANES), F32)] * 3
        + [pltpu.VMEM(shape, F32) for shape in extra] + [
            pltpu.SemaphoreType.DMA((slots,)),
            pltpu.SemaphoreType.DMA((48,)),
        ],
        compiler_params=pltpu.CompilerParams(vmem_limit_bytes=limit * MIB),
        name=name,
    )(*scalars, *vectors, *plain, *received)


def swap(shares):
    return lax.all_to_all(shares, ("tile", "row"), 0, 0, tiled=True)


def add_up(mine):
    return pl.pallas_call(
        share_kernel, out_shape=jax.ShapeDtypeStruct(mine.shape, F32), name="sum_shares",
    )(mine)


def simple(kernel, shape, name, limit, vectors):
    vmem = pl.BlockSpec(memory_space=pltpu.VMEM)
    return pl.pallas_call(
        kernel,
        out_shape=jax.ShapeDtypeStruct(shape, F32),
        in_specs=[vmem] * len(vectors),
        out_specs=vmem,
        compiler_params=pltpu.CompilerParams(vmem_limit_bytes=limit * MIB),
        name=name,
    )(*vectors)


def local(object_field, probe, intensity, pool_rows, pool_cols, batch, live):
    side = probe.shape[1]
    nrows, ncols = object_field.shape[1:]
    dims = (side, nrows, ncols)
    slots = batch.shape[1]
    t = side // LANES
    total = (ncols + side) // LANES
    probe_rate = 0.125 / math.sqrt(LIVE * lax.axis_size("tile") * lax.axis_size("row"))
    both = jnp.asarray(np.stack(tables(side)))
    current = probe.reshape(2, side, t, LANES).transpose(0, 2, 1, 3)

    first, rest = lax.optimization_barrier((object_field[:, :side, :side], object_field))
    below_a = passed_along(first, "row", -1)
    beside = passed_along(rest[:, :, :side], "tile", -1)
    below_b = passed_along(rest[:, :side, side:], "row", -1)
    corner = passed_along(below_a, "tile", -1)

    edge = jnp.stack([
        (lax.axis_index("row") == lax.axis_size("row") - 1).astype(jnp.int32),
        (lax.axis_index("tile") == lax.axis_size("tile") - 1).astype(jnp.int32)])
    scalars = (batch, live, pool_rows, pool_cols)
    devices = lax.axis_size("tile") * lax.axis_size("row")
    big = (2, total, nrows + side, LANES)
    corners = (2, 2, t, side, LANES)
    strip = (2, ncols // LANES - t, side, LANES)
    side_b = (2, t, nrows - side, LANES)
    part, gprobe, right_c, left_c, right_b, left_b, down_b, up_b = call(
        functools.partial(first_kernel, dims), dims, slots, scalars, (current,),
        (intensity, both, object_field), (below_a, below_b, beside, corner),
        [big, current.shape, corners, corners, side_b, side_b, strip, strip], [],
        52, "first_iteration")

    from_left_c = passed_along(right_c, "tile", 1)
    from_right_c = passed_along(left_c, "tile", -1)
    from_up_b = passed_along(down_b, "row", 1)
    from_down_b = passed_along(up_b, "row", -1)
    mine = swap(gprobe.reshape(devices, -1, LANES))
    mine, from_left_c, from_right_c = lax.optimization_barrier((mine, from_left_c, from_right_c))
    down_c = jnp.stack([left_c[1] + from_left_c[1], right_c[1] + from_right_c[1]])
    up_c = jnp.stack([left_c[0] + from_left_c[0], right_c[0] + from_right_c[0]])
    from_up_c = passed_along(down_c, "row", 1)
    from_down_c = passed_along(up_c, "row", -1)
    mine, from_up_b, from_down_b, _, _ = lax.optimization_barrier(
        (mine, from_up_b, from_down_b, down_c, up_c))
    given, right_b, left_b = lax.optimization_barrier((add_up(mine), right_b, left_b))
    from_left_b = passed_along(right_b, "tile", 1)
    from_right_b = passed_along(left_b, "tile", -1)
    sum_one = swap(given).reshape(current.shape)

    own, gprobe, right_c, right_ab, down_a, down_b = call(
        functools.partial(second_kernel, dims, probe_rate), dims, slots, scalars + (edge,),
        (current, sum_one), (intensity, both, part),
        (from_left_c, from_right_c, from_up_c, from_down_c,
         from_left_b, from_right_b, from_up_b, from_down_b),
        [(2, ncols // LANES, nrows, LANES), current.shape, (2, t, side, LANES),
         (2, t, nrows, LANES), (2, t, side, LANES), strip],
        [current.shape], 49, "second_iteration")

    from_left_c = passed_along(right_c, "tile", 1)
    above_b = passed_along(down_b, "row", 1)
    mine = swap(gprobe.reshape(devices, -1, LANES))
    down_a = down_a + from_left_c
    above_a = passed_along(down_a, "row", 1)
    mine, above_b, _ = lax.optimization_barrier((mine, above_b, down_a))
    given, right_ab = lax.optimization_barrier((add_up(mine), right_ab))
    left_ab = passed_along(right_ab, "tile", 1)
    sum_two = swap(given).reshape(current.shape)
    object_out = simple(functools.partial(object_kernel, dims), object_field.shape, "last_object",
                        16, (own, left_ab, above_a, above_b))
    sum_two, _ = lax.optimization_barrier((sum_two, object_out))
    probe_out = simple(functools.partial(probe_kernel, probe_rate), probe.shape, "last_probe",
                       8, (current, sum_one, sum_two))
    return (object_out, probe_out)


def solution(mesh):
    placed = (
        P(None, "row", "tile"),
        P(),
        P(("tile", "row"), None, None),
        P(("tile", "row")),
        P(("tile", "row")),
        P(None, ("tile", "row")),
        P(None, ("tile", "row")),
    )
    return jax.shard_map(
        local, mesh=mesh, in_specs=placed, out_specs=(P(None, "row", "tile"), P()), check_vma=False
    )
```

```python
import functools
import math

import jax
import jax.numpy as jnp
import numpy as np
from jax import lax
from jax.experimental import pallas as pl
from jax.experimental.pallas import tpu as pltpu
from jax.sharding import PartitionSpec as P

LIVE = 6
LANES = 128
MIB = 1024 * 1024
F32 = jnp.float32
BF16 = jnp.bfloat16


def passed_along(value, axis, steps):
    count = lax.axis_size(axis)
    first, last = (max(0, -steps), min(count, count - steps))
    return lax.ppermute(value, axis, [(source, source + steps) for source in range(first, last)])


def tables(length):
    counter = np.arange(length, dtype=np.int32)
    product = counter[:, None] * counter[None, :] % length
    angle = product.astype(np.float32) * np.float32(2.0 * math.pi / length)
    factor = np.float32(1.0 / math.sqrt(length))
    cosine = (np.cos(angle) * factor).astype(BF16)
    sine = (np.sin(angle) * factor).astype(BF16)
    forward = np.block([[cosine, sine], [-sine, cosine]])
    backward = np.block([[cosine, -sine], [sine, cosine]])
    return forward, backward


def mul(left, right):
    return jnp.dot(left, right, preferred_element_type=F32)


def start_slots(step, batch, intensity, measured, sems):
    copies = []
    for s in range(batch.shape[1]):
        copies.append(
            pltpu.make_async_copy(intensity.at[batch[step, s]], measured.at[s], sems.at[s]))
    for copy in copies:
        copy.start()
    return copies


def clear(grad, gprobe, waves, patches):
    grad[...] = jnp.zeros_like(grad)
    gprobe[...] = jnp.zeros_like(gprobe)
    waves[1][...] = jnp.zeros_like(waves[1])
    patches[1][...] = jnp.zeros_like(patches[1])


def slot_loop(step, side, batch, live, rows, cols, mats, probe, ext, grad, gprobe,
              measured, exits, waves, patches, apart):
    forward, backward = mats.at[0], mats.at[1]
    lane = lax.broadcasted_iota(jnp.int32, (side, LANES), 1)
    halves = side // LANES
    count = live[step, 0]

    def corner_of(s):
        stored = batch[step, s]
        col = cols[stored]
        return rows[stored], col // LANES, col % LANES

    def window(part, tile, row, shift):
        turn = (LANES - shift) & (LANES - 1)
        turned = [
            pltpu.roll(ext[part, tile + j, pl.ds(row, side), :], turn, 1) for j in range(halves + 1)
        ]
        keep = lane < LANES - shift
        return [jnp.where(keep, turned[j], turned[j + 1]) for j in range(halves)]

    def place(part, tile, row, shift, values):
        turned = [pltpu.roll(v, shift, 1) for v in values]
        keep = lane >= shift
        zero = jnp.zeros((side, LANES), F32)
        for j in range(halves + 1):
            here = turned[j] if j < halves else zero
            prior = turned[j - 1] if j else zero
            at = (part, tile + j, pl.ds(row, side), slice(None))
            grad[at] = grad[at] + jnp.where(keep, here, prior)

    def first_half(s, buffer, alive):
        row, tile, shift = corner_of(s)
        exit_in, wave, patch = exits[buffer], waves[buffer], patches[buffer]
        patch_r = window(0, tile, row, shift)
        patch_i = window(1, tile, row, shift)
        for j in range(halves):
            p_r, p_i = probe[0, j], probe[1, j]
            at = slice(j * LANES, (j + 1) * LANES)
            patch[0, j] = patch_r[j]
            patch[1, j] = patch_i[j]
            exit_in[0:side, at] = (p_r * patch_r[j] - p_i * patch_i[j]).astype(BF16)
            exit_in[side:, at] = (p_r * patch_i[j] + p_i * patch_r[j]).astype(BF16)
        half = mul(forward[...], exit_in[...]).astype(BF16)
        far = mul(jnp.concatenate([half[:side], half[side:]], axis=1), backward[...])
        far_r, far_i = far[:, :side], far[:, side:]
        excess = far_r * far_r + far_i * far_i - measured[s].astype(F32)
        if alive is not None:
            excess = excess * alive
        wave[0:side, :] = (excess * far_r).astype(BF16)
        wave[side:, :] = (excess * far_i).astype(BF16)

    def second_half(s, buffer):
        row, tile, shift = corner_of(s)
        wave, patch = waves[buffer], patches[buffer]
        mid = mul(backward[...], wave[...]).astype(BF16)
        back = mul(jnp.concatenate([mid[:side], mid[side:]], axis=1), forward[...])
        object_r, object_i = [], []
        for j in range(halves):
            p_r, p_i = probe[0, j], probe[1, j]
            o_r, o_i = patch[0, j], patch[1, j]
            b_r = back[:, j * LANES:(j + 1) * LANES]
            b_i = back[:, side + j * LANES:side + (j + 1) * LANES]
            object_r.append(p_r * b_r + p_i * b_i)
            object_i.append(p_r * b_i - p_i * b_r)
            gprobe[0, j] += o_r * b_r + o_i * b_i
            gprobe[1, j] += o_r * b_i - o_i * b_r
        place(0, tile, row, shift, object_r)
        place(1, tile, row, shift, object_i)

    def two_slots(k, carry):
        even = 2 * k
        odd = jnp.minimum(even + 1, batch.shape[1] - 1)
        alive = jnp.where(even + 1 < count, 1.0, 0.0).astype(F32)
        second_half(jnp.maximum(even - 1, 0), 1)
        first_half(even, 0, None)
        second_half(even, 0)
        first_half(odd, 1, alive)
        return carry

    def two_steps(k, carry):
        even = 2 * k
        odd = even + 1
        second_half(jnp.maximum(even - 1, 0), 1)
        first_half(even, 0, None)

        @pl.when(odd < count)
        def _():
            second_half(even, 0)
            first_half(odd, 1, None)

        @pl.when(odd == count)
        def _():
            second_half(even, 0)

        return carry

    pairs = (count + 1) // 2
    if apart:
        lax.fori_loop(0, pairs, two_steps, 0)

        @pl.when(count % 2 == 0)
        def _():
            second_half(count - 1, 1)
    else:
        lax.fori_loop(0, pairs, two_slots, 0)
        second_half(jnp.minimum(2 * pairs - 1, batch.shape[1] - 1), 1)


def tiled_copies(field, part_rows, part_cols, ext, row0, col0):
    pairs = []
    for part in range(2):
        for j in range(part_cols // LANES):
            pairs.append((
                field.at[part, :, pl.ds(j * LANES, LANES)],
                ext.at[part, col0 // LANES + j, pl.ds(row0, part_rows), :],
            ))
    return pairs


def run_copies(pairs, sems, base=0):
    copies = [pltpu.make_async_copy(src, dst, sems.at[base + i]) for i, (src, dst) in enumerate(pairs)]
    for copy in copies:
        copy.start()
    return copies


def update_out(ext, grad, target, sems, base):
    parts, tiles, rows = target.shape[:3]
    copies = []
    for part in range(parts):
        for j in range(tiles):
            ext[part, j, 0:rows, :] -= 0.25 * grad[part, j, 0:rows, :]
            copies += run_copies([(ext.at[part, j, pl.ds(0, rows), :], target.at[part, j])],
                                 sems, base + len(copies))
    return copies


def first_kernel(dims, batch, live, rows, cols, probe, intensity, tables_in,
                 field, below_a, below_b, beside, corner,
                 part_out, gprobe_out, right_c, left_c, right_b, left_b, down_b, up_b,
                 ext, grad, mats, measured, exit_0, exit_1, wave_0, wave_1, patch_0, patch_1,
                 gprobe, sems, moves):
    side, nrows, ncols = dims
    pairs = tiled_copies(field, nrows, ncols, ext, 0, 0)
    pairs += tiled_copies(below_a, side, side, ext, nrows, 0)
    pairs += tiled_copies(below_b, side, ncols - side, ext, nrows, side)
    pairs += tiled_copies(beside, nrows, side, ext, 0, ncols)
    pairs += tiled_copies(corner, side, side, ext, nrows, ncols)
    copies = run_copies(pairs + [(tables_in, mats)], moves)
    copies += start_slots(0, batch, intensity, measured, sems)
    waves, patches = (wave_0, wave_1), (patch_0, patch_1)
    clear(grad, gprobe, waves, patches)
    for copy in copies:
        copy.wait()
    slot_loop(0, side, batch, live, rows, cols, mats, probe, ext, grad, gprobe,
              measured, (exit_0, exit_1), waves, patches, False)
    t = side // LANES
    last = ncols // LANES
    a_rows, c_rows = pl.ds(0, side), pl.ds(nrows, side)
    b_rows = pl.ds(side, nrows - side)
    left, mid, right = pl.ds(0, t), pl.ds(t, last - t), pl.ds(last, t)
    pairs = [
        (gprobe, gprobe_out),
        (grad.at[:, right, a_rows, :], right_c.at[0]),
        (grad.at[:, right, c_rows, :], right_c.at[1]),
        (grad.at[:, left, a_rows, :], left_c.at[0]),
        (grad.at[:, left, c_rows, :], left_c.at[1]),
        (grad.at[:, right, b_rows, :], right_b),
        (grad.at[:, left, b_rows, :], left_b),
        (grad.at[:, mid, c_rows, :], down_b),
        (grad.at[:, mid, a_rows, :], up_b),
    ]
    copies = run_copies(pairs, moves)
    copies += update_out(ext, grad, part_out, moves, len(pairs))
    for copy in copies:
        copy.wait()


def share_kernel(received, given):
    summed = received[0]
    for i in range(1, received.shape[0]):
        summed = summed + received[i]
    for i in range(received.shape[0]):
        given[i] = summed


def second_kernel(dims, rate, batch, live, rows, cols, edge, probe, summed,
                  intensity, tables_in, part_in, from_left_c, from_right_c, from_up_c, from_down_c,
                  from_left, from_right, from_up, from_down,
                  own_out, gprobe_out, right_c, right_ab, down_a, down_b,
                  ext, grad, mats, measured, exit_0, exit_1, wave_0, wave_1, patch_0, patch_1,
                  gprobe, now, sems, moves):
    side, nrows, ncols = dims
    t = side // LANES
    last = ncols // LANES
    copies = run_copies([(part_in, ext), (tables_in, mats)], moves)
    copies += start_slots(1, batch, intensity, measured, sems)
    waves, patches = (wave_0, wave_1), (patch_0, patch_1)
    clear(grad, gprobe, waves, patches)
    now[...] = probe[...] - rate * summed[...]
    for copy in copies:
        copy.wait()
    a_rows, c_rows = slice(0, side), slice(nrows, nrows + side)
    b_rows = slice(side, nrows)
    left, mid, right = slice(0, t), slice(t, last), slice(last, last + t)
    for rows_of, corner, strip, k in ((a_rows, from_up_c, from_up, 0),
                                      (c_rows, from_down_c, from_down, 1)):
        ext[:, left, rows_of, :] -= 0.25 * (corner[0] + from_left_c[k])
        ext[:, mid, rows_of, :] -= 0.25 * strip[...]
        ext[:, right, rows_of, :] -= 0.25 * (corner[1] + from_right_c[k])
    ext[:, left, b_rows, :] -= 0.25 * from_left[...]
    ext[:, right, b_rows, :] -= 0.25 * from_right[...]

    @pl.when(edge[0] == 1)
    def _():
        ext[:, :, c_rows, :] = jnp.zeros((2, last + t, side, LANES), F32)

    @pl.when(edge[1] == 1)
    def _():
        ext[:, right, :, :] = jnp.zeros((2, t, nrows + side, LANES), F32)

    slot_loop(1, side, batch, live, rows, cols, mats, now, ext, grad, gprobe,
              measured, (exit_0, exit_1), waves, patches, True)
    c_rows, own_rows = pl.ds(nrows, side), pl.ds(0, nrows)
    right = pl.ds(last, t)
    pairs = [
        (gprobe, gprobe_out),
        (grad.at[:, right, c_rows, :], right_c),
        (grad.at[:, pl.ds(t, last - t), c_rows, :], down_b),
        (grad.at[:, pl.ds(0, t), c_rows, :], down_a),
        (grad.at[:, right, own_rows, :], right_ab),
    ]
    copies = run_copies(pairs, moves)
    copies += update_out(ext, grad, own_out, moves, len(pairs))
    for copy in copies:
        copy.wait()


def object_kernel(dims, own, left_ab, above_a, above_b, object_out):
    side, nrows, ncols = dims
    t = side // LANES
    for part in range(2):
        for j in range(ncols // LANES):
            lanes = slice(j * LANES, (j + 1) * LANES)
            if j < t:
                top = own[part, j, 0:side, :] - 0.25 * (
                    left_ab[part, j, 0:side, :] + above_a[part, j])
                low = own[part, j, side:, :] - 0.25 * left_ab[part, j, side:, :]
            else:
                top = own[part, j, 0:side, :] - 0.25 * above_b[part, j - t]
                low = own[part, j, side:, :]
            object_out[part, 0:side, lanes] = top
            object_out[part, side:, lanes] = low


def probe_kernel(rate, probe, sum_one, sum_two, probe_out):
    for part in range(2):
        for j in range(probe.shape[1]):
            probe_out[part, :, j * LANES:(j + 1) * LANES] = (
                probe[part, j] - rate * (sum_one[part, j] + sum_two[part, j]))


def call(kernel, dims, slots, scalars, vectors, plain, received, outs, extra, limit,
         name):
    side, nrows, ncols = dims
    big = (2, (ncols + side) // LANES, nrows + side, LANES)
    smem = pl.BlockSpec(memory_space=pltpu.SMEM)
    vmem = pl.BlockSpec(memory_space=pltpu.VMEM)
    hbm = pl.BlockSpec(memory_space=pltpu.HBM)
    return pl.pallas_call(
        kernel,
        out_shape=[jax.ShapeDtypeStruct(shape, F32) for shape in outs],
        in_specs=([smem] * len(scalars) + [vmem] * len(vectors) + [hbm] * len(plain)
                  + [vmem] * len(received)),
        out_specs=[hbm] * len(outs),
        scratch_shapes=[
            pltpu.VMEM(big, F32),
            pltpu.VMEM(big, F32),
            pltpu.VMEM((2, 2 * side, 2 * side), BF16),
            pltpu.VMEM((slots, side, side), BF16),
        ] + [pltpu.VMEM((2 * side, side), BF16)] * 4
        + [pltpu.VMEM((2, side // LANES, side, LANES), F32)] * 3
        + [pltpu.VMEM(shape, F32) for shape in extra] + [
            pltpu.SemaphoreType.DMA((slots,)),
            pltpu.SemaphoreType.DMA((48,)),
        ],
        compiler_params=pltpu.CompilerParams(vmem_limit_bytes=limit * MIB),
        name=name,
    )(*scalars, *vectors, *plain, *received)


def swap(shares):
    return lax.all_to_all(shares, ("tile", "row"), 0, 0, tiled=True)


def add_up(mine):
    return pl.pallas_call(
        share_kernel, out_shape=jax.ShapeDtypeStruct(mine.shape, F32), name="sum_shares",
    )(mine)


def simple(kernel, shape, name, limit, vectors):
    vmem = pl.BlockSpec(memory_space=pltpu.VMEM)
    return pl.pallas_call(
        kernel,
        out_shape=jax.ShapeDtypeStruct(shape, F32),
        in_specs=[vmem] * len(vectors),
        out_specs=vmem,
        compiler_params=pltpu.CompilerParams(vmem_limit_bytes=limit * MIB),
        name=name,
    )(*vectors)


def local(object_field, probe, intensity, pool_rows, pool_cols, batch, live):
    side = probe.shape[1]
    nrows, ncols = object_field.shape[1:]
    dims = (side, nrows, ncols)
    slots = batch.shape[1]
    t = side // LANES
    total = (ncols + side) // LANES
    probe_rate = 0.125 / math.sqrt(LIVE * lax.axis_size("tile") * lax.axis_size("row"))
    both = jnp.asarray(np.stack(tables(side)))
    current = probe.reshape(2, side, t, LANES).transpose(0, 2, 1, 3)

    first, rest = lax.optimization_barrier((object_field[:, :side, :side], object_field))
    below_a = passed_along(first, "row", -1)
    beside = passed_along(rest[:, :, :side], "tile", -1)
    below_b = passed_along(rest[:, :side, side:], "row", -1)
    corner = passed_along(below_a, "tile", -1)

    edge = jnp.stack([
        (lax.axis_index("row") == lax.axis_size("row") - 1).astype(jnp.int32),
        (lax.axis_index("tile") == lax.axis_size("tile") - 1).astype(jnp.int32)])
    scalars = (batch, live, pool_rows, pool_cols)
    devices = lax.axis_size("tile") * lax.axis_size("row")
    big = (2, total, nrows + side, LANES)
    corners = (2, 2, t, side, LANES)
    strip = (2, ncols // LANES - t, side, LANES)
    side_b = (2, t, nrows - side, LANES)
    part, gprobe, right_c, left_c, right_b, left_b, down_b, up_b = call(
        functools.partial(first_kernel, dims), dims, slots, scalars, (current,),
        (intensity, both, object_field, below_a, below_b, beside, corner), (),
        [big, current.shape, corners, corners, side_b, side_b, strip, strip], [],
        52, "first_iteration")

    from_left_c = passed_along(right_c, "tile", 1)
    from_right_c = passed_along(left_c, "tile", -1)
    from_up_b = passed_along(down_b, "row", 1)
    from_down_b = passed_along(up_b, "row", -1)
    mine = swap(gprobe.reshape(devices, -1, LANES))
    mine, from_left_c, from_right_c = lax.optimization_barrier((mine, from_left_c, from_right_c))
    down_c = jnp.stack([left_c[1] + from_left_c[1], right_c[1] + from_right_c[1]])
    up_c = jnp.stack([left_c[0] + from_left_c[0], right_c[0] + from_right_c[0]])
    from_up_c = passed_along(down_c, "row", 1)
    from_down_c = passed_along(up_c, "row", -1)
    mine, from_up_b, from_down_b, _, _ = lax.optimization_barrier(
        (mine, from_up_b, from_down_b, down_c, up_c))
    given, right_b, left_b = lax.optimization_barrier((add_up(mine), right_b, left_b))
    from_left_b = passed_along(right_b, "tile", 1)
    from_right_b = passed_along(left_b, "tile", -1)
    sum_one = swap(given).reshape(current.shape)

    own, gprobe, right_c, right_ab, down_a, down_b = call(
        functools.partial(second_kernel, dims, probe_rate), dims, slots, scalars + (edge,),
        (current, sum_one), (intensity, both, part),
        (from_left_c, from_right_c, from_up_c, from_down_c,
         from_left_b, from_right_b, from_up_b, from_down_b),
        [(2, ncols // LANES, nrows, LANES), current.shape, (2, t, side, LANES),
         (2, t, nrows, LANES), (2, t, side, LANES), strip],
        [current.shape], 49, "second_iteration")

    from_left_c = passed_along(right_c, "tile", 1)
    above_b = passed_along(down_b, "row", 1)
    mine = swap(gprobe.reshape(devices, -1, LANES))
    down_a = down_a + from_left_c
    above_a = passed_along(down_a, "row", 1)
    mine, above_b, _ = lax.optimization_barrier((mine, above_b, down_a))
    given, right_ab = lax.optimization_barrier((add_up(mine), right_ab))
    left_ab = passed_along(right_ab, "tile", 1)
    sum_two = swap(given).reshape(current.shape)
    object_out = simple(functools.partial(object_kernel, dims), object_field.shape, "last_object",
                        16, (own, left_ab, above_a, above_b))
    sum_two, _ = lax.optimization_barrier((sum_two, object_out))
    probe_out = simple(functools.partial(probe_kernel, probe_rate), probe.shape, "last_probe",
                       8, (current, sum_one, sum_two))
    return (object_out, probe_out)


def solution(mesh):
    placed = (
        P(None, "row", "tile"),
        P(),
        P(("tile", "row"), None, None),
        P(("tile", "row")),
        P(("tile", "row")),
        P(None, ("tile", "row")),
        P(None, ("tile", "row")),
    )
    return jax.shard_map(
        local, mesh=mesh, in_specs=placed, out_specs=(P(None, "row", "tile"), P()), check_vma=False
    )
```

```python
import functools
import math

import jax
import jax.numpy as jnp
import numpy as np
from jax import lax
from jax.experimental import pallas as pl
from jax.experimental.pallas import tpu as pltpu
from jax.sharding import PartitionSpec as P

LIVE = 6
LANES = 128
MIB = 1024 * 1024
F32 = jnp.float32
BF16 = jnp.bfloat16


def passed_along(value, axis, steps):
    count = lax.axis_size(axis)
    first, last = (max(0, -steps), min(count, count - steps))
    return lax.ppermute(value, axis, [(source, source + steps) for source in range(first, last)])


def tables(length):
    counter = np.arange(length, dtype=np.int32)
    product = counter[:, None] * counter[None, :] % length
    angle = product.astype(np.float32) * np.float32(2.0 * math.pi / length)
    factor = np.float32(1.0 / math.sqrt(length))
    cosine = (np.cos(angle) * factor).astype(BF16)
    sine = (np.sin(angle) * factor).astype(BF16)
    forward = np.block([[cosine, sine], [-sine, cosine]])
    backward = np.block([[cosine, -sine], [sine, cosine]])
    return forward, backward


def mul(left, right):
    return jnp.dot(left, right, preferred_element_type=F32)


def start_slots(step, batch, intensity, measured, sems):
    copies = []
    for s in range(batch.shape[1]):
        copies.append(
            pltpu.make_async_copy(intensity.at[batch[step, s]], measured.at[s], sems.at[s]))
    for copy in copies:
        copy.start()
    return copies


def clear(grad, gprobe, waves, patches):
    grad[...] = jnp.zeros_like(grad)
    gprobe[...] = jnp.zeros_like(gprobe)
    waves[1][...] = jnp.zeros_like(waves[1])
    patches[1][...] = jnp.zeros_like(patches[1])


def slot_loop(step, side, batch, live, rows, cols, mats, probe, ext, grad, gprobe,
              measured, exits, waves, patches):
    forward, backward = mats.at[0], mats.at[1]
    lane = lax.broadcasted_iota(jnp.int32, (side, LANES), 1)
    halves = side // LANES
    count = live[step, 0]

    def corner_of(s):
        stored = batch[step, s]
        col = cols[stored]
        return rows[stored], col // LANES, col % LANES

    def window(part, tile, row, shift):
        turn = (LANES - shift) & (LANES - 1)
        turned = [
            pltpu.roll(ext[part, tile + j, pl.ds(row, side), :], turn, 1) for j in range(halves + 1)
        ]
        keep = lane < LANES - shift
        return [jnp.where(keep, turned[j], turned[j + 1]) for j in range(halves)]

    def place(part, tile, row, shift, values):
        turned = [pltpu.roll(v, shift, 1) for v in values]
        keep = lane >= shift
        zero = jnp.zeros((side, LANES), F32)
        for j in range(halves + 1):
            here = turned[j] if j < halves else zero
            prior = turned[j - 1] if j else zero
            at = (part, tile + j, pl.ds(row, side), slice(None))
            grad[at] = grad[at] + jnp.where(keep, here, prior)

    def first_half(s, buffer, alive):
        row, tile, shift = corner_of(s)
        exit_in, wave, patch = exits[buffer], waves[buffer], patches[buffer]
        patch_r = window(0, tile, row, shift)
        patch_i = window(1, tile, row, shift)
        for j in range(halves):
            p_r, p_i = probe[0, j], probe[1, j]
            at = slice(j * LANES, (j + 1) * LANES)
            patch[0, j] = patch_r[j]
            patch[1, j] = patch_i[j]
            exit_in[0:side, at] = (p_r * patch_r[j] - p_i * patch_i[j]).astype(BF16)
            exit_in[side:, at] = (p_r * patch_i[j] + p_i * patch_r[j]).astype(BF16)
        half = mul(forward[...], exit_in[...]).astype(BF16)
        far = mul(jnp.concatenate([half[:side], half[side:]], axis=1), backward[...])
        far_r, far_i = far[:, :side], far[:, side:]
        excess = far_r * far_r + far_i * far_i - measured[s].astype(F32)
        if alive is not None:
            excess = excess * alive
        wave[0:side, :] = (excess * far_r).astype(BF16)
        wave[side:, :] = (excess * far_i).astype(BF16)

    def second_half(s, buffer):
        row, tile, shift = corner_of(s)
        wave, patch = waves[buffer], patches[buffer]
        mid = mul(backward[...], wave[...]).astype(BF16)
        back = mul(jnp.concatenate([mid[:side], mid[side:]], axis=1), forward[...])
        object_r, object_i = [], []
        for j in range(halves):
            p_r, p_i = probe[0, j], probe[1, j]
            o_r, o_i = patch[0, j], patch[1, j]
            b_r = back[:, j * LANES:(j + 1) * LANES]
            b_i = back[:, side + j * LANES:side + (j + 1) * LANES]
            object_r.append(p_r * b_r + p_i * b_i)
            object_i.append(p_r * b_i - p_i * b_r)
            gprobe[0, j] += o_r * b_r + o_i * b_i
            gprobe[1, j] += o_r * b_i - o_i * b_r
        place(0, tile, row, shift, object_r)
        place(1, tile, row, shift, object_i)

    def two_slots(k, carry):
        even = 2 * k
        odd = jnp.minimum(even + 1, batch.shape[1] - 1)
        alive = jnp.where(even + 1 < count, 1.0, 0.0).astype(F32)
        second_half(jnp.maximum(even - 1, 0), 1)
        first_half(even, 0, None)
        second_half(even, 0)
        first_half(odd, 1, alive)
        return carry

    pairs = (count + 1) // 2
    lax.fori_loop(0, pairs, two_slots, 0)
    second_half(jnp.minimum(2 * pairs - 1, batch.shape[1] - 1), 1)


def tiled_copies(field, part_rows, part_cols, ext, row0, col0):
    pairs = []
    for part in range(2):
        for j in range(part_cols // LANES):
            pairs.append((
                field.at[part, :, pl.ds(j * LANES, LANES)],
                ext.at[part, col0 // LANES + j, pl.ds(row0, part_rows), :],
            ))
    return pairs


def run_copies(pairs, sems, base=0):
    copies = [pltpu.make_async_copy(src, dst, sems.at[base + i]) for i, (src, dst) in enumerate(pairs)]
    for copy in copies:
        copy.start()
    return copies


def update_out(ext, grad, target, sems, base):
    parts, tiles, rows = target.shape[:3]
    copies = []
    for part in range(parts):
        for j in range(tiles):
            ext[part, j, 0:rows, :] -= 0.25 * grad[part, j, 0:rows, :]
            copies += run_copies([(ext.at[part, j, pl.ds(0, rows), :], target.at[part, j])],
                                 sems, base + len(copies))
    return copies


def first_kernel(dims, batch, live, rows, cols, probe, intensity, tables_in,
                 field, below_a, below_b, beside, corner,
                 old, middle, gprobe_out, right_c, left_c, right_b, left_b, down_b, up_b,
                 ext, grad, mats, measured, exit_0, exit_1, wave_0, wave_1, patch_0, patch_1,
                 gprobe, sems, moves):
    side, nrows, ncols = dims
    pairs = tiled_copies(field, nrows, ncols, ext, 0, 0)
    pairs += tiled_copies(below_a, side, side, ext, nrows, 0)
    pairs += tiled_copies(below_b, side, ncols - side, ext, nrows, side)
    pairs += tiled_copies(beside, nrows, side, ext, 0, ncols)
    pairs += tiled_copies(corner, side, side, ext, nrows, ncols)
    copies = run_copies(pairs + [(tables_in, mats)], moves)
    copies += start_slots(0, batch, intensity, measured, sems)
    waves, patches = (wave_0, wave_1), (patch_0, patch_1)
    clear(grad, gprobe, waves, patches)
    for copy in copies:
        copy.wait()
    keeping = pltpu.make_async_copy(ext, old, moves.at[len(pairs) + 1])
    keeping.start()
    slot_loop(0, side, batch, live, rows, cols, mats, probe, ext, grad, gprobe,
              measured, (exit_0, exit_1), waves, patches)
    t = side // LANES
    last = ncols // LANES
    a_rows, c_rows = pl.ds(0, side), pl.ds(nrows, side)
    b_rows = pl.ds(side, nrows - side)
    left, mid, right = pl.ds(0, t), pl.ds(t, last - t), pl.ds(last, t)
    pairs = [
        (gprobe, gprobe_out),
        (grad.at[:, right, a_rows, :], right_c.at[0]),
        (grad.at[:, right, c_rows, :], right_c.at[1]),
        (grad.at[:, left, a_rows, :], left_c.at[0]),
        (grad.at[:, left, c_rows, :], left_c.at[1]),
        (grad.at[:, right, b_rows, :], right_b),
        (grad.at[:, left, b_rows, :], left_b),
        (grad.at[:, mid, c_rows, :], down_b),
        (grad.at[:, mid, a_rows, :], up_b),
    ]
    pairs.append((grad.at[:, mid, b_rows, :], middle))
    copies = run_copies(pairs, moves)
    keeping.wait()
    for copy in copies:
        copy.wait()


def update_kernel(dims, edge, old, middle, left_c, right_c, left_b, right_b, down_b, up_b,
                  from_left_c, from_right_c, from_up, from_down,
                  part, ext, grad, lc_in, rc_in, u_in, d_in, moves):
    side, nrows, ncols = dims
    t = side // LANES
    last = ncols // LANES
    a_rows, c_rows = pl.ds(0, side), pl.ds(nrows, side)
    b_rows = pl.ds(side, nrows - side)
    left, mid, right = pl.ds(0, t), pl.ds(t, last - t), pl.ds(last, t)
    copies = run_copies([
        (old, ext), (from_left_c, lc_in), (from_right_c, rc_in), (from_up, u_in),
        (from_down, d_in),
        (right_c.at[0], grad.at[:, right, a_rows, :]),
        (right_c.at[1], grad.at[:, right, c_rows, :]),
        (left_c.at[0], grad.at[:, left, a_rows, :]),
        (left_c.at[1], grad.at[:, left, c_rows, :]),
        (right_b, grad.at[:, right, b_rows, :]),
        (left_b, grad.at[:, left, b_rows, :]),
        (down_b, grad.at[:, mid, c_rows, :]),
        (up_b, grad.at[:, mid, a_rows, :]),
        (middle, grad.at[:, mid, b_rows, :]),
    ], moves)
    for copy in copies:
        copy.wait()
    received = {
        (0, 0): lc_in[0], (0, 2): lc_in[1], (1, 0): u_in[...], (1, 2): d_in[...],
        (2, 0): rc_in[0], (2, 2): rc_in[1],
    }
    for i, tiles in enumerate((slice(0, t), slice(t, last), slice(last, last + t))):
        for k, band in enumerate((slice(0, side), slice(side, nrows), slice(nrows, nrows + side))):
            step = grad[:, tiles, band, :]
            if (i, k) in received:
                step = step + received[i, k]
            ext[:, tiles, band, :] = ext[:, tiles, band, :] - 0.25 * step

    @pl.when(edge[0] == 1)
    def _():
        ext[:, :, nrows:, :] = jnp.zeros((2, last + t, side, LANES), F32)

    @pl.when(edge[1] == 1)
    def _():
        ext[:, last:, :, :] = jnp.zeros((2, t, nrows + side, LANES), F32)

    for copy in run_copies([(ext, part)], moves):
        copy.wait()


def share_kernel(received, given):
    summed = received[0]
    for i in range(1, received.shape[0]):
        summed = summed + received[i]
    for i in range(received.shape[0]):
        given[i] = summed


def second_kernel(dims, rate, batch, live, rows, cols, edge, probe, summed,
                  intensity, tables_in, part_in, from_up_c, from_down_c, from_left, from_right,
                  own_out, gprobe_out, right_c, right_ab, down_a, down_b,
                  ext, grad, mats, measured, exit_0, exit_1, wave_0, wave_1, patch_0, patch_1,
                  gprobe, now, sems, moves):
    side, nrows, ncols = dims
    t = side // LANES
    last = ncols // LANES
    copies = run_copies([(part_in, ext), (tables_in, mats)], moves)
    copies += start_slots(1, batch, intensity, measured, sems)
    waves, patches = (wave_0, wave_1), (patch_0, patch_1)
    clear(grad, gprobe, waves, patches)
    now[...] = probe[...] - rate * summed[...]
    for copy in copies:
        copy.wait()
    a_rows, c_rows = slice(0, side), slice(nrows, nrows + side)
    b_rows = slice(side, nrows)
    left, right = slice(0, t), slice(last, last + t)
    for rows_of, corner in ((a_rows, from_up_c), (c_rows, from_down_c)):
        ext[:, left, rows_of, :] -= 0.25 * corner[0]
    ext[:, left, b_rows, :] -= 0.25 * from_left[...]

    @pl.when(edge[1] == 0)
    def _():
        for rows_of, corner in ((a_rows, from_up_c), (c_rows, from_down_c)):
            ext[:, right, rows_of, :] -= 0.25 * corner[1]
        ext[:, right, b_rows, :] -= 0.25 * from_right[...]

    slot_loop(1, side, batch, live, rows, cols, mats, now, ext, grad, gprobe,
              measured, (exit_0, exit_1), waves, patches)
    c_rows, own_rows = pl.ds(nrows, side), pl.ds(0, nrows)
    right = pl.ds(last, t)
    pairs = [
        (gprobe, gprobe_out),
        (grad.at[:, right, c_rows, :], right_c),
        (grad.at[:, pl.ds(t, last - t), c_rows, :], down_b),
        (grad.at[:, pl.ds(0, t), c_rows, :], down_a),
        (grad.at[:, right, own_rows, :], right_ab),
    ]
    copies = run_copies(pairs, moves)
    copies += update_out(ext, grad, own_out, moves, len(pairs))
    for copy in copies:
        copy.wait()


def object_kernel(dims, own, left_ab, above_a, above_b, object_out):
    side, nrows, ncols = dims
    t = side // LANES
    for part in range(2):
        for j in range(ncols // LANES):
            lanes = slice(j * LANES, (j + 1) * LANES)
            if j < t:
                top = own[part, j, 0:side, :] - 0.25 * (
                    left_ab[part, j, 0:side, :] + above_a[part, j])
                low = own[part, j, side:, :] - 0.25 * left_ab[part, j, side:, :]
            else:
                top = own[part, j, 0:side, :] - 0.25 * above_b[part, j - t]
                low = own[part, j, side:, :]
            object_out[part, 0:side, lanes] = top
            object_out[part, side:, lanes] = low


def probe_kernel(rate, probe, sum_one, sum_two, probe_out):
    for part in range(2):
        for j in range(probe.shape[1]):
            probe_out[part, :, j * LANES:(j + 1) * LANES] = (
                probe[part, j] - rate * (sum_one[part, j] + sum_two[part, j]))


def call(kernel, dims, slots, scalars, vectors, plain, received, outs, extra, limit,
         name):
    side, nrows, ncols = dims
    big = (2, (ncols + side) // LANES, nrows + side, LANES)
    smem = pl.BlockSpec(memory_space=pltpu.SMEM)
    vmem = pl.BlockSpec(memory_space=pltpu.VMEM)
    hbm = pl.BlockSpec(memory_space=pltpu.HBM)
    return pl.pallas_call(
        kernel,
        out_shape=[jax.ShapeDtypeStruct(shape, F32) for shape in outs],
        in_specs=([smem] * len(scalars) + [vmem] * len(vectors) + [hbm] * len(plain)
                  + [vmem] * len(received)),
        out_specs=[hbm] * len(outs),
        scratch_shapes=[
            pltpu.VMEM(big, F32),
            pltpu.VMEM(big, F32),
            pltpu.VMEM((2, 2 * side, 2 * side), BF16),
            pltpu.VMEM((slots, side, side), BF16),
        ] + [pltpu.VMEM((2 * side, side), BF16)] * 4
        + [pltpu.VMEM((2, side // LANES, side, LANES), F32)] * 3
        + [pltpu.VMEM(shape, F32) for shape in extra] + [
            pltpu.SemaphoreType.DMA((slots,)),
            pltpu.SemaphoreType.DMA((48,)),
        ],
        compiler_params=pltpu.CompilerParams(vmem_limit_bytes=limit * MIB),
        name=name,
    )(*scalars, *vectors, *plain, *received)


def swap(shares):
    return lax.all_to_all(shares, ("tile", "row"), 0, 0, tiled=True)


def add_up(mine):
    return pl.pallas_call(
        share_kernel, out_shape=jax.ShapeDtypeStruct(mine.shape, F32), name="sum_shares",
        compiler_params=pltpu.CompilerParams(vmem_limit_bytes=4 * MIB),
    )(mine)


def update(dims, edge, plain):
    hbm = pl.BlockSpec(memory_space=pltpu.HBM)
    scratch = [plain[0], plain[0]] + list(plain[8:])
    return pl.pallas_call(
        functools.partial(update_kernel, dims),
        out_shape=jax.ShapeDtypeStruct(plain[0].shape, F32),
        in_specs=[pl.BlockSpec(memory_space=pltpu.SMEM)] + [hbm] * len(plain),
        out_specs=hbm,
        scratch_shapes=[pltpu.VMEM(array.shape, F32) for array in scratch]
        + [pltpu.SemaphoreType.DMA((16,))],
        compiler_params=pltpu.CompilerParams(vmem_limit_bytes=56 * MIB),
        name="update_object",
    )(edge, *plain)


def simple(kernel, shape, name, limit, vectors):
    vmem = pl.BlockSpec(memory_space=pltpu.VMEM)
    return pl.pallas_call(
        kernel,
        out_shape=jax.ShapeDtypeStruct(shape, F32),
        in_specs=[vmem] * len(vectors),
        out_specs=vmem,
        compiler_params=pltpu.CompilerParams(vmem_limit_bytes=limit * MIB),
        name=name,
    )(*vectors)


def local(object_field, probe, intensity, pool_rows, pool_cols, batch, live):
    side = probe.shape[1]
    nrows, ncols = object_field.shape[1:]
    dims = (side, nrows, ncols)
    slots = batch.shape[1]
    t = side // LANES
    total = (ncols + side) // LANES
    probe_rate = 0.125 / math.sqrt(LIVE * lax.axis_size("tile") * lax.axis_size("row"))
    both = jnp.asarray(np.stack(tables(side)))
    current = probe.reshape(2, side, t, LANES).transpose(0, 2, 1, 3)

    first, rest = lax.optimization_barrier((object_field[:, :side, :side], object_field))
    below_a = passed_along(first, "row", -1)
    beside = passed_along(rest[:, :, :side], "tile", -1)
    below_b = passed_along(rest[:, :side, side:], "row", -1)
    corner = passed_along(below_a, "tile", -1)

    edge = jnp.stack([
        (lax.axis_index("row") == lax.axis_size("row") - 1).astype(jnp.int32),
        (lax.axis_index("tile") == lax.axis_size("tile") - 1).astype(jnp.int32)])
    scalars = (batch, live, pool_rows, pool_cols)
    devices = lax.axis_size("tile") * lax.axis_size("row")
    big = (2, total, nrows + side, LANES)
    corners = (2, 2, t, side, LANES)
    strip = (2, ncols // LANES - t, side, LANES)
    side_b = (2, t, nrows - side, LANES)
    middle_b = (2, ncols // LANES - t, nrows - side, LANES)
    old, middle, gprobe, right_c, left_c, right_b, left_b, down_b, up_b = call(
        functools.partial(first_kernel, dims), dims, slots, scalars, (current,),
        (intensity, both, object_field, below_a, below_b, beside, corner), (),
        [big, middle_b, current.shape, corners, corners, side_b, side_b, strip, strip], [],
        54, "first_iteration")

    from_left_c = passed_along(right_c, "tile", 1)
    from_right_c = passed_along(left_c, "tile", -1)
    from_up_b = passed_along(down_b, "row", 1)
    from_down_b = passed_along(up_b, "row", -1)
    mine = swap(gprobe.reshape(devices, -1, LANES))
    mine, from_left_c, from_right_c = lax.optimization_barrier((mine, from_left_c, from_right_c))
    down_c = jnp.stack([left_c[1] + from_left_c[1], right_c[1] + from_right_c[1]])
    up_c = jnp.stack([left_c[0] + from_left_c[0], right_c[0] + from_right_c[0]])
    from_up_c = passed_along(down_c, "row", 1)
    from_down_c = passed_along(up_c, "row", -1)
    mine, from_up_b, from_down_b, _, _ = lax.optimization_barrier(
        (mine, from_up_b, from_down_b, down_c, up_c))
    given, right_b, left_b = lax.optimization_barrier((add_up(mine), right_b, left_b))
    from_left_b = passed_along(right_b, "tile", 1)
    from_right_b = passed_along(left_b, "tile", -1)
    sum_one = swap(given).reshape(current.shape)
    part = update(dims, edge, (old, middle, left_c, right_c, left_b, right_b, down_b, up_b,
                               from_left_c, from_right_c, from_up_b, from_down_b))

    own, gprobe, right_c, right_ab, down_a, down_b = call(
        functools.partial(second_kernel, dims, probe_rate), dims, slots, scalars + (edge,),
        (current, sum_one), (intensity, both, part),
        (from_up_c, from_down_c, from_left_b, from_right_b),
        [(2, ncols // LANES, nrows, LANES), current.shape, (2, t, side, LANES),
         (2, t, nrows, LANES), (2, t, side, LANES), strip],
        [current.shape], 52, "second_iteration")

    from_left_c = passed_along(right_c, "tile", 1)
    above_b = passed_along(down_b, "row", 1)
    mine = swap(gprobe.reshape(devices, -1, LANES))
    down_a = down_a + from_left_c
    above_a = passed_along(down_a, "row", 1)
    mine, above_b, _ = lax.optimization_barrier((mine, above_b, down_a))
    given, right_ab = lax.optimization_barrier((add_up(mine), right_ab))
    left_ab = passed_along(right_ab, "tile", 1)
    sum_two = swap(given).reshape(current.shape)
    object_out = simple(functools.partial(object_kernel, dims), object_field.shape, "last_object",
                        16, (own, left_ab, above_a, above_b))
    sum_two, _ = lax.optimization_barrier((sum_two, object_out))
    probe_out = simple(functools.partial(probe_kernel, probe_rate), probe.shape, "last_probe",
                       8, (current, sum_one, sum_two))
    return (object_out, probe_out)


def solution(mesh):
    placed = (
        P(None, "row", "tile"),
        P(),
        P(("tile", "row"), None, None),
        P(("tile", "row")),
        P(("tile", "row")),
        P(None, ("tile", "row")),
        P(None, ("tile", "row")),
    )
    return jax.shard_map(
        local, mesh=mesh, in_specs=placed, out_specs=(P(None, "row", "tile"), P()), check_vma=False
    )
```

```python
import functools
import math

import jax
import jax.numpy as jnp
import numpy as np
from jax import lax
from jax.experimental import pallas as pl
from jax.experimental.pallas import tpu as pltpu
from jax.sharding import PartitionSpec as P

LIVE = 6
LANES = 128
MIB = 1024 * 1024
F32 = jnp.float32
BF16 = jnp.bfloat16


def passed_along(value, axis, steps):
    count = lax.axis_size(axis)
    first, last = (max(0, -steps), min(count, count - steps))
    return lax.ppermute(value, axis, [(source, source + steps) for source in range(first, last)])


def tables(length):
    counter = np.arange(length, dtype=np.int32)
    product = counter[:, None] * counter[None, :] % length
    angle = product.astype(np.float32) * np.float32(2.0 * math.pi / length)
    factor = np.float32(1.0 / math.sqrt(length))
    cosine = (np.cos(angle) * factor).astype(BF16)
    sine = (np.sin(angle) * factor).astype(BF16)
    forward = np.block([[cosine, sine], [-sine, cosine]])
    backward = np.block([[cosine, -sine], [sine, cosine]])
    return forward, backward


def mul(left, right):
    return jnp.dot(left, right, preferred_element_type=F32)


def start_slots(step, batch, intensity, measured, sems):
    copies = []
    for s in range(batch.shape[1]):
        copies.append(
            pltpu.make_async_copy(intensity.at[batch[step, s]], measured.at[s], sems.at[s]))
    for copy in copies:
        copy.start()
    return copies


def clear(grad, gprobe, waves, patches):
    grad[...] = jnp.zeros_like(grad)
    gprobe[...] = jnp.zeros_like(gprobe)
    waves[1][...] = jnp.zeros_like(waves[1])
    patches[1][...] = jnp.zeros_like(patches[1])


def slot_loop(step, side, batch, live, rows, cols, mats, probe, ext, grad, gprobe,
              measured, exits, waves, patches):
    forward, backward = mats.at[0], mats.at[1]
    lane = lax.broadcasted_iota(jnp.int32, (side, LANES), 1)
    halves = side // LANES
    count = live[step, 0]

    def corner_of(s):
        stored = batch[step, s]
        col = cols[stored]
        return rows[stored], col // LANES, col % LANES

    def window(part, tile, row, shift):
        turn = (LANES - shift) & (LANES - 1)
        turned = [
            pltpu.roll(ext[part, tile + j, pl.ds(row, side), :], turn, 1) for j in range(halves + 1)
        ]
        keep = lane < LANES - shift
        return [jnp.where(keep, turned[j], turned[j + 1]) for j in range(halves)]

    def place(part, tile, row, shift, values):
        turned = [pltpu.roll(v, shift, 1) for v in values]
        keep = lane >= shift
        zero = jnp.zeros((side, LANES), F32)
        for j in range(halves + 1):
            here = turned[j] if j < halves else zero
            prior = turned[j - 1] if j else zero
            at = (part, tile + j, pl.ds(row, side), slice(None))
            grad[at] = grad[at] + jnp.where(keep, here, prior)

    def first_half(s, buffer, alive):
        row, tile, shift = corner_of(s)
        exit_in, wave, patch = exits[buffer], waves[buffer], patches[buffer]
        patch_r = window(0, tile, row, shift)
        patch_i = window(1, tile, row, shift)
        for j in range(halves):
            p_r, p_i = probe[0, j], probe[1, j]
            at = slice(j * LANES, (j + 1) * LANES)
            patch[0, j] = patch_r[j]
            patch[1, j] = patch_i[j]
            exit_in[0:side, at] = (p_r * patch_r[j] - p_i * patch_i[j]).astype(BF16)
            exit_in[side:, at] = (p_r * patch_i[j] + p_i * patch_r[j]).astype(BF16)
        half = mul(forward[...], exit_in[...]).astype(BF16)
        far = mul(jnp.concatenate([half[:side], half[side:]], axis=1), backward[...])
        far_r, far_i = far[:, :side], far[:, side:]
        excess = far_r * far_r + far_i * far_i - measured[s].astype(F32)
        if alive is not None:
            excess = excess * alive
        wave[0:side, :] = (excess * far_r).astype(BF16)
        wave[side:, :] = (excess * far_i).astype(BF16)

    def second_half(s, buffer):
        row, tile, shift = corner_of(s)
        wave, patch = waves[buffer], patches[buffer]
        mid = mul(backward[...], wave[...]).astype(BF16)
        back = mul(jnp.concatenate([mid[:side], mid[side:]], axis=1), forward[...])
        object_r, object_i = [], []
        for j in range(halves):
            p_r, p_i = probe[0, j], probe[1, j]
            o_r, o_i = patch[0, j], patch[1, j]
            b_r = back[:, j * LANES:(j + 1) * LANES]
            b_i = back[:, side + j * LANES:side + (j + 1) * LANES]
            object_r.append(p_r * b_r + p_i * b_i)
            object_i.append(p_r * b_i - p_i * b_r)
            gprobe[0, j] += o_r * b_r + o_i * b_i
            gprobe[1, j] += o_r * b_i - o_i * b_r
        place(0, tile, row, shift, object_r)
        place(1, tile, row, shift, object_i)

    def two_slots(k, carry):
        even = 2 * k
        odd = jnp.minimum(even + 1, batch.shape[1] - 1)
        alive = jnp.where(even + 1 < count, 1.0, 0.0).astype(F32)
        second_half(jnp.maximum(even - 1, 0), 1)
        first_half(even, 0, None)
        second_half(even, 0)
        first_half(odd, 1, alive)
        return carry

    pairs = (count + 1) // 2
    lax.fori_loop(0, pairs, two_slots, 0)
    second_half(jnp.minimum(2 * pairs - 1, batch.shape[1] - 1), 1)


def tiled_copies(field, part_rows, part_cols, ext, row0, col0):
    pairs = []
    for part in range(2):
        for j in range(part_cols // LANES):
            pairs.append((
                field.at[part, :, pl.ds(j * LANES, LANES)],
                ext.at[part, col0 // LANES + j, pl.ds(row0, part_rows), :],
            ))
    return pairs


def run_copies(pairs, sems, base=0):
    copies = [pltpu.make_async_copy(src, dst, sems.at[base + i]) for i, (src, dst) in enumerate(pairs)]
    for copy in copies:
        copy.start()
    return copies


def update_out(ext, grad, target, sems, base):
    parts, tiles, rows = target.shape[:3]
    copies = []
    for part in range(parts):
        for j in range(tiles):
            ext[part, j, 0:rows, :] -= 0.25 * grad[part, j, 0:rows, :]
            copies += run_copies([(ext.at[part, j, pl.ds(0, rows), :], target.at[part, j])],
                                 sems, base + len(copies))
    return copies


def first_kernel(dims, batch, live, rows, cols, probe, intensity, tables_in,
                 field, below_a, below_b, beside_a, beside_b, corner,
                 old, middle, gprobe_out, right_c, left_c, right_b, left_b, down_b, up_b,
                 ext, grad, mats, measured, exit_0, exit_1, wave_0, wave_1, patch_0, patch_1,
                 gprobe, sems, moves):
    side, nrows, ncols = dims
    pairs = tiled_copies(field, nrows, ncols, ext, 0, 0)
    pairs += tiled_copies(below_a, side, side, ext, nrows, 0)
    pairs += tiled_copies(below_b, side, ncols - side, ext, nrows, side)
    pairs += tiled_copies(beside_a, side, side, ext, 0, ncols)
    pairs += tiled_copies(beside_b, nrows - side, side, ext, side, ncols)
    pairs += tiled_copies(corner, side, side, ext, nrows, ncols)
    copies = run_copies(pairs + [(tables_in, mats)], moves)
    copies += start_slots(0, batch, intensity, measured, sems)
    waves, patches = (wave_0, wave_1), (patch_0, patch_1)
    clear(grad, gprobe, waves, patches)
    for copy in copies:
        copy.wait()
    keeping = pltpu.make_async_copy(ext, old, moves.at[len(pairs) + 1])
    keeping.start()
    slot_loop(0, side, batch, live, rows, cols, mats, probe, ext, grad, gprobe,
              measured, (exit_0, exit_1), waves, patches)
    t = side // LANES
    last = ncols // LANES
    a_rows, c_rows = pl.ds(0, side), pl.ds(nrows, side)
    b_rows = pl.ds(side, nrows - side)
    left, mid, right = pl.ds(0, t), pl.ds(t, last - t), pl.ds(last, t)
    pairs = [
        (gprobe, gprobe_out),
        (grad.at[:, right, a_rows, :], right_c.at[0]),
        (grad.at[:, right, c_rows, :], right_c.at[1]),
        (grad.at[:, left, a_rows, :], left_c.at[0]),
        (grad.at[:, left, c_rows, :], left_c.at[1]),
        (grad.at[:, right, b_rows, :], right_b),
        (grad.at[:, left, b_rows, :], left_b),
        (grad.at[:, mid, c_rows, :], down_b),
        (grad.at[:, mid, a_rows, :], up_b),
    ]
    pairs.append((grad.at[:, mid, b_rows, :], middle))
    copies = run_copies(pairs, moves)
    keeping.wait()
    for copy in copies:
        copy.wait()


def update_kernel(dims, edge, old, middle, left_c, right_c, left_b, right_b, down_b, up_b,
                  from_left_c, from_right_c, from_up, from_down,
                  part, ext, grad, lc_in, rc_in, u_in, d_in, moves):
    side, nrows, ncols = dims
    t = side // LANES
    last = ncols // LANES
    a_rows, c_rows = pl.ds(0, side), pl.ds(nrows, side)
    b_rows = pl.ds(side, nrows - side)
    left, mid, right = pl.ds(0, t), pl.ds(t, last - t), pl.ds(last, t)
    copies = run_copies([
        (old, ext), (from_left_c, lc_in), (from_right_c, rc_in), (from_up, u_in),
        (from_down, d_in),
        (right_c.at[0], grad.at[:, right, a_rows, :]),
        (right_c.at[1], grad.at[:, right, c_rows, :]),
        (left_c.at[0], grad.at[:, left, a_rows, :]),
        (left_c.at[1], grad.at[:, left, c_rows, :]),
        (right_b, grad.at[:, right, b_rows, :]),
        (left_b, grad.at[:, left, b_rows, :]),
        (down_b, grad.at[:, mid, c_rows, :]),
        (up_b, grad.at[:, mid, a_rows, :]),
        (middle, grad.at[:, mid, b_rows, :]),
    ], moves)
    for copy in copies:
        copy.wait()
    received = {
        (0, 0): lc_in[0], (0, 2): lc_in[1], (1, 0): u_in[...], (1, 2): d_in[...],
        (2, 0): rc_in[0], (2, 2): rc_in[1],
    }
    for i, tiles in enumerate((slice(0, t), slice(t, last), slice(last, last + t))):
        for k, band in enumerate((slice(0, side), slice(side, nrows), slice(nrows, nrows + side))):
            step = grad[:, tiles, band, :]
            if (i, k) in received:
                step = step + received[i, k]
            ext[:, tiles, band, :] = ext[:, tiles, band, :] - 0.25 * step

    @pl.when(edge[0] == 1)
    def _():
        ext[:, :, nrows:, :] = jnp.zeros((2, last + t, side, LANES), F32)

    @pl.when(edge[1] == 1)
    def _():
        ext[:, last:, :, :] = jnp.zeros((2, t, nrows + side, LANES), F32)

    for copy in run_copies([(ext, part)], moves):
        copy.wait()


def share_kernel(received, given):
    summed = received[0]
    for i in range(1, received.shape[0]):
        summed = summed + received[i]
    for i in range(received.shape[0]):
        given[i] = summed


def second_kernel(dims, rate, batch, live, rows, cols, edge, probe, summed,
                  intensity, tables_in, part_in, from_up_c, from_down_c, from_left, from_right,
                  own_out, gprobe_out, right_c, right_ab, down_a, down_b,
                  ext, grad, mats, measured, exit_0, exit_1, wave_0, wave_1, patch_0, patch_1,
                  gprobe, now, sems, moves):
    side, nrows, ncols = dims
    t = side // LANES
    last = ncols // LANES
    copies = run_copies([(part_in, ext), (tables_in, mats)], moves)
    copies += start_slots(1, batch, intensity, measured, sems)
    waves, patches = (wave_0, wave_1), (patch_0, patch_1)
    clear(grad, gprobe, waves, patches)
    now[...] = probe[...] - rate * summed[...]
    for copy in copies:
        copy.wait()
    a_rows, c_rows = slice(0, side), slice(nrows, nrows + side)
    b_rows = slice(side, nrows)
    left, right = slice(0, t), slice(last, last + t)
    for rows_of, corner in ((a_rows, from_up_c), (c_rows, from_down_c)):
        ext[:, left, rows_of, :] -= 0.25 * corner[0]
    ext[:, left, b_rows, :] -= 0.25 * from_left[...]

    @pl.when(edge[1] == 0)
    def _():
        for rows_of, corner in ((a_rows, from_up_c), (c_rows, from_down_c)):
            ext[:, right, rows_of, :] -= 0.25 * corner[1]
        ext[:, right, b_rows, :] -= 0.25 * from_right[...]

    slot_loop(1, side, batch, live, rows, cols, mats, now, ext, grad, gprobe,
              measured, (exit_0, exit_1), waves, patches)
    c_rows, own_rows = pl.ds(nrows, side), pl.ds(0, nrows)
    right = pl.ds(last, t)
    pairs = [
        (gprobe, gprobe_out),
        (grad.at[:, right, c_rows, :], right_c),
        (grad.at[:, pl.ds(t, last - t), c_rows, :], down_b),
        (grad.at[:, pl.ds(0, t), c_rows, :], down_a),
        (grad.at[:, right, own_rows, :], right_ab),
    ]
    copies = run_copies(pairs, moves)
    copies += update_out(ext, grad, own_out, moves, len(pairs))
    for copy in copies:
        copy.wait()


def object_kernel(dims, own, left_ab, above_a, above_b, object_out):
    side, nrows, ncols = dims
    t = side // LANES
    for part in range(2):
        for j in range(ncols // LANES):
            lanes = slice(j * LANES, (j + 1) * LANES)
            if j < t:
                top = own[part, j, 0:side, :] - 0.25 * (
                    left_ab[part, j, 0:side, :] + above_a[part, j])
                low = own[part, j, side:, :] - 0.25 * left_ab[part, j, side:, :]
            else:
                top = own[part, j, 0:side, :] - 0.25 * above_b[part, j - t]
                low = own[part, j, side:, :]
            object_out[part, 0:side, lanes] = top
            object_out[part, side:, lanes] = low


def probe_kernel(rate, probe, sum_one, sum_two, probe_out):
    for part in range(2):
        for j in range(probe.shape[1]):
            probe_out[part, :, j * LANES:(j + 1) * LANES] = (
                probe[part, j] - rate * (sum_one[part, j] + sum_two[part, j]))


def call(kernel, dims, slots, scalars, vectors, plain, received, outs, extra, limit,
         name):
    side, nrows, ncols = dims
    big = (2, (ncols + side) // LANES, nrows + side, LANES)
    smem = pl.BlockSpec(memory_space=pltpu.SMEM)
    vmem = pl.BlockSpec(memory_space=pltpu.VMEM)
    hbm = pl.BlockSpec(memory_space=pltpu.HBM)
    return pl.pallas_call(
        kernel,
        out_shape=[jax.ShapeDtypeStruct(shape, F32) for shape in outs],
        in_specs=([smem] * len(scalars) + [vmem] * len(vectors) + [hbm] * len(plain)
                  + [vmem] * len(received)),
        out_specs=[hbm] * len(outs),
        scratch_shapes=[
            pltpu.VMEM(big, F32),
            pltpu.VMEM(big, F32),
            pltpu.VMEM((2, 2 * side, 2 * side), BF16),
            pltpu.VMEM((slots, side, side), BF16),
        ] + [pltpu.VMEM((2 * side, side), BF16)] * 4
        + [pltpu.VMEM((2, side // LANES, side, LANES), F32)] * 3
        + [pltpu.VMEM(shape, F32) for shape in extra] + [
            pltpu.SemaphoreType.DMA((slots,)),
            pltpu.SemaphoreType.DMA((48,)),
        ],
        compiler_params=pltpu.CompilerParams(vmem_limit_bytes=limit * MIB),
        name=name,
    )(*scalars, *vectors, *plain, *received)


def swap(shares):
    return lax.all_to_all(shares, ("tile", "row"), 0, 0, tiled=True)


def add_up(mine):
    return pl.pallas_call(
        share_kernel, out_shape=jax.ShapeDtypeStruct(mine.shape, F32), name="sum_shares",
        compiler_params=pltpu.CompilerParams(vmem_limit_bytes=4 * MIB),
    )(mine)


def update(dims, edge, plain):
    hbm = pl.BlockSpec(memory_space=pltpu.HBM)
    scratch = [plain[0], plain[0]] + list(plain[8:])
    return pl.pallas_call(
        functools.partial(update_kernel, dims),
        out_shape=jax.ShapeDtypeStruct(plain[0].shape, F32),
        in_specs=[pl.BlockSpec(memory_space=pltpu.SMEM)] + [hbm] * len(plain),
        out_specs=hbm,
        scratch_shapes=[pltpu.VMEM(array.shape, F32) for array in scratch]
        + [pltpu.SemaphoreType.DMA((16,))],
        compiler_params=pltpu.CompilerParams(vmem_limit_bytes=56 * MIB),
        name="update_object",
    )(edge, *plain)


def simple(kernel, shape, name, limit, vectors):
    vmem = pl.BlockSpec(memory_space=pltpu.VMEM)
    return pl.pallas_call(
        kernel,
        out_shape=jax.ShapeDtypeStruct(shape, F32),
        in_specs=[vmem] * len(vectors),
        out_specs=vmem,
        compiler_params=pltpu.CompilerParams(vmem_limit_bytes=limit * MIB),
        name=name,
    )(*vectors)


def local(object_field, probe, intensity, pool_rows, pool_cols, batch, live):
    side = probe.shape[1]
    nrows, ncols = object_field.shape[1:]
    dims = (side, nrows, ncols)
    slots = batch.shape[1]
    t = side // LANES
    total = (ncols + side) // LANES
    probe_rate = 0.125 / math.sqrt(LIVE * lax.axis_size("tile") * lax.axis_size("row"))
    both = jnp.asarray(np.stack(tables(side)))
    current = probe.reshape(2, side, t, LANES).transpose(0, 2, 1, 3)

    first, rest = lax.optimization_barrier((object_field[:, :side, :side], object_field))
    below_a = passed_along(first, "row", -1)
    beside_a = passed_along(first, "tile", -1)
    beside_b = passed_along(rest[:, side:, :side], "tile", -1)
    below_b = passed_along(rest[:, :side, side:], "row", -1)
    corner = passed_along(below_a, "tile", -1)

    edge = jnp.stack([
        (lax.axis_index("row") == lax.axis_size("row") - 1).astype(jnp.int32),
        (lax.axis_index("tile") == lax.axis_size("tile") - 1).astype(jnp.int32)])
    scalars = (batch, live, pool_rows, pool_cols)
    devices = lax.axis_size("tile") * lax.axis_size("row")
    big = (2, total, nrows + side, LANES)
    corners = (2, 2, t, side, LANES)
    strip = (2, ncols // LANES - t, side, LANES)
    side_b = (2, t, nrows - side, LANES)
    middle_b = (2, ncols // LANES - t, nrows - side, LANES)
    old, middle, gprobe, right_c, left_c, right_b, left_b, down_b, up_b = call(
        functools.partial(first_kernel, dims), dims, slots, scalars, (current,),
        (intensity, both, object_field, below_a, below_b, beside_a, beside_b, corner), (),
        [big, middle_b, current.shape, corners, corners, side_b, side_b, strip, strip], [],
        54, "first_iteration")

    from_left_c = passed_along(right_c, "tile", 1)
    from_right_c = passed_along(left_c, "tile", -1)
    from_up_b = passed_along(down_b, "row", 1)
    from_down_b = passed_along(up_b, "row", -1)
    mine = swap(gprobe.reshape(devices, -1, LANES))
    mine, from_left_c, from_right_c = lax.optimization_barrier((mine, from_left_c, from_right_c))
    down_c = jnp.stack([left_c[1] + from_left_c[1], right_c[1] + from_right_c[1]])
    up_c = jnp.stack([left_c[0] + from_left_c[0], right_c[0] + from_right_c[0]])
    from_up_c = passed_along(down_c, "row", 1)
    from_down_c = passed_along(up_c, "row", -1)
    mine, from_up_b, from_down_b, _, _ = lax.optimization_barrier(
        (mine, from_up_b, from_down_b, down_c, up_c))
    given, right_b, left_b = lax.optimization_barrier((add_up(mine), right_b, left_b))
    from_left_b = passed_along(right_b, "tile", 1)
    from_right_b = passed_along(left_b, "tile", -1)
    sum_one = swap(given).reshape(current.shape)
    part = update(dims, edge, (old, middle, left_c, right_c, left_b, right_b, down_b, up_b,
                               from_left_c, from_right_c, from_up_b, from_down_b))

    own, gprobe, right_c, right_ab, down_a, down_b = call(
        functools.partial(second_kernel, dims, probe_rate), dims, slots, scalars + (edge,),
        (current, sum_one), (intensity, both, part),
        (from_up_c, from_down_c, from_left_b, from_right_b),
        [(2, ncols // LANES, nrows, LANES), current.shape, (2, t, side, LANES),
         (2, t, nrows, LANES), (2, t, side, LANES), strip],
        [current.shape], 52, "second_iteration")

    given = add_up(swap(gprobe.reshape(devices, -1, LANES)))
    given, right_c, right_ab, down_b = lax.optimization_barrier((given, right_c, right_ab, down_b))
    from_left_c = passed_along(right_c, "tile", 1)
    above_b = passed_along(down_b, "row", 1)
    left_ab = passed_along(right_ab, "tile", 1)
    above_a = passed_along(down_a + from_left_c, "row", 1)
    sum_two = swap(given).reshape(current.shape)
    object_out = simple(functools.partial(object_kernel, dims), object_field.shape, "last_object",
                        16, (own, left_ab, above_a, above_b))
    sum_two, _ = lax.optimization_barrier((sum_two, object_out))
    probe_out = simple(functools.partial(probe_kernel, probe_rate), probe.shape, "last_probe",
                       8, (current, sum_one, sum_two))
    return (object_out, probe_out)


def solution(mesh):
    placed = (
        P(None, "row", "tile"),
        P(),
        P(("tile", "row"), None, None),
        P(("tile", "row")),
        P(("tile", "row")),
        P(None, ("tile", "row")),
        P(None, ("tile", "row")),
    )
    return jax.shard_map(
        local, mesh=mesh, in_specs=placed, out_specs=(P(None, "row", "tile"), P()), check_vma=False
    )
```

```python
import functools
import math

import jax
import jax.numpy as jnp
import numpy as np
from jax import lax
from jax.experimental import pallas as pl
from jax.experimental.pallas import tpu as pltpu
from jax.sharding import PartitionSpec as P

LIVE = 6
LANES = 128
MIB = 1024 * 1024
F32 = jnp.float32
BF16 = jnp.bfloat16


def passed_along(value, axis, steps):
    count = lax.axis_size(axis)
    first, last = (max(0, -steps), min(count, count - steps))
    return lax.ppermute(value, axis, [(source, source + steps) for source in range(first, last)])


def tables(length):
    counter = np.arange(length, dtype=np.int32)
    product = counter[:, None] * counter[None, :] % length
    angle = product.astype(np.float32) * np.float32(2.0 * math.pi / length)
    factor = np.float32(1.0 / math.sqrt(length))
    cosine = (np.cos(angle) * factor).astype(BF16)
    sine = (np.sin(angle) * factor).astype(BF16)
    forward = np.block([[cosine, sine], [-sine, cosine]])
    backward = np.block([[cosine, -sine], [sine, cosine]])
    return forward, backward


def mul(left, right):
    return jnp.dot(left, right, preferred_element_type=F32)


def start_slots(step, batch, intensity, measured, sems):
    copies = []
    for s in range(batch.shape[1]):
        copies.append(
            pltpu.make_async_copy(intensity.at[batch[step, s]], measured.at[s], sems.at[s]))
    for copy in copies:
        copy.start()
    return copies


def clear(grad, gprobe, waves, patches):
    grad[...] = jnp.zeros_like(grad)
    gprobe[...] = jnp.zeros_like(gprobe)
    waves[1][...] = jnp.zeros_like(waves[1])
    patches[1][...] = jnp.zeros_like(patches[1])


def slot_loop(step, side, batch, live, rows, cols, mats, probe, ext, grad, gprobe,
              measured, exits, waves, patches):
    forward, backward = mats.at[0], mats.at[1]
    lane = lax.broadcasted_iota(jnp.int32, (side, LANES), 1)
    halves = side // LANES
    count = live[step, 0]

    def corner_of(s):
        stored = batch[step, s]
        col = cols[stored]
        return rows[stored], col // LANES, col % LANES

    def window(part, tile, row, shift):
        turn = (LANES - shift) & (LANES - 1)
        turned = [
            pltpu.roll(ext[part, tile + j, pl.ds(row, side), :], turn, 1) for j in range(halves + 1)
        ]
        keep = lane < LANES - shift
        return [jnp.where(keep, turned[j], turned[j + 1]) for j in range(halves)]

    def place(part, tile, row, shift, values):
        turned = [pltpu.roll(v, shift, 1) for v in values]
        keep = lane >= shift
        zero = jnp.zeros((side, LANES), F32)
        for j in range(halves + 1):
            here = turned[j] if j < halves else zero
            prior = turned[j - 1] if j else zero
            at = (part, tile + j, pl.ds(row, side), slice(None))
            grad[at] = grad[at] + jnp.where(keep, here, prior)

    def first_half(s, buffer, alive):
        row, tile, shift = corner_of(s)
        exit_in, wave, patch = exits[buffer], waves[buffer], patches[buffer]
        patch_r = window(0, tile, row, shift)
        patch_i = window(1, tile, row, shift)
        for j in range(halves):
            p_r, p_i = probe[0, j], probe[1, j]
            at = slice(j * LANES, (j + 1) * LANES)
            patch[0, j] = patch_r[j]
            patch[1, j] = patch_i[j]
            exit_in[0:side, at] = (p_r * patch_r[j] - p_i * patch_i[j]).astype(BF16)
            exit_in[side:, at] = (p_r * patch_i[j] + p_i * patch_r[j]).astype(BF16)
        half = mul(forward[...], exit_in[...]).astype(BF16)
        far = mul(jnp.concatenate([half[:side], half[side:]], axis=1), backward[...])
        far_r, far_i = far[:, :side], far[:, side:]
        excess = far_r * far_r + far_i * far_i - measured[s].astype(F32)
        if alive is not None:
            excess = excess * alive
        wave[0:side, :] = (excess * far_r).astype(BF16)
        wave[side:, :] = (excess * far_i).astype(BF16)

    def second_half(s, buffer):
        row, tile, shift = corner_of(s)
        wave, patch = waves[buffer], patches[buffer]
        mid = mul(backward[...], wave[...]).astype(BF16)
        back = mul(jnp.concatenate([mid[:side], mid[side:]], axis=1), forward[...])
        object_r, object_i = [], []
        for j in range(halves):
            p_r, p_i = probe[0, j], probe[1, j]
            o_r, o_i = patch[0, j], patch[1, j]
            b_r = back[:, j * LANES:(j + 1) * LANES]
            b_i = back[:, side + j * LANES:side + (j + 1) * LANES]
            object_r.append(p_r * b_r + p_i * b_i)
            object_i.append(p_r * b_i - p_i * b_r)
            gprobe[0, j] += o_r * b_r + o_i * b_i
            gprobe[1, j] += o_r * b_i - o_i * b_r
        place(0, tile, row, shift, object_r)
        place(1, tile, row, shift, object_i)

    def two_slots(k, carry):
        even = 2 * k
        odd = jnp.minimum(even + 1, batch.shape[1] - 1)
        alive = jnp.where(even + 1 < count, 1.0, 0.0).astype(F32)
        second_half(jnp.maximum(even - 1, 0), 1)
        first_half(even, 0, None)
        second_half(even, 0)
        first_half(odd, 1, alive)
        return carry

    pairs = (count + 1) // 2
    lax.fori_loop(0, pairs, two_slots, 0)
    second_half(jnp.minimum(2 * pairs - 1, batch.shape[1] - 1), 1)


def tiled_copies(field, part_rows, part_cols, ext, row0, col0):
    pairs = []
    for part in range(2):
        for j in range(part_cols // LANES):
            pairs.append((
                field.at[part, :, pl.ds(j * LANES, LANES)],
                ext.at[part, col0 // LANES + j, pl.ds(row0, part_rows), :],
            ))
    return pairs


def run_copies(pairs, sems, base=0):
    copies = [pltpu.make_async_copy(src, dst, sems.at[base + i]) for i, (src, dst) in enumerate(pairs)]
    for copy in copies:
        copy.start()
    return copies


def update_out(ext, grad, target, sems, base):
    parts, tiles, rows = target.shape[:3]
    copies = []
    for part in range(parts):
        for j in range(tiles):
            ext[part, j, 0:rows, :] -= 0.25 * grad[part, j, 0:rows, :]
            copies += run_copies([(ext.at[part, j, pl.ds(0, rows), :], target.at[part, j])],
                                 sems, base + len(copies))
    return copies


def first_kernel(dims, batch, live, rows, cols, probe, intensity, tables_in,
                 field, below_a, below_b, beside_a, beside_b, corner,
                 old, middle, gprobe_out, right_c, left_c, right_b, left_b, down_b, up_b,
                 ext, grad, mats, measured, exit_0, exit_1, wave_0, wave_1, patch_0, patch_1,
                 gprobe, sems, moves):
    side, nrows, ncols = dims
    pairs = tiled_copies(field, nrows, ncols, ext, 0, 0)
    pairs += tiled_copies(below_a, side, side, ext, nrows, 0)
    pairs += tiled_copies(below_b, side, ncols - side, ext, nrows, side)
    pairs += tiled_copies(beside_a, side, side, ext, 0, ncols)
    pairs += tiled_copies(beside_b, nrows - side, side, ext, side, ncols)
    pairs += tiled_copies(corner, side, side, ext, nrows, ncols)
    copies = run_copies(pairs + [(tables_in, mats)], moves)
    copies += start_slots(0, batch, intensity, measured, sems)
    waves, patches = (wave_0, wave_1), (patch_0, patch_1)
    clear(grad, gprobe, waves, patches)
    for copy in copies:
        copy.wait()
    keeping = pltpu.make_async_copy(ext, old, moves.at[len(pairs) + 1])
    keeping.start()
    slot_loop(0, side, batch, live, rows, cols, mats, probe, ext, grad, gprobe,
              measured, (exit_0, exit_1), waves, patches)
    t = side // LANES
    last = ncols // LANES
    a_rows, c_rows = pl.ds(0, side), pl.ds(nrows, side)
    b_rows = pl.ds(side, nrows - side)
    left, mid, right = pl.ds(0, t), pl.ds(t, last - t), pl.ds(last, t)
    pairs = [
        (gprobe, gprobe_out),
        (grad.at[:, right, a_rows, :], right_c.at[0]),
        (grad.at[:, right, c_rows, :], right_c.at[1]),
        (grad.at[:, left, a_rows, :], left_c.at[0]),
        (grad.at[:, left, c_rows, :], left_c.at[1]),
        (grad.at[:, right, b_rows, :], right_b),
        (grad.at[:, left, b_rows, :], left_b),
        (grad.at[:, mid, c_rows, :], down_b),
        (grad.at[:, mid, a_rows, :], up_b),
    ]
    pairs.append((grad.at[:, mid, b_rows, :], middle))
    copies = run_copies(pairs, moves)
    keeping.wait()
    for copy in copies:
        copy.wait()


def update_kernel(dims, edge, old, middle, left_c, right_c, left_b, right_b, down_b, up_b,
                  from_left_c, from_right_c, from_up, from_down,
                  part, ext, grad, lc_in, rc_in, u_in, d_in, moves):
    side, nrows, ncols = dims
    t = side // LANES
    last = ncols // LANES
    a_rows, c_rows = pl.ds(0, side), pl.ds(nrows, side)
    b_rows = pl.ds(side, nrows - side)
    left, mid, right = pl.ds(0, t), pl.ds(t, last - t), pl.ds(last, t)
    copies = run_copies([
        (old, ext), (from_left_c, lc_in), (from_right_c, rc_in), (from_up, u_in),
        (from_down, d_in),
        (right_c.at[0], grad.at[:, right, a_rows, :]),
        (right_c.at[1], grad.at[:, right, c_rows, :]),
        (left_c.at[0], grad.at[:, left, a_rows, :]),
        (left_c.at[1], grad.at[:, left, c_rows, :]),
        (right_b, grad.at[:, right, b_rows, :]),
        (left_b, grad.at[:, left, b_rows, :]),
        (down_b, grad.at[:, mid, c_rows, :]),
        (up_b, grad.at[:, mid, a_rows, :]),
        (middle, grad.at[:, mid, b_rows, :]),
    ], moves)
    for copy in copies:
        copy.wait()
    received = {
        (0, 0): lc_in[0], (0, 2): lc_in[1], (1, 0): u_in[...], (1, 2): d_in[...],
        (2, 0): rc_in[0], (2, 2): rc_in[1],
    }
    for i, tiles in enumerate((slice(0, t), slice(t, last), slice(last, last + t))):
        for k, band in enumerate((slice(0, side), slice(side, nrows), slice(nrows, nrows + side))):
            step = grad[:, tiles, band, :]
            if (i, k) in received:
                step = step + received[i, k]
            ext[:, tiles, band, :] = ext[:, tiles, band, :] - 0.25 * step

    @pl.when(edge[0] == 1)
    def _():
        ext[:, :, nrows:, :] = jnp.zeros((2, last + t, side, LANES), F32)

    @pl.when(edge[1] == 1)
    def _():
        ext[:, last:, :, :] = jnp.zeros((2, t, nrows + side, LANES), F32)

    for copy in run_copies([(ext, part)], moves):
        copy.wait()


def share_kernel(received, given):
    summed = received[0]
    for i in range(1, received.shape[0]):
        summed = summed + received[i]
    for i in range(received.shape[0]):
        given[i] = summed


def second_kernel(dims, rate, batch, live, rows, cols, edge, probe, summed,
                  intensity, tables_in, part_in, from_up_c, from_down_c, from_left, from_right,
                  own_out, gprobe_out, right_c, right_ab, down_a, down_b,
                  ext, grad, mats, measured, exit_0, exit_1, wave_0, wave_1, patch_0, patch_1,
                  gprobe, now, sems, moves):
    side, nrows, ncols = dims
    t = side // LANES
    last = ncols // LANES
    copies = run_copies([(part_in, ext), (tables_in, mats)], moves)
    copies += start_slots(1, batch, intensity, measured, sems)
    waves, patches = (wave_0, wave_1), (patch_0, patch_1)
    clear(grad, gprobe, waves, patches)
    now[...] = probe[...] - rate * summed[...]
    for copy in copies:
        copy.wait()
    a_rows, c_rows = slice(0, side), slice(nrows, nrows + side)
    b_rows = slice(side, nrows)
    left, right = slice(0, t), slice(last, last + t)
    for rows_of, corner in ((a_rows, from_up_c), (c_rows, from_down_c)):
        ext[:, left, rows_of, :] -= 0.25 * corner[0]
    ext[:, left, b_rows, :] -= 0.25 * from_left[...]

    @pl.when(edge[1] == 0)
    def _():
        for rows_of, corner in ((a_rows, from_up_c), (c_rows, from_down_c)):
            ext[:, right, rows_of, :] -= 0.25 * corner[1]
        ext[:, right, b_rows, :] -= 0.25 * from_right[...]

    slot_loop(1, side, batch, live, rows, cols, mats, now, ext, grad, gprobe,
              measured, (exit_0, exit_1), waves, patches)
    c_rows, own_rows = pl.ds(nrows, side), pl.ds(0, nrows)
    right = pl.ds(last, t)
    pairs = [
        (gprobe, gprobe_out),
        (grad.at[:, right, c_rows, :], right_c),
        (grad.at[:, pl.ds(t, last - t), c_rows, :], down_b),
        (grad.at[:, pl.ds(0, t), c_rows, :], down_a),
        (grad.at[:, right, own_rows, :], right_ab),
    ]
    copies = run_copies(pairs, moves)
    copies += update_out(ext, grad, own_out, moves, len(pairs))
    for copy in copies:
        copy.wait()


def object_kernel(dims, own, left_ab, above_a, above_b, object_out):
    side, nrows, ncols = dims
    t = side // LANES
    for part in range(2):
        for j in range(ncols // LANES):
            lanes = slice(j * LANES, (j + 1) * LANES)
            if j < t:
                top = own[part, j, 0:side, :] - 0.25 * (
                    left_ab[part, j, 0:side, :] + above_a[part, j])
                low = own[part, j, side:, :] - 0.25 * left_ab[part, j, side:, :]
            else:
                top = own[part, j, 0:side, :] - 0.25 * above_b[part, j - t]
                low = own[part, j, side:, :]
            object_out[part, 0:side, lanes] = top
            object_out[part, side:, lanes] = low


def probe_kernel(rate, probe, sum_one, sum_two, probe_out):
    for part in range(2):
        for j in range(probe.shape[1]):
            probe_out[part, :, j * LANES:(j + 1) * LANES] = (
                probe[part, j] - rate * (sum_one[part, j] + sum_two[part, j]))


def call(kernel, dims, slots, scalars, vectors, plain, received, outs, extra, limit,
         name):
    side, nrows, ncols = dims
    big = (2, (ncols + side) // LANES, nrows + side, LANES)
    smem = pl.BlockSpec(memory_space=pltpu.SMEM)
    vmem = pl.BlockSpec(memory_space=pltpu.VMEM)
    hbm = pl.BlockSpec(memory_space=pltpu.HBM)
    return pl.pallas_call(
        kernel,
        out_shape=[jax.ShapeDtypeStruct(shape, F32) for shape in outs],
        in_specs=([smem] * len(scalars) + [vmem] * len(vectors) + [hbm] * len(plain)
                  + [vmem] * len(received)),
        out_specs=[hbm] * len(outs),
        scratch_shapes=[
            pltpu.VMEM(big, F32),
            pltpu.VMEM(big, F32),
            pltpu.VMEM((2, 2 * side, 2 * side), BF16),
            pltpu.VMEM((slots, side, side), BF16),
        ] + [pltpu.VMEM((2 * side, side), BF16)] * 4
        + [pltpu.VMEM((2, side // LANES, side, LANES), F32)] * 3
        + [pltpu.VMEM(shape, F32) for shape in extra] + [
            pltpu.SemaphoreType.DMA((slots,)),
            pltpu.SemaphoreType.DMA((48,)),
        ],
        compiler_params=pltpu.CompilerParams(vmem_limit_bytes=limit * MIB),
        name=name,
    )(*scalars, *vectors, *plain, *received)


def swap(shares):
    return lax.all_to_all(shares, ("tile", "row"), 0, 0, tiled=True)


def add_up(mine):
    return pl.pallas_call(
        share_kernel, out_shape=jax.ShapeDtypeStruct(mine.shape, F32), name="sum_shares",
        compiler_params=pltpu.CompilerParams(vmem_limit_bytes=4 * MIB),
    )(mine)


def update(dims, edge, plain):
    hbm = pl.BlockSpec(memory_space=pltpu.HBM)
    scratch = [plain[0], plain[0]] + list(plain[8:])
    return pl.pallas_call(
        functools.partial(update_kernel, dims),
        out_shape=jax.ShapeDtypeStruct(plain[0].shape, F32),
        in_specs=[pl.BlockSpec(memory_space=pltpu.SMEM)] + [hbm] * len(plain),
        out_specs=hbm,
        scratch_shapes=[pltpu.VMEM(array.shape, F32) for array in scratch]
        + [pltpu.SemaphoreType.DMA((16,))],
        compiler_params=pltpu.CompilerParams(vmem_limit_bytes=56 * MIB),
        name="update_object",
    )(edge, *plain)


def simple(kernel, shape, name, limit, vectors):
    vmem = pl.BlockSpec(memory_space=pltpu.VMEM)
    return pl.pallas_call(
        kernel,
        out_shape=jax.ShapeDtypeStruct(shape, F32),
        in_specs=[vmem] * len(vectors),
        out_specs=vmem,
        compiler_params=pltpu.CompilerParams(vmem_limit_bytes=limit * MIB),
        name=name,
    )(*vectors)


def local(object_field, probe, intensity, pool_rows, pool_cols, batch, live):
    side = probe.shape[1]
    nrows, ncols = object_field.shape[1:]
    dims = (side, nrows, ncols)
    slots = batch.shape[1]
    t = side // LANES
    total = (ncols + side) // LANES
    probe_rate = 0.125 / math.sqrt(LIVE * lax.axis_size("tile") * lax.axis_size("row"))
    both = jnp.asarray(np.stack(tables(side)))
    current = probe.reshape(2, side, t, LANES).transpose(0, 2, 1, 3)

    first, rest = lax.optimization_barrier((object_field[:, :side, :side], object_field))
    below_a = passed_along(first, "row", -1)
    beside_a = passed_along(first, "tile", -1)
    beside_b = passed_along(rest[:, side:, :side], "tile", -1)
    below_b = passed_along(rest[:, :side, side:], "row", -1)
    corner = passed_along(below_a, "tile", -1)

    edge = jnp.stack([
        (lax.axis_index("row") == lax.axis_size("row") - 1).astype(jnp.int32),
        (lax.axis_index("tile") == lax.axis_size("tile") - 1).astype(jnp.int32)])
    scalars = (batch, live, pool_rows, pool_cols)
    devices = lax.axis_size("tile") * lax.axis_size("row")
    big = (2, total, nrows + side, LANES)
    corners = (2, 2, t, side, LANES)
    strip = (2, ncols // LANES - t, side, LANES)
    side_b = (2, t, nrows - side, LANES)
    middle_b = (2, ncols // LANES - t, nrows - side, LANES)
    old, middle, gprobe, right_c, left_c, right_b, left_b, down_b, up_b = call(
        functools.partial(first_kernel, dims), dims, slots, scalars, (current,),
        (intensity, both, object_field, below_a, below_b, beside_a, beside_b, corner), (),
        [big, middle_b, current.shape, corners, corners, side_b, side_b, strip, strip], [],
        54, "first_iteration")

    from_left_c = passed_along(right_c, "tile", 1)
    from_right_c = passed_along(left_c, "tile", -1)
    from_up_b = passed_along(down_b, "row", 1)
    from_down_b = passed_along(up_b, "row", -1)
    mine = swap(gprobe.reshape(devices, -1, LANES))
    mine, from_left_c, from_right_c = lax.optimization_barrier((mine, from_left_c, from_right_c))
    down_c = jnp.stack([left_c[1] + from_left_c[1], right_c[1] + from_right_c[1]])
    up_c = jnp.stack([left_c[0] + from_left_c[0], right_c[0] + from_right_c[0]])
    from_left_b = passed_along(right_b, "tile", 1)
    from_right_b = passed_along(left_b, "tile", -1)
    down_c, up_c, from_up_b, from_down_b, from_left_b, from_right_b = lax.optimization_barrier(
        (down_c, up_c, from_up_b, from_down_b, from_left_b, from_right_b))
    from_up_c = passed_along(down_c, "row", 1)
    from_down_c = passed_along(up_c, "row", -1)
    mine, from_up_b, from_down_b, _, _ = lax.optimization_barrier(
        (mine, from_up_b, from_down_b, down_c, up_c))
    given = add_up(mine)
    sum_one = swap(given).reshape(current.shape)
    part = update(dims, edge, (old, middle, left_c, right_c, left_b, right_b, down_b, up_b,
                               from_left_c, from_right_c, from_up_b, from_down_b))

    own, gprobe, right_c, right_ab, down_a, down_b = call(
        functools.partial(second_kernel, dims, probe_rate), dims, slots, scalars + (edge,),
        (current, sum_one), (intensity, both, part),
        (from_up_c, from_down_c, from_left_b, from_right_b),
        [(2, ncols // LANES, nrows, LANES), current.shape, (2, t, side, LANES),
         (2, t, nrows, LANES), (2, t, side, LANES), strip],
        [current.shape], 50, "second_iteration")

    from_left_c = passed_along(right_c, "tile", 1)
    above_b = passed_along(down_b, "row", 1)
    mine = swap(gprobe.reshape(devices, -1, LANES))
    down_a = down_a + from_left_c
    above_a = passed_along(down_a, "row", 1)
    mine, above_b, _ = lax.optimization_barrier((mine, above_b, down_a))
    given, right_ab = lax.optimization_barrier((add_up(mine), right_ab))
    left_ab = passed_along(right_ab, "tile", 1)
    sum_two = swap(given).reshape(current.shape)
    object_out = simple(functools.partial(object_kernel, dims), object_field.shape, "last_object",
                        16, (own, left_ab, above_a, above_b))
    sum_two, _ = lax.optimization_barrier((sum_two, object_out))
    probe_out = simple(functools.partial(probe_kernel, probe_rate), probe.shape, "last_probe",
                       8, (current, sum_one, sum_two))
    return (object_out, probe_out)


def solution(mesh):
    placed = (
        P(None, "row", "tile"),
        P(),
        P(("tile", "row"), None, None),
        P(("tile", "row")),
        P(("tile", "row")),
        P(None, ("tile", "row")),
        P(None, ("tile", "row")),
    )
    return jax.shard_map(
        local, mesh=mesh, in_specs=placed, out_specs=(P(None, "row", "tile"), P()), check_vma=False
    )
```

```python
import functools
import math

import jax
import jax.numpy as jnp
import numpy as np
from jax import lax
from jax.experimental import pallas as pl
from jax.experimental.pallas import tpu as pltpu
from jax.sharding import PartitionSpec as P

LIVE = 6
LANES = 128
MIB = 1024 * 1024
F32 = jnp.float32
BF16 = jnp.bfloat16


def passed_along(value, axis, steps):
    count = lax.axis_size(axis)
    first, last = (max(0, -steps), min(count, count - steps))
    return lax.ppermute(value, axis, [(source, source + steps) for source in range(first, last)])


def tables(length):
    counter = np.arange(length, dtype=np.int32)
    product = counter[:, None] * counter[None, :] % length
    angle = product.astype(np.float32) * np.float32(2.0 * math.pi / length)
    factor = np.float32(1.0 / math.sqrt(length))
    cosine = (np.cos(angle) * factor).astype(BF16)
    sine = (np.sin(angle) * factor).astype(BF16)
    forward = np.block([[cosine, sine], [-sine, cosine]])
    backward = np.block([[cosine, -sine], [sine, cosine]])
    return forward, backward


def mul(left, right):
    return jnp.dot(left, right, preferred_element_type=F32)


def start_slots(step, batch, intensity, measured, sems):
    copies = []
    for s in range(batch.shape[1]):
        copies.append(
            pltpu.make_async_copy(intensity.at[batch[step, s]], measured.at[s], sems.at[s]))
    for copy in copies:
        copy.start()
    return copies


def clear(grad, gprobe, waves, patches):
    grad[...] = jnp.zeros_like(grad)
    gprobe[...] = jnp.zeros_like(gprobe)
    waves[1][...] = jnp.zeros_like(waves[1])
    patches[1][...] = jnp.zeros_like(patches[1])


def slot_loop(step, side, batch, live, rows, cols, mats, probe, ext, grad, gprobe,
              measured, exits, waves, patches):
    forward, backward = mats.at[0], mats.at[1]
    lane = lax.broadcasted_iota(jnp.int32, (side, LANES), 1)
    halves = side // LANES
    count = live[step, 0]

    def corner_of(s):
        stored = batch[step, s]
        col = cols[stored]
        return rows[stored], col // LANES, col % LANES

    def window(part, tile, row, shift):
        turn = (LANES - shift) & (LANES - 1)
        turned = [
            pltpu.roll(ext[part, tile + j, pl.ds(row, side), :], turn, 1) for j in range(halves + 1)
        ]
        keep = lane < LANES - shift
        return [jnp.where(keep, turned[j], turned[j + 1]) for j in range(halves)]

    def place(part, tile, row, shift, values):
        turned = [pltpu.roll(v, shift, 1) for v in values]
        keep = lane >= shift
        zero = jnp.zeros((side, LANES), F32)
        for j in range(halves + 1):
            here = turned[j] if j < halves else zero
            prior = turned[j - 1] if j else zero
            at = (part, tile + j, pl.ds(row, side), slice(None))
            grad[at] = grad[at] + jnp.where(keep, here, prior)

    def first_half(s, buffer, alive):
        row, tile, shift = corner_of(s)
        exit_in, wave, patch = exits[buffer], waves[buffer], patches[buffer]
        patch_r = window(0, tile, row, shift)
        patch_i = window(1, tile, row, shift)
        for j in range(halves):
            p_r, p_i = probe[0, j], probe[1, j]
            at = slice(j * LANES, (j + 1) * LANES)
            patch[0, j] = patch_r[j]
            patch[1, j] = patch_i[j]
            exit_in[0:side, at] = (p_r * patch_r[j] - p_i * patch_i[j]).astype(BF16)
            exit_in[side:, at] = (p_r * patch_i[j] + p_i * patch_r[j]).astype(BF16)
        half = mul(forward[...], exit_in[...]).astype(BF16)
        far = mul(jnp.concatenate([half[:side], half[side:]], axis=1), backward[...])
        far_r, far_i = far[:, :side], far[:, side:]
        excess = far_r * far_r + far_i * far_i - measured[s].astype(F32)
        if alive is not None:
            excess = excess * alive
        wave[0:side, :] = (excess * far_r).astype(BF16)
        wave[side:, :] = (excess * far_i).astype(BF16)

    def second_half(s, buffer):
        row, tile, shift = corner_of(s)
        wave, patch = waves[buffer], patches[buffer]
        mid = mul(backward[...], wave[...]).astype(BF16)
        back = mul(jnp.concatenate([mid[:side], mid[side:]], axis=1), forward[...])
        object_r, object_i = [], []
        for j in range(halves):
            p_r, p_i = probe[0, j], probe[1, j]
            o_r, o_i = patch[0, j], patch[1, j]
            b_r = back[:, j * LANES:(j + 1) * LANES]
            b_i = back[:, side + j * LANES:side + (j + 1) * LANES]
            object_r.append(p_r * b_r + p_i * b_i)
            object_i.append(p_r * b_i - p_i * b_r)
            gprobe[0, j] += o_r * b_r + o_i * b_i
            gprobe[1, j] += o_r * b_i - o_i * b_r
        place(0, tile, row, shift, object_r)
        place(1, tile, row, shift, object_i)

    def two_slots(k, carry):
        even = 2 * k
        odd = jnp.minimum(even + 1, batch.shape[1] - 1)
        alive = jnp.where(even + 1 < count, 1.0, 0.0).astype(F32)
        second_half(jnp.maximum(even - 1, 0), 1)
        first_half(even, 0, None)
        second_half(even, 0)
        first_half(odd, 1, alive)
        return carry

    pairs = (count + 1) // 2
    lax.fori_loop(0, pairs, two_slots, 0)
    second_half(jnp.minimum(2 * pairs - 1, batch.shape[1] - 1), 1)


def tiled_copies(field, part_rows, part_cols, ext, row0, col0):
    pairs = []
    for part in range(2):
        for j in range(part_cols // LANES):
            pairs.append((
                field.at[part, :, pl.ds(j * LANES, LANES)],
                ext.at[part, col0 // LANES + j, pl.ds(row0, part_rows), :],
            ))
    return pairs


def run_copies(pairs, sems, base=0):
    copies = [pltpu.make_async_copy(src, dst, sems.at[base + i]) for i, (src, dst) in enumerate(pairs)]
    for copy in copies:
        copy.start()
    return copies


def update_out(ext, grad, target, sems, base):
    parts, tiles, rows = target.shape[:3]
    copies = []
    for part in range(parts):
        for j in range(tiles):
            ext[part, j, 0:rows, :] -= 0.25 * grad[part, j, 0:rows, :]
            copies += run_copies([(ext.at[part, j, pl.ds(0, rows), :], target.at[part, j])],
                                 sems, base + len(copies))
    return copies


def first_kernel(dims, batch, live, rows, cols, probe, intensity, tables_in,
                 field, below_a, below_b, beside_a, beside_b, corner,
                 old, middle, gprobe_out, right_c, left_c, right_b, left_b, down_b, up_b,
                 ext, grad, mats, measured, exit_0, exit_1, wave_0, wave_1, patch_0, patch_1,
                 gprobe, sems, moves):
    side, nrows, ncols = dims
    pairs = tiled_copies(field, nrows, ncols, ext, 0, 0)
    pairs += tiled_copies(below_a, side, side, ext, nrows, 0)
    pairs += tiled_copies(below_b, side, ncols - side, ext, nrows, side)
    pairs += tiled_copies(beside_a, side, side, ext, 0, ncols)
    pairs += tiled_copies(beside_b, nrows - side, side, ext, side, ncols)
    pairs += tiled_copies(corner, side, side, ext, nrows, ncols)
    copies = run_copies(pairs + [(tables_in, mats)], moves)
    copies += start_slots(0, batch, intensity, measured, sems)
    waves, patches = (wave_0, wave_1), (patch_0, patch_1)
    clear(grad, gprobe, waves, patches)
    for copy in copies:
        copy.wait()
    keeping = pltpu.make_async_copy(ext, old, moves.at[len(pairs) + 1])
    keeping.start()
    slot_loop(0, side, batch, live, rows, cols, mats, probe, ext, grad, gprobe,
              measured, (exit_0, exit_1), waves, patches)
    t = side // LANES
    last = ncols // LANES
    a_rows, c_rows = pl.ds(0, side), pl.ds(nrows, side)
    b_rows = pl.ds(side, nrows - side)
    left, mid, right = pl.ds(0, t), pl.ds(t, last - t), pl.ds(last, t)
    pairs = [
        (gprobe, gprobe_out),
        (grad.at[:, right, a_rows, :], right_c.at[0]),
        (grad.at[:, right, c_rows, :], right_c.at[1]),
        (grad.at[:, left, a_rows, :], left_c.at[0]),
        (grad.at[:, left, c_rows, :], left_c.at[1]),
        (grad.at[:, right, b_rows, :], right_b),
        (grad.at[:, left, b_rows, :], left_b),
        (grad.at[:, mid, c_rows, :], down_b),
        (grad.at[:, mid, a_rows, :], up_b),
    ]
    pairs.append((grad.at[:, mid, b_rows, :], middle))
    copies = run_copies(pairs, moves)
    keeping.wait()
    for copy in copies:
        copy.wait()


def update_kernel(dims, edge, old, middle, left_c, right_c, left_b, right_b, down_b, up_b,
                  from_left_c, from_right_c, from_up, from_down,
                  part, ext, grad, lc_in, rc_in, u_in, d_in, moves):
    side, nrows, ncols = dims
    t = side // LANES
    last = ncols // LANES
    a_rows, c_rows = pl.ds(0, side), pl.ds(nrows, side)
    b_rows = pl.ds(side, nrows - side)
    left, mid, right = pl.ds(0, t), pl.ds(t, last - t), pl.ds(last, t)
    copies = run_copies([
        (old, ext), (from_left_c, lc_in), (from_right_c, rc_in), (from_up, u_in),
        (from_down, d_in),
        (right_c.at[0], grad.at[:, right, a_rows, :]),
        (right_c.at[1], grad.at[:, right, c_rows, :]),
        (left_c.at[0], grad.at[:, left, a_rows, :]),
        (left_c.at[1], grad.at[:, left, c_rows, :]),
        (right_b, grad.at[:, right, b_rows, :]),
        (left_b, grad.at[:, left, b_rows, :]),
        (down_b, grad.at[:, mid, c_rows, :]),
        (up_b, grad.at[:, mid, a_rows, :]),
        (middle, grad.at[:, mid, b_rows, :]),
    ], moves)
    for copy in copies:
        copy.wait()
    received = {
        (0, 0): lc_in[0], (0, 2): lc_in[1], (1, 0): u_in[...], (1, 2): d_in[...],
        (2, 0): rc_in[0], (2, 2): rc_in[1],
    }
    for i, tiles in enumerate((slice(0, t), slice(t, last), slice(last, last + t))):
        for k, band in enumerate((slice(0, side), slice(side, nrows), slice(nrows, nrows + side))):
            step = grad[:, tiles, band, :]
            if (i, k) in received:
                step = step + received[i, k]
            ext[:, tiles, band, :] = ext[:, tiles, band, :] - 0.25 * step

    @pl.when(edge[0] == 1)
    def _():
        ext[:, :, nrows:, :] = jnp.zeros((2, last + t, side, LANES), F32)

    @pl.when(edge[1] == 1)
    def _():
        ext[:, last:, :, :] = jnp.zeros((2, t, nrows + side, LANES), F32)

    for copy in run_copies([(ext, part)], moves):
        copy.wait()


def share_kernel(received, given):
    summed = received[0]
    for i in range(1, received.shape[0]):
        summed = summed + received[i]
    for i in range(received.shape[0]):
        given[i] = summed


def second_kernel(dims, rate, batch, live, rows, cols, edge, probe, summed,
                  intensity, tables_in, part_in, from_up_c, from_down_c, from_left, from_right,
                  own_out, gprobe_out, right_c, right_ab, down_a, down_b,
                  ext, grad, mats, measured, exit_0, exit_1, wave_0, wave_1, patch_0, patch_1,
                  gprobe, now, sems, moves):
    side, nrows, ncols = dims
    t = side // LANES
    last = ncols // LANES
    copies = run_copies([(part_in, ext), (tables_in, mats)], moves)
    copies += start_slots(1, batch, intensity, measured, sems)
    waves, patches = (wave_0, wave_1), (patch_0, patch_1)
    clear(grad, gprobe, waves, patches)
    now[...] = probe[...] - rate * summed[...]
    for copy in copies:
        copy.wait()
    a_rows, c_rows = slice(0, side), slice(nrows, nrows + side)
    b_rows = slice(side, nrows)
    left, right = slice(0, t), slice(last, last + t)
    for rows_of, corner in ((a_rows, from_up_c), (c_rows, from_down_c)):
        ext[:, left, rows_of, :] -= 0.25 * corner[0]
    ext[:, left, b_rows, :] -= 0.25 * from_left[...]

    @pl.when(edge[1] == 0)
    def _():
        for rows_of, corner in ((a_rows, from_up_c), (c_rows, from_down_c)):
            ext[:, right, rows_of, :] -= 0.25 * corner[1]
        ext[:, right, b_rows, :] -= 0.25 * from_right[...]

    slot_loop(1, side, batch, live, rows, cols, mats, now, ext, grad, gprobe,
              measured, (exit_0, exit_1), waves, patches)
    c_rows, own_rows = pl.ds(nrows, side), pl.ds(0, nrows)
    right = pl.ds(last, t)
    pairs = [
        (gprobe, gprobe_out),
        (grad.at[:, right, c_rows, :], right_c),
        (grad.at[:, pl.ds(t, last - t), c_rows, :], down_b),
        (grad.at[:, pl.ds(0, t), c_rows, :], down_a),
        (grad.at[:, right, own_rows, :], right_ab),
    ]
    copies = run_copies(pairs, moves)
    copies += update_out(ext, grad, own_out, moves, len(pairs))
    for copy in copies:
        copy.wait()


def object_kernel(dims, own, left_ab, above_a, above_b, object_out):
    side, nrows, ncols = dims
    t = side // LANES
    for part in range(2):
        for j in range(ncols // LANES):
            lanes = slice(j * LANES, (j + 1) * LANES)
            if j < t:
                top = own[part, j, 0:side, :] - 0.25 * (
                    left_ab[part, j, 0:side, :] + above_a[part, j])
                low = own[part, j, side:, :] - 0.25 * left_ab[part, j, side:, :]
            else:
                top = own[part, j, 0:side, :] - 0.25 * above_b[part, j - t]
                low = own[part, j, side:, :]
            object_out[part, 0:side, lanes] = top
            object_out[part, side:, lanes] = low


def probe_kernel(rate, probe, sum_one, sum_two, probe_out):
    for part in range(2):
        for j in range(probe.shape[1]):
            probe_out[part, :, j * LANES:(j + 1) * LANES] = (
                probe[part, j] - rate * (sum_one[part, j] + sum_two[part, j]))


def call(kernel, dims, slots, scalars, vectors, plain, received, outs, extra, limit,
         name):
    side, nrows, ncols = dims
    big = (2, (ncols + side) // LANES, nrows + side, LANES)
    smem = pl.BlockSpec(memory_space=pltpu.SMEM)
    vmem = pl.BlockSpec(memory_space=pltpu.VMEM)
    hbm = pl.BlockSpec(memory_space=pltpu.HBM)
    return pl.pallas_call(
        kernel,
        out_shape=[jax.ShapeDtypeStruct(shape, F32) for shape in outs],
        in_specs=([smem] * len(scalars) + [vmem] * len(vectors) + [hbm] * len(plain)
                  + [vmem] * len(received)),
        out_specs=[hbm] * len(outs),
        scratch_shapes=[
            pltpu.VMEM(big, F32),
            pltpu.VMEM(big, F32),
            pltpu.VMEM((2, 2 * side, 2 * side), BF16),
            pltpu.VMEM((slots, side, side), BF16),
        ] + [pltpu.VMEM((2 * side, side), BF16)] * 4
        + [pltpu.VMEM((2, side // LANES, side, LANES), F32)] * 3
        + [pltpu.VMEM(shape, F32) for shape in extra] + [
            pltpu.SemaphoreType.DMA((slots,)),
            pltpu.SemaphoreType.DMA((48,)),
        ],
        compiler_params=pltpu.CompilerParams(vmem_limit_bytes=limit * MIB),
        name=name,
    )(*scalars, *vectors, *plain, *received)


def swap(shares):
    return lax.all_to_all(shares, ("tile", "row"), 0, 0, tiled=True)


def add_up(mine):
    return pl.pallas_call(
        share_kernel, out_shape=jax.ShapeDtypeStruct(mine.shape, F32), name="sum_shares",
        compiler_params=pltpu.CompilerParams(vmem_limit_bytes=4 * MIB),
    )(mine)


def update(dims, edge, plain):
    hbm = pl.BlockSpec(memory_space=pltpu.HBM)
    scratch = [plain[0], plain[0]] + list(plain[8:])
    return pl.pallas_call(
        functools.partial(update_kernel, dims),
        out_shape=jax.ShapeDtypeStruct(plain[0].shape, F32),
        in_specs=[pl.BlockSpec(memory_space=pltpu.SMEM)] + [hbm] * len(plain),
        out_specs=hbm,
        scratch_shapes=[pltpu.VMEM(array.shape, F32) for array in scratch]
        + [pltpu.SemaphoreType.DMA((16,))],
        compiler_params=pltpu.CompilerParams(vmem_limit_bytes=56 * MIB),
        name="update_object",
    )(edge, *plain)


def simple(kernel, shape, name, limit, vectors):
    vmem = pl.BlockSpec(memory_space=pltpu.VMEM)
    return pl.pallas_call(
        kernel,
        out_shape=jax.ShapeDtypeStruct(shape, F32),
        in_specs=[vmem] * len(vectors),
        out_specs=vmem,
        compiler_params=pltpu.CompilerParams(vmem_limit_bytes=limit * MIB),
        name=name,
    )(*vectors)


def local(object_field, probe, intensity, pool_rows, pool_cols, batch, live):
    side = probe.shape[1]
    nrows, ncols = object_field.shape[1:]
    dims = (side, nrows, ncols)
    slots = batch.shape[1]
    t = side // LANES
    total = (ncols + side) // LANES
    probe_rate = 0.125 / math.sqrt(LIVE * lax.axis_size("tile") * lax.axis_size("row"))
    both = jnp.asarray(np.stack(tables(side)))
    current = probe.reshape(2, side, t, LANES).transpose(0, 2, 1, 3)

    first, rest = lax.optimization_barrier((object_field[:, :side, :side], object_field))
    below_a = passed_along(first, "row", -1)
    beside_a = passed_along(first, "tile", -1)
    beside_b = passed_along(rest[:, side:, :side], "tile", -1)
    below_b = passed_along(rest[:, :side, side:], "row", -1)
    corner = passed_along(below_a, "tile", -1)

    edge = jnp.stack([
        (lax.axis_index("row") == lax.axis_size("row") - 1).astype(jnp.int32),
        (lax.axis_index("tile") == lax.axis_size("tile") - 1).astype(jnp.int32)])
    scalars = (batch, live, pool_rows, pool_cols)
    devices = lax.axis_size("tile") * lax.axis_size("row")
    big = (2, total, nrows + side, LANES)
    corners = (2, 2, t, side, LANES)
    strip = (2, ncols // LANES - t, side, LANES)
    side_b = (2, t, nrows - side, LANES)
    middle_b = (2, ncols // LANES - t, nrows - side, LANES)
    old, middle, gprobe, right_c, left_c, right_b, left_b, down_b, up_b = call(
        functools.partial(first_kernel, dims), dims, slots, scalars, (current,),
        (intensity, both, object_field, below_a, below_b, beside_a, beside_b, corner), (),
        [big, middle_b, current.shape, corners, corners, side_b, side_b, strip, strip], [],
        54, "first_iteration")

    from_left_c = passed_along(right_c, "tile", 1)
    from_right_c = passed_along(left_c, "tile", -1)
    from_up_b = passed_along(down_b, "row", 1)
    from_down_b = passed_along(up_b, "row", -1)
    mine = swap(gprobe.reshape(devices, -1, LANES))
    mine, from_left_c, from_right_c = lax.optimization_barrier((mine, from_left_c, from_right_c))
    down_c = jnp.stack([left_c[1] + from_left_c[1], right_c[1] + from_right_c[1]])
    up_c = jnp.stack([left_c[0] + from_left_c[0], right_c[0] + from_right_c[0]])
    from_up_c = passed_along(down_c, "row", 1)
    from_down_c = passed_along(up_c, "row", -1)
    mine, from_up_b, from_down_b, _, _ = lax.optimization_barrier(
        (mine, from_up_b, from_down_b, down_c, up_c))
    given, right_b, left_b = lax.optimization_barrier((add_up(mine), right_b, left_b))
    from_left_b = passed_along(right_b, "tile", 1)
    from_right_b = passed_along(left_b, "tile", -1)
    sum_one = swap(given).reshape(current.shape)
    part = update(dims, edge, (old, middle, left_c, right_c, left_b, right_b, down_b, up_b,
                               from_left_c, from_right_c, from_up_b, from_down_b))

    own, gprobe, right_c, right_ab, down_a, down_b = call(
        functools.partial(second_kernel, dims, probe_rate), dims, slots, scalars + (edge,),
        (current, sum_one), (intensity, both, part),
        (from_up_c, from_down_c, from_left_b, from_right_b),
        [(2, ncols // LANES, nrows, LANES), current.shape, (2, t, side, LANES),
         (2, t, nrows, LANES), (2, t, side, LANES), strip],
        [current.shape], 50, "second_iteration")

    from_left_c = passed_along(right_c, "tile", 1)
    above_b = passed_along(down_b, "row", 1)
    mine = swap(gprobe.reshape(devices, -1, LANES))
    down_a = down_a + from_left_c
    above_a = passed_along(down_a, "row", 1)
    mine, above_b, _ = lax.optimization_barrier((mine, above_b, down_a))
    given, right_ab = lax.optimization_barrier((add_up(mine), right_ab))
    left_ab = passed_along(right_ab, "tile", 1)
    sum_two = swap(given).reshape(current.shape)
    object_out = simple(functools.partial(object_kernel, dims), object_field.shape, "last_object",
                        16, (own, left_ab, above_a, above_b))
    sum_two, _ = lax.optimization_barrier((sum_two, object_out))
    probe_out = simple(functools.partial(probe_kernel, probe_rate), probe.shape, "last_probe",
                       8, (current, sum_one, sum_two))
    return (object_out, probe_out)


def solution(mesh):
    placed = (
        P(None, "row", "tile"),
        P(),
        P(("tile", "row"), None, None),
        P(("tile", "row")),
        P(("tile", "row")),
        P(None, ("tile", "row")),
        P(None, ("tile", "row")),
    )
    return jax.shard_map(
        local, mesh=mesh, in_specs=placed, out_specs=(P(None, "row", "tile"), P()), check_vma=False
    )
```

```python
import functools
import math

import jax
import jax.numpy as jnp
import numpy as np
from jax import lax
from jax.experimental import pallas as pl
from jax.experimental.pallas import tpu as pltpu
from jax.sharding import PartitionSpec as P

LIVE = 6
LANES = 128
MIB = 1024 * 1024
F32 = jnp.float32
BF16 = jnp.bfloat16


def passed_along(value, axis, steps):
    count = lax.axis_size(axis)
    first, last = (max(0, -steps), min(count, count - steps))
    return lax.ppermute(value, axis, [(source, source + steps) for source in range(first, last)])


def tables(length):
    counter = np.arange(length, dtype=np.int32)
    product = counter[:, None] * counter[None, :] % length
    angle = product.astype(np.float32) * np.float32(2.0 * math.pi / length)
    factor = np.float32(1.0 / math.sqrt(length))
    cosine = (np.cos(angle) * factor).astype(BF16)
    sine = (np.sin(angle) * factor).astype(BF16)
    forward = np.block([[cosine, sine], [-sine, cosine]])
    backward = np.block([[cosine, -sine], [sine, cosine]])
    return forward, backward


def mul(left, right):
    return jnp.dot(left, right, preferred_element_type=F32)


def start_slots(step, batch, intensity, measured, sems):
    copies = []
    for s in range(batch.shape[1]):
        copies.append(
            pltpu.make_async_copy(intensity.at[batch[step, s]], measured.at[s], sems.at[s]))
    for copy in copies:
        copy.start()
    return copies


def clear(grad, gprobe, waves, patches):
    grad[...] = jnp.zeros_like(grad)
    gprobe[...] = jnp.zeros_like(gprobe)
    waves[1][...] = jnp.zeros_like(waves[1])
    patches[1][...] = jnp.zeros_like(patches[1])


def slot_loop(step, side, batch, live, rows, cols, mats, probe, ext, grad, gprobe,
              measured, exits, waves, patches):
    forward, backward = mats.at[0], mats.at[1]
    lane = lax.broadcasted_iota(jnp.int32, (side, LANES), 1)
    halves = side // LANES
    count = live[step, 0]

    def corner_of(s):
        stored = batch[step, s]
        col = cols[stored]
        return rows[stored], col // LANES, col % LANES

    def window(part, tile, row, shift):
        turn = (LANES - shift) & (LANES - 1)
        turned = [
            pltpu.roll(ext[part, tile + j, pl.ds(row, side), :], turn, 1) for j in range(halves + 1)
        ]
        keep = lane < LANES - shift
        return [jnp.where(keep, turned[j], turned[j + 1]) for j in range(halves)]

    def place(part, tile, row, shift, values):
        turned = [pltpu.roll(v, shift, 1) for v in values]
        keep = lane >= shift
        zero = jnp.zeros((side, LANES), F32)
        for j in range(halves + 1):
            here = turned[j] if j < halves else zero
            prior = turned[j - 1] if j else zero
            at = (part, tile + j, pl.ds(row, side), slice(None))
            grad[at] = grad[at] + jnp.where(keep, here, prior)

    def first_half(s, buffer, alive):
        row, tile, shift = corner_of(s)
        exit_in, wave, patch = exits[buffer], waves[buffer], patches[buffer]
        patch_r = window(0, tile, row, shift)
        patch_i = window(1, tile, row, shift)
        for j in range(halves):
            p_r, p_i = probe[0, j], probe[1, j]
            at = slice(j * LANES, (j + 1) * LANES)
            patch[0, j] = patch_r[j]
            patch[1, j] = patch_i[j]
            exit_in[0:side, at] = (p_r * patch_r[j] - p_i * patch_i[j]).astype(BF16)
            exit_in[side:, at] = (p_r * patch_i[j] + p_i * patch_r[j]).astype(BF16)
        half = mul(forward[...], exit_in[...]).astype(BF16)
        far = mul(jnp.concatenate([half[:side], half[side:]], axis=1), backward[...])
        far_r, far_i = far[:, :side], far[:, side:]
        excess = far_r * far_r + far_i * far_i - measured[s].astype(F32)
        if alive is not None:
            excess = excess * alive
        wave[0:side, :] = (excess * far_r).astype(BF16)
        wave[side:, :] = (excess * far_i).astype(BF16)

    def second_half(s, buffer):
        row, tile, shift = corner_of(s)
        wave, patch = waves[buffer], patches[buffer]
        mid = mul(backward[...], wave[...]).astype(BF16)
        back = mul(jnp.concatenate([mid[:side], mid[side:]], axis=1), forward[...])
        object_r, object_i = [], []
        for j in range(halves):
            p_r, p_i = probe[0, j], probe[1, j]
            o_r, o_i = patch[0, j], patch[1, j]
            b_r = back[:, j * LANES:(j + 1) * LANES]
            b_i = back[:, side + j * LANES:side + (j + 1) * LANES]
            object_r.append(p_r * b_r + p_i * b_i)
            object_i.append(p_r * b_i - p_i * b_r)
            gprobe[0, j] += o_r * b_r + o_i * b_i
            gprobe[1, j] += o_r * b_i - o_i * b_r
        place(0, tile, row, shift, object_r)
        place(1, tile, row, shift, object_i)

    def two_slots(k, carry):
        even = 2 * k
        odd = jnp.minimum(even + 1, batch.shape[1] - 1)
        alive = jnp.where(even + 1 < count, 1.0, 0.0).astype(F32)
        second_half(jnp.maximum(even - 1, 0), 1)
        first_half(even, 0, None)
        second_half(even, 0)
        first_half(odd, 1, alive)
        return carry

    pairs = (count + 1) // 2
    lax.fori_loop(0, pairs, two_slots, 0)
    second_half(jnp.minimum(2 * pairs - 1, batch.shape[1] - 1), 1)


def tiled_copies(field, part_rows, part_cols, ext, row0, col0):
    pairs = []
    for part in range(2):
        for j in range(part_cols // LANES):
            pairs.append((
                field.at[part, :, pl.ds(j * LANES, LANES)],
                ext.at[part, col0 // LANES + j, pl.ds(row0, part_rows), :],
            ))
    return pairs


def run_copies(pairs, sems, base=0):
    copies = [pltpu.make_async_copy(src, dst, sems.at[base + i]) for i, (src, dst) in enumerate(pairs)]
    for copy in copies:
        copy.start()
    return copies


def update_out(ext, grad, target, sems, base):
    parts, tiles, rows = target.shape[:3]
    copies = []
    for part in range(parts):
        for j in range(tiles):
            ext[part, j, 0:rows, :] -= 0.25 * grad[part, j, 0:rows, :]
            copies += run_copies([(ext.at[part, j, pl.ds(0, rows), :], target.at[part, j])],
                                 sems, base + len(copies))
    return copies


def first_kernel(dims, batch, live, rows, cols, probe, intensity, tables_in,
                 field, below_a, below_b, beside_a, beside_b, corner,
                 old, middle, gprobe_out, right_c, left_c, right_b, left_b, down_b, up_b,
                 ext, grad, mats, measured, exit_0, exit_1, wave_0, wave_1, patch_0, patch_1,
                 gprobe, sems, moves):
    side, nrows, ncols = dims
    pairs = tiled_copies(field, nrows, ncols, ext, 0, 0)
    pairs += tiled_copies(below_a, side, side, ext, nrows, 0)
    pairs += tiled_copies(below_b, side, ncols - side, ext, nrows, side)
    pairs += tiled_copies(beside_a, side, side, ext, 0, ncols)
    pairs += tiled_copies(beside_b, nrows - side, side, ext, side, ncols)
    pairs += tiled_copies(corner, side, side, ext, nrows, ncols)
    copies = run_copies(pairs + [(tables_in, mats)], moves)
    copies += start_slots(0, batch, intensity, measured, sems)
    waves, patches = (wave_0, wave_1), (patch_0, patch_1)
    clear(grad, gprobe, waves, patches)
    for copy in copies:
        copy.wait()
    keeping = pltpu.make_async_copy(ext, old, moves.at[len(pairs) + 1])
    keeping.start()
    slot_loop(0, side, batch, live, rows, cols, mats, probe, ext, grad, gprobe,
              measured, (exit_0, exit_1), waves, patches)
    t = side // LANES
    last = ncols // LANES
    a_rows, c_rows = pl.ds(0, side), pl.ds(nrows, side)
    b_rows = pl.ds(side, nrows - side)
    left, mid, right = pl.ds(0, t), pl.ds(t, last - t), pl.ds(last, t)
    pairs = [
        (gprobe, gprobe_out),
        (grad.at[:, right, a_rows, :], right_c.at[0]),
        (grad.at[:, right, c_rows, :], right_c.at[1]),
        (grad.at[:, left, a_rows, :], left_c.at[0]),
        (grad.at[:, left, c_rows, :], left_c.at[1]),
        (grad.at[:, right, b_rows, :], right_b),
        (grad.at[:, left, b_rows, :], left_b),
        (grad.at[:, mid, c_rows, :], down_b),
        (grad.at[:, mid, a_rows, :], up_b),
    ]
    pairs.append((grad.at[:, mid, b_rows, :], middle))
    copies = run_copies(pairs, moves)
    keeping.wait()
    for copy in copies:
        copy.wait()


def update_kernel(dims, edge, old, middle, left_c, right_c, left_b, right_b, down_b, up_b,
                  from_left_c, from_right_c, from_up, from_down,
                  part, ext, grad, lc_in, rc_in, u_in, d_in, moves):
    side, nrows, ncols = dims
    t = side // LANES
    last = ncols // LANES
    a_rows, c_rows = pl.ds(0, side), pl.ds(nrows, side)
    b_rows = pl.ds(side, nrows - side)
    left, mid, right = pl.ds(0, t), pl.ds(t, last - t), pl.ds(last, t)
    copies = run_copies([
        (old, ext), (from_left_c, lc_in), (from_right_c, rc_in), (from_up, u_in),
        (from_down, d_in),
        (right_c.at[0], grad.at[:, right, a_rows, :]),
        (right_c.at[1], grad.at[:, right, c_rows, :]),
        (left_c.at[0], grad.at[:, left, a_rows, :]),
        (left_c.at[1], grad.at[:, left, c_rows, :]),
        (right_b, grad.at[:, right, b_rows, :]),
        (left_b, grad.at[:, left, b_rows, :]),
        (down_b, grad.at[:, mid, c_rows, :]),
        (up_b, grad.at[:, mid, a_rows, :]),
        (middle, grad.at[:, mid, b_rows, :]),
    ], moves)
    for copy in copies:
        copy.wait()
    received = {
        (0, 0): lc_in[0], (0, 2): lc_in[1], (1, 0): u_in[...], (1, 2): d_in[...],
        (2, 0): rc_in[0], (2, 2): rc_in[1],
    }
    for i, tiles in enumerate((slice(0, t), slice(t, last), slice(last, last + t))):
        for k, band in enumerate((slice(0, side), slice(side, nrows), slice(nrows, nrows + side))):
            step = grad[:, tiles, band, :]
            if (i, k) in received:
                step = step + received[i, k]
            ext[:, tiles, band, :] = ext[:, tiles, band, :] - 0.25 * step

    @pl.when(edge[0] == 1)
    def _():
        ext[:, :, nrows:, :] = jnp.zeros((2, last + t, side, LANES), F32)

    @pl.when(edge[1] == 1)
    def _():
        ext[:, last:, :, :] = jnp.zeros((2, t, nrows + side, LANES), F32)

    for copy in run_copies([(ext, part)], moves):
        copy.wait()


def share_kernel(received, given):
    summed = received[0]
    for i in range(1, received.shape[0]):
        summed = summed + received[i]
    for i in range(received.shape[0]):
        given[i] = summed


def second_kernel(dims, rate, batch, live, rows, cols, edge, probe, summed,
                  intensity, tables_in, part_in, from_up_c, from_down_c, from_left, from_right,
                  own_out, gprobe_out, right_c, right_ab, down_a, down_b,
                  ext, grad, mats, measured, exit_0, exit_1, wave_0, wave_1, patch_0, patch_1,
                  gprobe, now, sems, moves):
    side, nrows, ncols = dims
    t = side // LANES
    last = ncols // LANES
    copies = run_copies([(part_in, ext), (tables_in, mats)], moves)
    copies += start_slots(1, batch, intensity, measured, sems)
    waves, patches = (wave_0, wave_1), (patch_0, patch_1)
    clear(grad, gprobe, waves, patches)
    now[...] = probe[...] - rate * summed[...]
    for copy in copies:
        copy.wait()
    a_rows, c_rows = slice(0, side), slice(nrows, nrows + side)
    b_rows = slice(side, nrows)
    left, right = slice(0, t), slice(last, last + t)
    for rows_of, corner in ((a_rows, from_up_c), (c_rows, from_down_c)):
        ext[:, left, rows_of, :] -= 0.25 * corner[0]
    ext[:, left, b_rows, :] -= 0.25 * from_left[...]

    @pl.when(edge[1] == 0)
    def _():
        for rows_of, corner in ((a_rows, from_up_c), (c_rows, from_down_c)):
            ext[:, right, rows_of, :] -= 0.25 * corner[1]
        ext[:, right, b_rows, :] -= 0.25 * from_right[...]

    slot_loop(1, side, batch, live, rows, cols, mats, now, ext, grad, gprobe,
              measured, (exit_0, exit_1), waves, patches)
    c_rows, own_rows = pl.ds(nrows, side), pl.ds(0, nrows)
    right = pl.ds(last, t)
    pairs = [
        (gprobe, gprobe_out),
        (grad.at[:, right, c_rows, :], right_c),
        (grad.at[:, pl.ds(t, last - t), c_rows, :], down_b),
        (grad.at[:, pl.ds(0, t), c_rows, :], down_a),
        (grad.at[:, right, own_rows, :], right_ab),
    ]
    copies = run_copies(pairs, moves)
    copies += update_out(ext, grad, own_out, moves, len(pairs))
    for copy in copies:
        copy.wait()


def object_kernel(dims, own, left_ab, above_a, above_b, object_out):
    side, nrows, ncols = dims
    t = side // LANES
    for part in range(2):
        for j in range(ncols // LANES):
            lanes = slice(j * LANES, (j + 1) * LANES)
            if j < t:
                top = own[part, j, 0:side, :] - 0.25 * (
                    left_ab[part, j, 0:side, :] + above_a[part, j])
                low = own[part, j, side:, :] - 0.25 * left_ab[part, j, side:, :]
            else:
                top = own[part, j, 0:side, :] - 0.25 * above_b[part, j - t]
                low = own[part, j, side:, :]
            object_out[part, 0:side, lanes] = top
            object_out[part, side:, lanes] = low


def probe_kernel(rate, probe, sum_one, sum_two, probe_out):
    for part in range(2):
        for j in range(probe.shape[1]):
            probe_out[part, :, j * LANES:(j + 1) * LANES] = (
                probe[part, j] - rate * (sum_one[part, j] + sum_two[part, j]))


def call(kernel, dims, slots, scalars, vectors, plain, received, outs, extra, limit,
         name):
    side, nrows, ncols = dims
    big = (2, (ncols + side) // LANES, nrows + side, LANES)
    smem = pl.BlockSpec(memory_space=pltpu.SMEM)
    vmem = pl.BlockSpec(memory_space=pltpu.VMEM)
    hbm = pl.BlockSpec(memory_space=pltpu.HBM)
    return pl.pallas_call(
        kernel,
        out_shape=[jax.ShapeDtypeStruct(shape, F32) for shape in outs],
        in_specs=([smem] * len(scalars) + [vmem] * len(vectors) + [hbm] * len(plain)
                  + [vmem] * len(received)),
        out_specs=[hbm] * len(outs),
        scratch_shapes=[
            pltpu.VMEM(big, F32),
            pltpu.VMEM(big, F32),
            pltpu.VMEM((2, 2 * side, 2 * side), BF16),
            pltpu.VMEM((slots, side, side), BF16),
        ] + [pltpu.VMEM((2 * side, side), BF16)] * 4
        + [pltpu.VMEM((2, side // LANES, side, LANES), F32)] * 3
        + [pltpu.VMEM(shape, F32) for shape in extra] + [
            pltpu.SemaphoreType.DMA((slots,)),
            pltpu.SemaphoreType.DMA((48,)),
        ],
        compiler_params=pltpu.CompilerParams(vmem_limit_bytes=limit * MIB),
        name=name,
    )(*scalars, *vectors, *plain, *received)


def swap(shares):
    return lax.all_to_all(shares, ("tile", "row"), 0, 0, tiled=True)


def add_up(mine):
    return pl.pallas_call(
        share_kernel, out_shape=jax.ShapeDtypeStruct(mine.shape, F32), name="sum_shares",
        compiler_params=pltpu.CompilerParams(vmem_limit_bytes=4 * MIB),
    )(mine)


def update(dims, edge, plain):
    hbm = pl.BlockSpec(memory_space=pltpu.HBM)
    scratch = [plain[0], plain[0]] + list(plain[8:])
    return pl.pallas_call(
        functools.partial(update_kernel, dims),
        out_shape=jax.ShapeDtypeStruct(plain[0].shape, F32),
        in_specs=[pl.BlockSpec(memory_space=pltpu.SMEM)] + [hbm] * len(plain),
        out_specs=hbm,
        scratch_shapes=[pltpu.VMEM(array.shape, F32) for array in scratch]
        + [pltpu.SemaphoreType.DMA((16,))],
        compiler_params=pltpu.CompilerParams(vmem_limit_bytes=56 * MIB),
        name="update_object",
    )(edge, *plain)


def simple(kernel, shape, name, limit, vectors):
    vmem = pl.BlockSpec(memory_space=pltpu.VMEM)
    return pl.pallas_call(
        kernel,
        out_shape=jax.ShapeDtypeStruct(shape, F32),
        in_specs=[vmem] * len(vectors),
        out_specs=vmem,
        compiler_params=pltpu.CompilerParams(vmem_limit_bytes=limit * MIB),
        name=name,
    )(*vectors)


def local(object_field, probe, intensity, pool_rows, pool_cols, batch, live):
    side = probe.shape[1]
    nrows, ncols = object_field.shape[1:]
    dims = (side, nrows, ncols)
    slots = batch.shape[1]
    t = side // LANES
    total = (ncols + side) // LANES
    probe_rate = 0.125 / math.sqrt(LIVE * lax.axis_size("tile") * lax.axis_size("row"))
    both = jnp.asarray(np.stack(tables(side)))
    current = probe.reshape(2, side, t, LANES).transpose(0, 2, 1, 3)

    first, rest = lax.optimization_barrier((object_field[:, :side, :side], object_field))
    below_a = passed_along(first, "row", -1)
    beside_a = passed_along(first, "tile", -1)
    beside_b = passed_along(rest[:, side:, :side], "tile", -1)
    below_b = passed_along(rest[:, :side, side:], "row", -1)
    corner = passed_along(below_a, "tile", -1)

    edge = jnp.stack([
        (lax.axis_index("row") == lax.axis_size("row") - 1).astype(jnp.int32),
        (lax.axis_index("tile") == lax.axis_size("tile") - 1).astype(jnp.int32)])
    scalars = (batch, live, pool_rows, pool_cols)
    devices = lax.axis_size("tile") * lax.axis_size("row")
    big = (2, total, nrows + side, LANES)
    corners = (2, 2, t, side, LANES)
    strip = (2, ncols // LANES - t, side, LANES)
    side_b = (2, t, nrows - side, LANES)
    middle_b = (2, ncols // LANES - t, nrows - side, LANES)
    old, middle, gprobe, right_c, left_c, right_b, left_b, down_b, up_b = call(
        functools.partial(first_kernel, dims), dims, slots, scalars, (current,),
        (intensity, both, object_field, below_a, below_b, beside_a, beside_b, corner), (),
        [big, middle_b, current.shape, corners, corners, side_b, side_b, strip, strip], [],
        54, "first_iteration")

    from_left_c = passed_along(right_c, "tile", 1)
    from_right_c = passed_along(left_c, "tile", -1)
    from_up_b = passed_along(down_b, "row", 1)
    from_down_b = passed_along(up_b, "row", -1)
    mine = swap(gprobe.reshape(devices, -1, LANES))
    mine, from_left_c, from_right_c = lax.optimization_barrier((mine, from_left_c, from_right_c))
    down_c = jnp.stack([left_c[1] + from_left_c[1], right_c[1] + from_right_c[1]])
    up_c = jnp.stack([left_c[0] + from_left_c[0], right_c[0] + from_right_c[0]])
    from_up_c = passed_along(down_c, "row", 1)
    from_down_c = passed_along(up_c, "row", -1)
    mine, from_up_b, from_down_b, _, _ = lax.optimization_barrier(
        (mine, from_up_b, from_down_b, down_c, up_c))
    given, right_b, left_b = lax.optimization_barrier((add_up(mine), right_b, left_b))
    from_left_b = passed_along(right_b, "tile", 1)
    from_right_b = passed_along(left_b, "tile", -1)
    sum_one = swap(given).reshape(current.shape)
    part = update(dims, edge, (old, middle, left_c, right_c, left_b, right_b, down_b, up_b,
                               from_left_c, from_right_c, from_up_b, from_down_b))

    own, gprobe, right_c, right_ab, down_a, down_b = call(
        functools.partial(second_kernel, dims, probe_rate), dims, slots, scalars + (edge,),
        (current, sum_one), (intensity, both, part),
        (from_up_c, from_down_c, from_left_b, from_right_b),
        [(2, ncols // LANES, nrows, LANES), current.shape, (2, t, side, LANES),
         (2, t, nrows, LANES), (2, t, side, LANES), strip],
        [current.shape], 50, "second_iteration")

    from_left_c = passed_along(right_c, "tile", 1)
    mine = swap(gprobe.reshape(devices, -1, LANES))
    down_a = down_a + from_left_c
    mine, down_a = lax.optimization_barrier((mine, down_a))
    given, right_ab, down_b = lax.optimization_barrier((add_up(mine), right_ab, down_b))
    above_a = passed_along(down_a, "row", 1)
    above_b = passed_along(down_b, "row", 1)
    left_ab = passed_along(right_ab, "tile", 1)
    sum_two = swap(given).reshape(current.shape)
    object_out = simple(functools.partial(object_kernel, dims), object_field.shape, "last_object",
                        16, (own, left_ab, above_a, above_b))
    sum_two, _ = lax.optimization_barrier((sum_two, object_out))
    probe_out = simple(functools.partial(probe_kernel, probe_rate), probe.shape, "last_probe",
                       8, (current, sum_one, sum_two))
    return (object_out, probe_out)


def solution(mesh):
    placed = (
        P(None, "row", "tile"),
        P(),
        P(("tile", "row"), None, None),
        P(("tile", "row")),
        P(("tile", "row")),
        P(None, ("tile", "row")),
        P(None, ("tile", "row")),
    )
    return jax.shard_map(
        local, mesh=mesh, in_specs=placed, out_specs=(P(None, "row", "tile"), P()), check_vma=False
    )
```
